32 devices in a mesh: tm: 16 (over z, y, x), mp: 2 (over core).
Axes of the slice: x: 2, y: 2, z: 4, core: 2. Of those that a mesh axis runs over, the one named last changes fastest.
Arguments:
- x_input: float32 [8192, 512], P('tm', 'mp')
- mel_frames: float32 [80, 8192], P(None, 'tm'), may hold values from -6 to 6
- sample_mask: int32 [8192], P('tm'), may hold values 0 or 1
- clip_length_array: int32 [8], replicated, may hold values from 1 to 8185, as said below
- speaker_ids: int32 [8], replicated, may hold values from 0 to 108
- cot_out: float32 [8192, 512], P('tm', 'mp')
- cot_skip: float32 [8192, 512], P('tm', 'mp')
- dilated_kernel_weight: float32 [2, 2, 512, 2, 512], P(None, None, 'tm', None, 'mp'), may hold values from -0.1875 to 0.1875
- dilated_first_moment: float32 [2, 2, 512, 2, 512], P(None, None, 'tm', None, 'mp'), may hold values from -0.0007324219 to 0.0007324219
- dilated_second_moment: float32 [2, 2, 512, 2, 512], P(None, None, 'tm', None, 'mp'), may hold values from 2.828976e-10 to 1.1315904e-09
- gate_bias: float32 [2, 2, 512], P(None, None, ('mp', 'tm')), may hold values from -1.5 to 1.5
- bias_mean: float32 [2, 2, 512], P(None, None, ('mp', 'tm')), may hold values from -0.0007324219 to 0.0007324219
- bias_square: float32 [2, 2, 512], P(None, None, ('mp', 'tm')), may hold values from 2.828976e-10 to 1.1315904e-09
- mel_weight: float32 [2, 80, 2, 512], P(None, None, None, ('mp', 'tm')), may hold values from -0.625 to 0.625
- mel_mean: float32 [2, 80, 2, 512], P(None, None, None, ('mp', 'tm')), may hold values from -0.0007324219 to 0.0007324219
- mel_square: float32 [2, 80, 2, 512], P(None, None, None, ('mp', 'tm')), may hold values from 2.828976e-10 to 1.1315904e-09
- speaker_table: float32 [2, 109, 2, 512], P(None, None, None, ('mp', 'tm')), may hold values from -4 to 4
- table_mean: float32 [2, 109, 2, 512], P(None, None, None, ('mp', 'tm')), may hold values from -0.0007324219 to 0.0007324219
- table_square: float32 [2, 109, 2, 512], P(None, None, None, ('mp', 'tm')), may hold values from 2.828976e-10 to 1.1315904e-09
- residual_weight: float32 [2, 512, 512], P(None, 'mp', 'tm')
- residual_mean: float32 [2, 512, 512], P(None, 'mp', 'tm'), may hold values from -0.0007324219 to 0.0007324219
- residual_square: float32 [2, 512, 512], P(None, 'mp', 'tm'), may hold values from 2.828976e-10 to 1.1315904e-09
- skip_weight: float32 [2, 512, 512], P(None, 'mp', 'tm')
- skip_mean: float32 [2, 512, 512], P(None, 'mp', 'tm'), may hold values from -0.0007324219 to 0.0007324219
- skip_square: float32 [2, 512, 512], P(None, 'mp', 'tm'), may hold values from 2.828976e-10 to 1.1315904e-09
Outputs:
- mixed: float32 [8192, 512], P('tm', 'mp')
- skip_total: float32 [8192, 512], P('tm', 'mp')
- grad_input: float32 [8192, 512], P('tm', 'mp')
- grad_norm: float32 [], replicated
- grad_dilated: float32 [2, 2, 512, 2, 512], P(None, None, 'tm', None, 'mp')
- grad_bias: float32 [2, 2, 512], P(None, None, ('mp', 'tm'))
- grad_mel: float32 [2, 80, 2, 512], P(None, None, None, ('mp', 'tm'))
- grad_table: float32 [2, 109, 2, 512], P(None, None, None, ('mp', 'tm'))
- grad_residual: float32 [2, 512, 512], P(None, 'mp', 'tm')
- grad_skip: float32 [2, 512, 512], P(None, 'mp', 'tm')
- new_dilated_weight: float32 [2, 2, 512, 2, 512], P(None, None, 'tm', None, 'mp')
- new_dilated_mean: float32 [2, 2, 512, 2, 512], P(None, None, 'tm', None, 'mp')
- new_dilated_square: float32 [2, 2, 512, 2, 512], P(None, None, 'tm', None, 'mp')
- new_gate_bias: float32 [2, 2, 512], P(None, None, ('mp', 'tm'))
- new_bias_mean: float32 [2, 2, 512], P(None, None, ('mp', 'tm'))
- new_bias_square: float32 [2, 2, 512], P(None, None, ('mp', 'tm'))
- new_mel_weight: float32 [2, 80, 2, 512], P(None, None, None, ('mp', 'tm'))
- new_mel_mean: float32 [2, 80, 2, 512], P(None, None, None, ('mp', 'tm'))
- new_mel_square: float32 [2, 80, 2, 512], P(None, None, None, ('mp', 'tm'))
- new_speaker_table: float32 [2, 109, 2, 512], P(None, None, None, ('mp', 'tm'))
- new_table_mean: float32 [2, 109, 2, 512], P(None, None, None, ('mp', 'tm'))
- new_table_square: float32 [2, 109, 2, 512], P(None, None, None, ('mp', 'tm'))
- new_residual_weight: float32 [2, 512, 512], P(None, 'mp', 'tm')
- new_residual_mean: float32 [2, 512, 512], P(None, 'mp', 'tm')
- new_residual_square: float32 [2, 512, 512], P(None, 'mp', 'tm')
- new_skip_weight: float32 [2, 512, 512], P(None, 'mp', 'tm')
- new_skip_mean: float32 [2, 512, 512], P(None, 'mp', 'tm')
- new_skip_square: float32 [2, 512, 512], P(None, 'mp', 'tm')
- low_dilated: bfloat16 [2, 2, 512, 2, 512], P(None, None, 'tm', None, 'mp')
- low_bias: bfloat16 [2, 2, 512], P(None, None, ('mp', 'tm'))
- low_mel: bfloat16 [2, 80, 2, 512], P(None, None, None, ('mp', 'tm'))
- low_table: bfloat16 [2, 109, 2, 512], P(None, None, None, ('mp', 'tm'))
- low_residual: bfloat16 [2, 512, 512], P(None, 'mp', 'tm')
- low_skip: bfloat16 [2, 512, 512], P(None, 'mp', 'tm')
The draws below stay inside these ranges and needn't reach their ends.
Inputs may be any that keep to these rules, and one draw needn't show every extreme that they name: `clip_length_array`: the lengths sum to 8192; one clip, which one drawn from the seed, starts within the first 512 samples and ends within the last 512; every other clip is shorter than 64.
All inputs are finite; a program needn't handle non-finite values. No bound on the sum of `sample_mask` on one device may be relied on, other than what follows from the above.
Results may differ from the reference program's by a relative error of at most 0.0083.
The reference program's roundings to bfloat16 on the way count: a program that leaves them out, or rounds other values in their place, can miss the bound.
Values may be sent and summed in bfloat16 or wider, within the bound.
No kernel may reach another device: no remote copies, remote signals or barrier semaphores. Data moves between devices by JAX's collectives and lax.ppermute only.
A program may use at most 128 MiB of HBM per device.

```python
import math
import jax
import jax.numpy as jnp
import numpy as np
from jax import lax

RESIDUAL_WIDTH = 512
GATE_CHANNELS = 1024
SKIP = 512
MEL = 80
SPK = 109
FIRST_DILATION = 512
CLIPS = 8
STEP = 10
SAMP_DEV = 512
HALF = 512
SAMPLES = 8192
PARAMS = 3534848


def ramp_scaled(key, input_rows, cols, ramp_axis):
    length = (input_rows, cols)[ramp_axis]
    ramp = jnp.arange(length, dtype=jnp.float32) / (length - 1)
    base = jax.random.normal(key, (input_rows, cols), jnp.float32)
    scale = 0.6 + 1.2 * ramp
    if ramp_axis == 1:
        return base * scale[None, :]
    return base * scale[:, None]


def draw_x_input(key, part):
    key = jax.random.fold_in(key, 11)
    return ramp_scaled(key, SAMPLES, RESIDUAL_WIDTH, 1)


def draw_cot_out(key, part):
    key = jax.random.fold_in(key, 12)
    return ramp_scaled(key, SAMPLES, RESIDUAL_WIDTH, 1)


def draw_cot_skip(key, part):
    key = jax.random.fold_in(key, 13)
    return ramp_scaled(key, SAMPLES, SKIP, 1)


def draw_residual_weight(key, part):
    key = jax.random.fold_in(key, 14)
    first = ramp_scaled(jax.random.fold_in(key, 0), HALF, RESIDUAL_WIDTH, 0)
    second = ramp_scaled(jax.random.fold_in(key, 1), HALF, RESIDUAL_WIDTH, 0)
    return jnp.stack([first, second]) * (2.0 / HALF ** 0.5)


def draw_skip_weight(key, part):
    key = jax.random.fold_in(key, 15)
    first = ramp_scaled(jax.random.fold_in(key, 0), HALF, SKIP, 0)
    second = ramp_scaled(jax.random.fold_in(key, 1), HALF, SKIP, 0)
    return jnp.stack([first, second]) * (1.0 / HALF ** 0.5)


def draw_clip_length_array(key, part):
    key = jax.random.fold_in(key, 16)
    pick_key, size_key = jax.random.split(key)
    chosen = jax.random.randint(pick_key, (), 0, CLIPS)
    small = jax.random.randint(size_key, (CLIPS,), 1, SAMP_DEV // CLIPS)
    index = jnp.arange(CLIPS)
    small = jnp.where(index == chosen, 0, small)
    return jnp.where(index == chosen, SAMPLES - jnp.sum(small), small).astype(jnp.int32)


def place_ends(entries, stream_key, low, high):
    index_at = [jax.random.randint(jax.random.fold_in(stream_key, axis), (), 0, length) for axis, length in enumerate(entries.shape)]
    main_axis = entries.shape.index(max(entries.shape))
    beside = index_at[:main_axis] + [(index_at[main_axis] + 1) % entries.shape[main_axis]] + index_at[main_axis + 1:]
    return entries.at[tuple(index_at)].set(low).at[tuple(beside)].set(high)


def block_levels(rng, shape, pieces, least, largest):
    def one(dim, parts):
        steps = jax.random.uniform(jax.random.fold_in(jax.random.fold_in(rng, 6), dim), (parts,), jnp.float32, least / len(pieces), largest / len(pieces))
        return jnp.repeat(jnp.exp(steps), shape[dim] // parts).reshape((-1,) + (1,) * (len(shape) - dim - 1))

    loudness = one(*pieces[0])
    for cut in pieces[1:]:
        loudness = loudness * one(*cut)
    return loudness


def rank_table(amount, slope):
    loads = [(1 << 20) // math.isqrt(standing ** slope) + 1 for standing in range(1, amount + 1)]
    spread = 1 + sum(loads) // (1 << 30)
    return np.cumsum(np.array([max(1, weight // spread) for weight in loads]))


def ranked_ids(rng, dims, number_of, lean):
    table = rank_table(number_of, lean)
    ticket = jax.random.randint(jax.random.fold_in(rng, 1), dims, 0, int(table[number_of - 1]))
    standing = jnp.searchsorted(jnp.asarray(table, jnp.int32), ticket, side="right")
    return jax.random.permutation(jax.random.fold_in(rng, 2), number_of)[standing].astype(jnp.int32)


def centred(key, dims, deviation, limit, pieces=(), held_as=jnp.bfloat16):
    level = block_levels(key, dims, pieces, -0.22, 0.18) if pieces else 1.0
    array = jax.random.normal(key, dims, jnp.float32) * deviation * level
    return jnp.minimum(jnp.maximum(array, -limit), limit).astype(held_as)


def setup_inputs(seed: int = 0) -> dict:
    seeds = jax.random.split(jax.random.key(seed), 26)
    x_input = draw_x_input(jax.random.fold_in(seeds[25], 71), 0)
    mel_frames = centred(seeds[1], (MEL, SAMPLES), 1.0, 6.0, ((1, 16),), jnp.float32)
    sample_mask = place_ends((jax.random.randint(seeds[2], (SAMPLES,), 0, 8) < 7).astype(jnp.int32), jax.random.fold_in(seeds[2], 1), 0, 1)
    clip_length_array = draw_clip_length_array(jax.random.fold_in(seeds[25], 71), 0)
    speaker_ids = place_ends(ranked_ids(seeds[4], (CLIPS,), SPK, 2), jax.random.fold_in(seeds[4], 3), 0, SPK - 1).astype(jnp.int32)
    cot_out = draw_cot_out(jax.random.fold_in(seeds[25], 71), 0)
    cot_skip = draw_cot_skip(jax.random.fold_in(seeds[25], 71), 0)
    dilated_kernel_weight = centred(seeds[7], (2, 2, RESIDUAL_WIDTH, 2, HALF), (2 * RESIDUAL_WIDTH) ** -0.5, 0.1875, ((2, 16), (4, 2)), jnp.float32)
    dilated_first_moment = centred(seeds[8], (2, 2, RESIDUAL_WIDTH, 2, HALF), (0.1 * PARAMS ** -0.5), 0.0007324219, ((2, 16), (4, 2)), jnp.float32)
    dilated_second_moment = jnp.clip(jnp.exp(math.log(1.1315903769570923e-09) - 1.3862944 * jax.random.uniform(seeds[9], (2, 2, RESIDUAL_WIDTH, 2, HALF), jnp.float32) ** block_levels(seeds[9], (2, 2, RESIDUAL_WIDTH, 2, HALF), ((2, 16), (4, 2)), -0.2, 0.2)), 2.828975942392731e-10, 1.1315903769570923e-09)
    gate_bias = centred(seeds[10], (2, 2, HALF), 0.1, 1.5, ((2, 32),), jnp.float32)
    bias_mean = centred(seeds[11], (2, 2, HALF), (0.1 * PARAMS ** -0.5), 0.0007324219, ((2, 32),), jnp.float32)
    bias_square = jnp.clip(jnp.exp(math.log(1.1315903769570923e-09) - 1.3862944 * jax.random.uniform(seeds[12], (2, 2, HALF), jnp.float32) ** block_levels(seeds[12], (2, 2, HALF), ((2, 32),), -0.2, 0.2)), 2.828975942392731e-10, 1.1315903769570923e-09)
    mel_weight = centred(seeds[13], (2, MEL, 2, HALF), MEL ** -0.5, 0.625, ((3, 32),), jnp.float32)
    mel_mean = centred(seeds[14], (2, MEL, 2, HALF), (0.1 * PARAMS ** -0.5), 0.0007324219, ((3, 32),), jnp.float32)
    mel_square = jnp.clip(jnp.exp(math.log(1.1315903769570923e-09) - 1.3862944 * jax.random.uniform(seeds[15], (2, MEL, 2, HALF), jnp.float32) ** block_levels(seeds[15], (2, MEL, 2, HALF), ((3, 32),), -0.2, 0.2)), 2.828975942392731e-10, 1.1315903769570923e-09)
    speaker_table = centred(seeds[16], (2, SPK, 2, HALF), 0.3, 4.0, ((3, 32),), jnp.float32)
    table_mean = centred(seeds[17], (2, SPK, 2, HALF), (0.1 * PARAMS ** -0.5), 0.0007324219, ((3, 32),), jnp.float32)
    table_square = jnp.clip(jnp.exp(math.log(1.1315903769570923e-09) - 1.3862944 * jax.random.uniform(seeds[18], (2, SPK, 2, HALF), jnp.float32) ** block_levels(seeds[18], (2, SPK, 2, HALF), ((3, 32),), -0.2, 0.2)), 2.828975942392731e-10, 1.1315903769570923e-09)
    residual_weight = draw_residual_weight(jax.random.fold_in(seeds[25], 71), 0)
    residual_mean = centred(seeds[20], (2, HALF, RESIDUAL_WIDTH), (0.1 * PARAMS ** -0.5), 0.0007324219, ((1, 2), (2, 16)), jnp.float32)
    residual_square = jnp.clip(jnp.exp(math.log(1.1315903769570923e-09) - 1.3862944 * jax.random.uniform(seeds[21], (2, HALF, RESIDUAL_WIDTH), jnp.float32) ** block_levels(seeds[21], (2, HALF, RESIDUAL_WIDTH), ((1, 2), (2, 16)), -0.2, 0.2)), 2.828975942392731e-10, 1.1315903769570923e-09)
    skip_weight = draw_skip_weight(jax.random.fold_in(seeds[25], 71), 0)
    skip_mean = centred(seeds[23], (2, HALF, SKIP), (0.1 * PARAMS ** -0.5), 0.0007324219, ((1, 2), (2, 16)), jnp.float32)
    skip_square = jnp.clip(jnp.exp(math.log(1.1315903769570923e-09) - 1.3862944 * jax.random.uniform(seeds[24], (2, HALF, SKIP), jnp.float32) ** block_levels(seeds[24], (2, HALF, SKIP), ((1, 2), (2, 16)), -0.2, 0.2)), 2.828975942392731e-10, 1.1315903769570923e-09)
    return dict(x_input=x_input, mel_frames=mel_frames, sample_mask=sample_mask, clip_length_array=clip_length_array, speaker_ids=speaker_ids, cot_out=cot_out, cot_skip=cot_skip, dilated_kernel_weight=dilated_kernel_weight, dilated_first_moment=dilated_first_moment, dilated_second_moment=dilated_second_moment, gate_bias=gate_bias, bias_mean=bias_mean, bias_square=bias_square, mel_weight=mel_weight, mel_mean=mel_mean, mel_square=mel_square, speaker_table=speaker_table, table_mean=table_mean, table_square=table_square, residual_weight=residual_weight, residual_mean=residual_mean, residual_square=residual_square, skip_weight=skip_weight, skip_mean=skip_mean, skip_square=skip_square)


ROOT_HALF = 0.7071067811865476
BETA_ONE = 0.9
BETA_TWO = 0.999
ADAM_EPS = 1e-08
LEARN_RATE = 0.07
DECAY = 0.01
CLIP_NORM = 1.0
HIGH = lax.Precision.HIGHEST

@jax.custom_vjp
def lowered_value(v):
    return lax.optimization_barrier(v.astype(jnp.bfloat16)).astype(jnp.float32)

@jax.custom_vjp
def low_back(v):
    return v

def low_keep(v):
    return (lowered_value(v), None)

def low_pass(kept, gradient_value):
    return (gradient_value,)

def back_keep(v):
    return (v, None)

def back_low(kept, gradient_value):
    return (lowered_value(gradient_value),)
lowered_value.defvjp(low_keep, low_pass)
low_back.defvjp(back_keep, back_low)

def segment_ids(sample_positions, clip_length_array):
    ends = jnp.cumsum(clip_length_array).astype(jnp.int32)
    return lax.optimization_barrier(jnp.sum((sample_positions[:, None] >= ends[None, :]).astype(jnp.int32), axis=1))

def lagged_valid_mask(sample_positions, clip_length_array, span):
    here = segment_ids(sample_positions, clip_length_array)
    there = segment_ids(sample_positions - span, clip_length_array)
    return ((sample_positions >= span) & (here == there)).astype(jnp.float32)

def matmul(a, b):
    return jnp.dot(a, b, precision=HIGH)

def gate_branch(lag, xin, far_tap_input, near_tap_input, bias_row, mel_low, mel_map, speaker_hot, table, keep, res_map, skip_map):
    z_value = matmul(lag, far_tap_input) + matmul(xin, near_tap_input) + bias_row[None, :]
    z_value = z_value + matmul(mel_low.T, mel_map) + matmul(speaker_hot, table)
    z_value = low_back(z_value)
    gate_a = z_value[:, :HALF]
    gate_b = z_value[:, HALF:]
    hidden = lowered_value(keep * jnp.tanh(gate_a) * jax.nn.sigmoid(gate_b))
    return (low_back(matmul(hidden, res_map)), low_back(matmul(hidden, skip_map)))

def adamw_update_step(weight, mean, square, gradient_value, scale_factor):
    clipped = gradient_value * scale_factor
    new_mean = BETA_ONE * mean + (1.0 - BETA_ONE) * clipped
    new_square = BETA_TWO * square + (1.0 - BETA_TWO) * clipped * clipped
    fix_one = 1.0 - BETA_ONE ** STEP
    fix_two = 1.0 - BETA_TWO ** STEP
    update = new_mean / fix_one / (jnp.sqrt(new_square / fix_two) + ADAM_EPS)
    return (weight - LEARN_RATE * (update + DECAY * weight), new_mean, new_square)

def reference(x_input, mel_frames, sample_mask, clip_length_array, speaker_ids, cot_out, cot_skip, dilated_kernel_weight, dilated_first_moment, dilated_second_moment, gate_bias, bias_mean, bias_square, mel_weight, mel_mean, mel_square, speaker_table, table_mean, table_square, residual_weight, residual_mean, residual_square, skip_weight, skip_mean, skip_square):
    sample_positions = jnp.arange(SAMPLES, dtype=jnp.int32)
    valid_mask_list = (lagged_valid_mask(sample_positions, clip_length_array, FIRST_DILATION), lagged_valid_mask(sample_positions, clip_length_array, 1))
    keep = sample_mask.astype(jnp.float32)[:, None]
    segment = segment_ids(sample_positions, clip_length_array)
    clip_hot = (segment[:, None] == jnp.arange(CLIPS, dtype=jnp.int32)[None, :]).astype(jnp.float32)
    speaker_clip = (speaker_ids[:, None] == jnp.arange(SPK, dtype=jnp.int32)[None, :]).astype(jnp.float32)
    speaker_hot = matmul(clip_hot, speaker_clip)
    clip_spans = (FIRST_DILATION, 1)
    branch = jax.checkpoint(gate_branch)

    def forward_pass(input_value, weight_dilated, weight_bias, weight_mel_projection, weight_speaker_table, weight_residual, weight_skip):
        mel_low = lowered_value(mel_frames)
        state = input_value
        skip_sum = jnp.zeros((SAMPLES, SKIP), jnp.float32)
        for layer_number in range(2):
            span = clip_spans[layer_number]
            xin = lowered_value(state)
            shifted = jnp.concatenate([jnp.zeros((span, RESIDUAL_WIDTH), jnp.float32), xin[:-span]], axis=0)
            lag = low_back(shifted * valid_mask_list[layer_number][:, None])
            far_tap_input = lowered_value(weight_dilated[layer_number, 0]).reshape(RESIDUAL_WIDTH, GATE_CHANNELS)
            near_tap_input = lowered_value(weight_dilated[layer_number, 1]).reshape(RESIDUAL_WIDTH, GATE_CHANNELS)
            bias_row = lowered_value(weight_bias[layer_number]).reshape(GATE_CHANNELS)
            mel_map = lowered_value(weight_mel_projection[layer_number]).reshape(MEL, GATE_CHANNELS)
            table = lowered_value(weight_speaker_table[layer_number]).reshape(SPK, GATE_CHANNELS)
            res_part, skip_part = branch(lag, xin, far_tap_input, near_tap_input, bias_row, mel_low, mel_map, speaker_hot, table, keep, lowered_value(weight_residual[layer_number]), lowered_value(weight_skip[layer_number]))
            state = (state + res_part) * ROOT_HALF
            skip_sum = skip_sum + skip_part
        return (state, skip_sum)
    (mixed, skip_total), pullback = jax.vjp(forward_pass, x_input, dilated_kernel_weight, gate_bias, mel_weight, speaker_table, residual_weight, skip_weight)
    grads = pullback((cot_out, cot_skip))
    grad_input = grads[0]
    weight_grads = grads[1:]
    total = jnp.float32(0.0)
    for gradient_value in weight_grads:
        total = total + jnp.sum(gradient_value * gradient_value)
    grad_norm = jnp.sqrt(total)
    scale_factor = jnp.minimum(1.0, CLIP_NORM / grad_norm)
    states = ((dilated_kernel_weight, dilated_first_moment, dilated_second_moment), (gate_bias, bias_mean, bias_square), (mel_weight, mel_mean, mel_square), (speaker_table, table_mean, table_square), (residual_weight, residual_mean, residual_square), (skip_weight, skip_mean, skip_square))
    result_list = []
    for index in range(6):
        weight, mean, square = states[index]
        result_list.extend(adamw_update_step(weight, mean, square, weight_grads[index], scale_factor))
    lows = [result_list[3 * index].astype(jnp.bfloat16) for index in range(6)]
    return (mixed, skip_total, grad_input, grad_norm, weight_grads[0], weight_grads[1], weight_grads[2], weight_grads[3], weight_grads[4], weight_grads[5], result_list[0], result_list[1], result_list[2], result_list[3], result_list[4], result_list[5], result_list[6], result_list[7], result_list[8], result_list[9], result_list[10], result_list[11], result_list[12], result_list[13], result_list[14], result_list[15], result_list[16], result_list[17], lows[0], lows[1], lows[2], lows[3], lows[4], lows[5])
```

```python
import functools

import jax
import jax.numpy as jnp
from jax import lax
from jax.experimental import pallas as pl
from jax.experimental.pallas import tpu as pltpu
from jax.sharding import PartitionSpec as P

FIRST_DILATION = 512
STEP = 10
ROOT_HALF = 0.7071067811865476
BETA_ONE = 0.9
BETA_TWO = 0.999
ADAM_EPS = 1e-08
LEARN_RATE = 0.07
DECAY = 0.01
CLIP_NORM = 1.0

F32 = jnp.float32
BF16 = jnp.bfloat16
LANES = 128
EDGE = 8
BLOCKS = 16
NEAR = 4
VMEM_BYTES = 26 * 1024 * 1024
BOTH = ("tm", "mp")


def struct(shape, dtype=F32):
    return jax.ShapeDtypeStruct(shape, dtype)


def call(body, out_shape, *operands, scalars=(), scratch=(), space=pltpu.VMEM, unread=(), flops=1024, grant=VMEM_BYTES):
    specs = [pl.BlockSpec(memory_space=pltpu.SMEM)] * len(scalars)
    specs += [pl.BlockSpec(memory_space=space)] * len(operands)
    specs += [pl.BlockSpec(memory_space=pl.ANY)] * len(unread)
    return pl.pallas_call(
        body,
        out_shape=out_shape,
        in_specs=specs,
        scratch_shapes=list(scratch),
        compiler_params=pltpu.CompilerParams(vmem_limit_bytes=grant),
        cost_estimate=pl.CostEstimate(flops=flops, bytes_accessed=1024, transcendentals=0),
    )(*scalars, *operands, *unread)


def dot(left, right):
    return jnp.dot(left, right, preferred_element_type=F32)


def dot_right(left, right):
    return lax.dot_general(left, right, (((1,), (1,)), ((), ())), preferred_element_type=F32)


def dot_left(left, right):
    return lax.dot_general(left, right, (((0,), (0,)), ((), ())), preferred_element_type=F32)


def place():
    index = lax.axis_index("tm")
    core = lax.axis_index("mp")
    return index // NEAR, index % NEAR, core, 1 + core, 2 - core


def route(target):
    return [
        (index * 2 + core, target(index, core) * 2 + core)
        for index in range(lax.axis_size("tm"))
        for core in range(2)
    ]


def across(value, bit):
    return lax.ppermute(value, BOTH, route(lambda i, c: i ^ (1 + (c ^ bit))))


def along_far(value, distance):
    far = lax.axis_size("tm") // NEAR
    return lax.ppermute(
        value, BOTH, route(lambda i, c: (i // NEAR + distance) % far * NEAR + i % NEAR)
    )


def swap_cores(value):
    return lax.ppermute(value, "mp", [(0, 1), (1, 0)])


def shifted(value, axis, distance):
    devices = range(lax.axis_size(axis))
    pairs = [(i - distance, i) for i in devices if i - distance in devices]
    return lax.ppermute(value, axis, pairs)


def crossed(value, distance):
    parts = lax.axis_size("tm")
    pairs = [
        (index * 2 + core, (index + distance) * 2 + 1 - core)
        for index in range(parts)
        for core in range(2)
        if 0 <= index + distance < parts
    ]
    return lax.ppermute(value, BOTH, pairs)


def sections(rows):
    found, at = [], 0
    for count in (rows,) * 6 + (rows // 2,):
        found.append((at, count))
        at += count
    return found, at


WHERE, ROWS = sections(32)


def dilated_view(array):
    layers, taps, rows, halves, width = array.shape
    tiles = width // LANES
    split = array.reshape(layers, taps, rows, halves, tiles, LANES)
    return split.transpose(0, 1, 2, 4, 3, 5).reshape(-1, LANES)


def dilated_back(array, shape):
    layers, taps, rows, halves, width = shape
    tiles = width // LANES
    split = array.reshape(layers, taps, rows, tiles, halves, LANES)
    return split.transpose(0, 1, 2, 4, 3, 5).reshape(shape)


def strided(layer, tap, half, tile, rows):
    return pl.ds((layer * 2 + tap) * rows * 4 + tile * 2 + half, rows, stride=4)


def start_body(rows, mel, clips, who, *refs):
    sources, inputs, (out_one, out_two, kept, given, low) = refs[:6], refs[6:9], refs[9:14]
    held, samples, sems = refs[14:20], refs[20], refs[21]
    core = place()[2]
    own, width = kept.shape[0], kept.shape[1] // 3
    copies = [
        pltpu.make_async_copy(source, target, sems.at[index])
        for index, (source, target) in enumerate(zip(sources + inputs[:1], held + (samples,)))
    ]
    moves = []
    for index, source in enumerate(inputs):
        columns = pl.ds(index * width, width)
        for half, target in ((core, kept), (1 - core, given)):
            moves.append(
                pltpu.make_async_copy(
                    source.at[pl.ds(half * own, own), :],
                    target.at[:, columns],
                    sems.at[len(copies) + len(moves)],
                )
            )
    for copy in copies + moves:
        copy.start()
    dil, res, skip, mel_w, table, bias = held
    where, total = sections(rows)
    chans = rows // 2
    speakers = table.shape[-1]
    lane = lax.broadcasted_iota(jnp.int32, (1, speakers), 1)
    hot = jnp.concatenate([(lane == who[k]).astype(F32) for k in range(clips)], axis=0).astype(BF16)
    eye = lax.broadcasted_iota(jnp.int32, (chans, chans), 0) == lax.broadcasted_iota(
        jnp.int32, (chans, chans), 1
    )

    def write(out, at, count, columns, value):
        out[at : at + count, columns] = value.astype(out.dtype)

    for copy in copies:
        copy.wait()
    for layer, out in enumerate((out_one, out_two)):
        for tap in range(2):
            for half in range(2):
                at, count = where[2 * tap + half]
                for tile in range(2):
                    part = dil[strided(layer, tap, half, tile, rows), :]
                    write(out, at, count, slice(tile * LANES, (tile + 1) * LANES), part)
        for kind, source in ((4, res), (5, skip)):
            at, count = where[kind]
            write(out, at, count, slice(None), source[layer])
        at, count = where[6]
        for half in range(2):
            picked = dot_right(table[layer, half].astype(BF16), hot)
            line = jnp.broadcast_to(bias[layer, half : half + 1, :], (chans, chans))
            column = jnp.sum(jnp.where(eye, line, 0.0), axis=1, keepdims=True)
            blank = jnp.zeros((chans, LANES - mel - clips - 1), F32)
            row = jnp.concatenate([mel_w[layer, half], picked, column, blank], axis=1)
            columns = slice(half * LANES, (half + 1) * LANES)
            write(out, at, count, columns, row.astype(BF16).astype(F32))
    low[...] = samples[...].astype(BF16)
    for move in moves:
        move.wait()


def assemble_body(group, first, second, last, *refs):
    out = refs[-1]
    count = group.shape[0]
    far, near, _, first_bit, second_bit = place()
    for ref, mask in ((group, 0), (first, first_bit), (second, second_bit), (last, 3)):
        for back in range(count):
            out[lax.rem(far + count - back, count) * NEAR + (near ^ mask)] = ref[back]


def relay_body(value, *refs):
    out, token = refs[-2:]
    out[...] = value[...]
    token[...] = jnp.zeros_like(token)


TOKEN = struct((8, LANES))
LONG = 20_000_000_000


def stack_body(count, *refs):
    out, token = refs[-2:]
    for index in range(count):
        out[index] = refs[index][...]
    token[...] = jnp.zeros_like(token)


def along_all(pack, unread):
    far = lax.axis_size("tm") // NEAR
    got = [along_far(pack, distance) for distance in range(1, far)]
    return call(
        functools.partial(stack_body, far),
        (struct((far,) + pack.shape, BF16), TOKEN),
        pack,
        *got,
        unread=unread,
    )


def near_exchange(group, before_last):
    first = across(group, 0)
    second = across(group, 1)
    passed, token = call(
        relay_body, (struct(first.shape, BF16), TOKEN), first, unread=(second,) + before_last
    )
    return (group, first, second, across(passed, 1)), token


def joined(parts, before_end):
    count = NEAR * parts[0].shape[0]
    own = call(
        assemble_body, struct((count,) + parts[0].shape[1:], BF16), *parts, unread=before_end
    )
    if count != BLOCKS:
        own = to_canonical(own)
    return own, swap_cores(own)


def to_canonical(gathered):
    parts = gathered.shape[0]
    where, total = sections(BLOCKS * 32 // parts)
    return jnp.concatenate(
        [gathered[:, at : at + n, :].reshape(BLOCKS, -1, 256) for at, n in where], axis=1
    )


def from_canonical(packed, parts):
    where, total = sections(32)
    return jnp.concatenate(
        [packed[:, at : at + n, :].reshape(parts, -1, 256) for at, n in where], axis=1
    )


def piece(ref, kind):
    at, count = WHERE[kind]
    return ref[:, at : at + count, :].reshape(-1, 256)


def conditioning(ref, half):
    at, count = WHERE[6]
    return ref[:, at : at + count, half * LANES : (half + 1) * LANES].reshape(-1, LANES)


def slot(ordered, first, block):
    if not ordered:
        return block
    near = lax.axis_index("tm") % NEAR
    mask = (block % NEAR) ^ near
    group = jnp.where(mask == 3, 0, jnp.where(mask == 0, 3, jnp.where(mask == first, 2, 1)))
    return group * (BLOCKS // NEAR) + block // NEAR


def store(ref, slots, kind, value):
    at, count = WHERE[kind]
    value = value.astype(BF16)
    for block in range(BLOCKS):
        ref[slots[block], at : at + count, :] = value[block * count : (block + 1) * count]


def store_conditioning(ref, slots, half, value):
    at, count = WHERE[6]
    value = value.astype(BF16)
    for block in range(BLOCKS):
        ref[slots[block], at : at + count, half * LANES : (half + 1) * LANES] = value[
            block * count : (block + 1) * count
        ]


def order_body(own, other, own_out, other_out):
    parts = own.shape[0]
    far = parts // NEAR
    _, near, _, first, second = place()
    for source, out, bit, next_bit in (
        (own, own_out, first, second),
        (other, other_out, second, first),
    ):
        for group, mask in enumerate((3, next_bit, bit, 0)):
            for index in range(far):
                out[group * far + index] = source[index * NEAR + (near ^ mask)]


def first_sum_body(own, got, *refs):
    out, token = refs[-2:]
    half = out.shape[0]
    out[...] = own[:half] + got[:half]
    token[...] = jnp.zeros_like(token)


def second_sum_body(own, got, near_got, *refs):
    out, token = refs[-2:]
    count = out.shape[0]
    kept = slice(2 * count, 3 * count)
    out[...] = (
        own[kept].astype(F32) + got[kept].astype(F32) + near_got[:count].astype(F32)
    ).astype(BF16)
    token[...] = jnp.zeros_like(token)


def third_sum_body(own, got, near_got, last_got, *refs):
    far = place()[0]
    count = last_got.shape[0]
    token = refs[-1]
    token[...] = jnp.zeros_like(token)
    for distance, out in enumerate(refs[-count - 1 : -1]):
        index = lax.rem(far + distance, count)
        out[...] = (
            own[3 * count + index].astype(F32)
            + got[3 * count + index].astype(F32)
            + near_got[count + index].astype(F32)
            + last_got[index].astype(F32)
        ).astype(out.dtype)


def ordered(grads):
    parts = lax.axis_size("tm")
    return grads if parts == BLOCKS else from_canonical(grads, parts)


def cores_summed(own, other, unread=()):
    own, other = ordered(own), ordered(other)
    if own.shape[0] != BLOCKS:
        own, other = call(order_body, (struct(own.shape, BF16),) * 2, own, other)
    got = swap_cores(other)
    half = struct((own.shape[0] // 2,) + own.shape[1:], BF16)
    sent, token = call(first_sum_body, (half, TOKEN), own, got, unread=unread)
    return (own, got), sent, token


def near_summed(grads, sent, flops=1024, unread=()):
    near_got = across(sent, 1)
    shape = (grads[0].shape[0] // NEAR,) + grads[0].shape[1:]
    sent, token = call(
        second_sum_body,
        (struct(shape, BF16), TOKEN),
        *grads,
        near_got,
        flops=flops,
        unread=unread,
    )
    return grads + (near_got,), sent, token


def far_terms(grads, last_got, unread=()):
    far, *shape = last_got.shape
    kept, *sends, token = call(
        third_sum_body,
        (struct(shape),) + (struct(shape, BF16),) * (far - 1) + (TOKEN,),
        *grads,
        last_got,
        unread=unread,
    )
    return [kept] + [along_far(value, k + 1) for k, value in enumerate(sends)], token


def gates(weights, lag, xin, cond):
    za = dot(lag, piece(weights, 0)) + dot(xin, piece(weights, 2))
    za = za + dot_right(cond, conditioning(weights, 0))
    zb = dot(lag, piece(weights, 1)) + dot(xin, piece(weights, 3))
    zb = zb + dot_right(cond, conditioning(weights, 1))
    return jnp.tanh(za), jax.nn.sigmoid(zb)


def gate_gradients(weights, res_grad, skip_grad, keep, tanh_a, sig_b):
    hidden_grad = dot(res_grad, piece(weights, 4)) + dot(skip_grad, piece(weights, 5))
    hidden_grad = hidden_grad * keep
    grad_a = (hidden_grad * sig_b * (1.0 - tanh_a * tanh_a)).astype(BF16)
    grad_b = (hidden_grad * tanh_a * sig_b * (1.0 - sig_b)).astype(BF16)
    return grad_a, grad_b


def weight_gradients(out, bit, lag, xin, cond, grad_a, grad_b, res_grad, skip_grad, hidden):
    slots = [slot(lax.axis_size("tm") == BLOCKS, bit, block) for block in range(BLOCKS)]
    store(out, slots, 0, dot_left(lag, grad_a))
    store(out, slots, 1, dot_left(lag, grad_b))
    store(out, slots, 2, dot_left(xin, grad_a))
    store(out, slots, 3, dot_left(xin, grad_b))
    store(out, slots, 4, dot_left(res_grad, hidden))
    store(out, slots, 5, dot_left(skip_grad, hidden))
    store_conditioning(out, slots, 0, dot_left(grad_a, cond))
    store_conditioning(out, slots, 1, dot_left(grad_b, cond))


def first_body(own, x, lag_raw, cond, marks, weights, *refs):
    earlier, (u2, s1, lag_out, ta, sb, hid, token) = refs[:-7], refs[-7:]
    token[...] = jnp.zeros_like(token)
    keep = marks[:, 0:1]
    xin = x[...].astype(BF16)
    lag = (lag_raw[...].astype(F32) * marks[:, 1:2]).astype(BF16)
    tanh_a, sig_b = gates(weights, lag, xin, cond[...])
    hidden = (keep * tanh_a * sig_b).astype(BF16)
    res = dot_right(hidden, piece(weights, 4))
    skip = dot_right(hidden[:own], piece(weights, 5))
    ta[...] = tanh_a[:own]
    sb[...] = sig_b[:own]
    hid[...] = hidden[:own]
    lag_out[...] = lag[:own]
    if len(earlier) == 2:
        u2[...] = (x[...] + (earlier[0][...] + res)) * ROOT_HALF
        s1[...] = earlier[1][...] + skip
    else:
        u2[...] = res
        s1[...] = skip


def second_input(u2, marks):
    xin = u2[...].astype(BF16)
    lag = (pltpu.roll(xin.astype(F32), 1, 0) * marks[:, 2:3]).astype(BF16)
    return xin, lag


def second_forward_body(u2, cond, marks, weights, ta, sb):
    xin, lag = second_input(u2, marks)
    ta[...], sb[...] = gates(weights, lag, xin, cond[...])


def second_body(own, u2, s1, cond, marks, cot, cot_skip, weights, *refs):
    last = len(refs) > 5
    earlier, (mixed, total, g2, lag_sum, grads) = refs[:-5], refs[-5:]
    rows = u2.shape[0]
    keep = marks[:, 0:1]
    xin, lag = second_input(u2, marks)
    res_grad = (cot[...] * ROOT_HALF).astype(BF16)
    skip_grad = cot_skip[...]
    if last:
        tanh_a, sig_b = earlier[4][...], earlier[5][...]
    else:
        tanh_a, sig_b = gates(weights, lag, xin, cond[...])
    hidden = (keep * tanh_a * sig_b).astype(BF16)[:own]
    grad_a, grad_b = gate_gradients(weights, res_grad, skip_grad, keep, tanh_a, sig_b)
    _, _, _, first_bit, second_bit = place()
    weight_gradients(
        grads,
        first_bit if last else second_bit,
        lag[:own],
        xin[:own],
        cond[:own, :],
        grad_a[:own],
        grad_b[:own],
        res_grad[:own],
        skip_grad[:own],
        hidden,
    )
    res = dot_right(hidden, piece(weights, 4))
    skip = dot_right(hidden, piece(weights, 5))
    lag_grad = dot_right(grad_a, piece(weights, 0)) + dot_right(grad_b, piece(weights, 1))
    now = dot_right(grad_a[:own], piece(weights, 2)) + dot_right(grad_b[:own], piece(weights, 3))
    if last:
        res, skip, now, lag_grad = (
            before[...] + value for before, value in zip(earlier, (res, skip, now, lag_grad))
        )
        mixed[...] = (u2[:own, :] + res) * ROOT_HALF
        total[...] = s1[...] + skip
        pushed = (lag_grad * marks[:, 2:3]).astype(BF16).astype(F32)
        g2[...] = cot[:own, :] * ROOT_HALF + now + pltpu.roll(pushed, rows - 1, 0)[:own]
    else:
        mixed[...] = res
        total[...] = skip
        g2[...] = now
        lag_sum[...] = lag_grad


def third_body(own, last, g2, x, lag, cond, marks, cot_skip, ta, sb, hid, weights, *refs):
    earlier, (g1, dlag, lag_sum, grads) = refs[:-4], refs[-4:]
    keep = marks[:own, 0:1]
    xin = x[:own, :].astype(BF16)
    res_grad = (g2[...] * ROOT_HALF).astype(BF16)
    skip_grad = cot_skip[:own, :]
    grad_a, grad_b = gate_gradients(weights, res_grad, skip_grad, keep, ta[...], sb[...])
    _, _, _, first_bit, second_bit = place()
    weight_gradients(
        grads,
        first_bit if last else second_bit,
        lag[...],
        xin,
        cond[:own, :],
        grad_a,
        grad_b,
        res_grad,
        skip_grad,
        hid[...],
    )
    lag_grad = dot_right(grad_a, piece(weights, 0)) + dot_right(grad_b, piece(weights, 1))
    now = dot_right(grad_a, piece(weights, 2)) + dot_right(grad_b, piece(weights, 3))
    if last:
        g1[...] = g2[...] * ROOT_HALF + (earlier[0][...] + now)
        dlag[...] = ((earlier[1][...] + lag_grad) * marks[:own, 1:2]).astype(BF16)
    else:
        g1[...] = now
        lag_sum[...] = lag_grad


def join_body(kept, got, mel, mask, x, cot, skip, side, before, after, tail):
    core = place()[2]
    own, width = kept.shape[0], kept.shape[1] // 3
    for index, ref in enumerate((x, cot, skip)):
        for source, at in ((kept, core), (got, 1 - core)):
            value = source[:, index * width : (index + 1) * width]
            ref[:, pl.ds(at * width, width)] = value.astype(ref.dtype)
    bands = mel.shape[0]
    samples = pl.ds(core * own, own)
    stack = jnp.concatenate(
        [
            mel[:, samples],
            mask[:, samples].astype(F32),
            jnp.zeros((LANES - bands - 1, own), F32),
        ],
        axis=0,
    )
    side[...] = stack.T
    full = 2 * width
    for ref, edge in ((before, own - EDGE), (after, 0)):
        ref[:, :LANES] = side[edge : edge + EDGE, :]
        ref[:, LANES : LANES + full] = x[edge : edge + EDGE, :]
    before[:, LANES + full :] = x[:EDGE, :]
    tail[...] = x[own - EDGE :, :]
    after[:, LANES + full : LANES + 2 * full] = cot[:EDGE, :]
    after[:, LANES + 2 * full :] = skip[:EDGE, :]


def widen_body(
    mel,
    clips,
    lengths,
    x,
    cot,
    skip,
    side,
    before,
    after,
    x_out,
    cot_out,
    skip_out,
    cond,
    marks,
):
    far, near, core = place()[:3]
    own, full = x.shape
    wide = own + 2 * EDGE

    def widened(at, inner):
        return jnp.concatenate(
            [inner, after[:, at : at + inner.shape[1]], before[:, at : at + inner.shape[1]]], axis=0
        )

    x_wide = widened(LANES, x[...])
    x_out[...] = x_wide
    blank = jnp.zeros((EDGE, full), F32)
    cot_out[...] = jnp.concatenate(
        [cot[...], after[:, LANES + full : LANES + 2 * full], blank], axis=0
    )
    skip_out[...] = jnp.concatenate([skip[...], after[:, LANES + 2 * full :], blank], axis=0).astype(
        BF16
    )
    side_wide = widened(0, side[...])
    lane = lax.broadcasted_iota(jnp.int32, (wide, LANES), 1)
    line = lax.broadcasted_iota(jnp.int32, (wide, LANES), 0)
    first = ((far * NEAR + near) * 2 + core) * own
    position = first + jnp.where(line < own + EDGE, line, line - wide)

    def segment(at):
        total = jnp.zeros((wide, LANES), jnp.int32)
        end = jnp.int32(0)
        for clip in range(clips):
            end = end + lengths[clip]
            total = total + (at >= end).astype(jnp.int32)
        return total

    here = segment(position)

    def valid(span):
        return ((position >= span) & (segment(position - span) == here)).astype(F32)

    hot = ((lane - mel) == here).astype(F32)
    value = jnp.where(lane < mel, side_wide, jnp.where(lane < mel + clips, hot, 0.0))
    cond[...] = jnp.where(lane == mel + clips, 1.0, value).astype(BF16)
    keep = side_wide[:, mel : mel + 1]
    marks[...] = jnp.where(
        lane == 0, keep, jnp.where(lane == 1, valid(FIRST_DILATION), valid(1))
    )


def lag_body(same, other, before, tail, out):
    core = place()[2]
    own, width = same.shape[0] // 2, same.shape[1]
    for source, at in ((same, core), (other, 1 - core)):
        out[:own, pl.ds(at * width, width)] = source[pl.ds(core * own, own), :]
    edges = [before[:, LANES + 2 * width :], tail[...]]
    out[own:, :] = jnp.concatenate(edges, axis=0).astype(BF16)


def divide_body(mixed, total, g1, kept, given):
    core = place()[2]
    width = kept.shape[1] // 3
    for index, ref in enumerate((mixed, total, g1)):
        kept[:, index * width : (index + 1) * width] = ref[:, pl.ds(core * width, width)]
        given[:, index * width : (index + 1) * width] = ref[:, pl.ds((1 - core) * width, width)]


def finish_body(kept, got, *refs):
    core = place()[2]
    outs, token = refs[:-1], refs[-1]
    token[...] = jnp.zeros_like(token)
    own, width = kept.shape[0], kept.shape[1] // 3
    for index, ref in enumerate(outs):
        for source, at in ((kept, core), (got, 1 - core)):
            ref[pl.ds(at * own, own), :] = source[:, index * width : (index + 1) * width]


def push_body(dlag, *refs):
    core = place()[2]
    same, other = refs[-2:]
    width = same.shape[1]
    same[...] = dlag[:, pl.ds(core * width, width)]
    other[...] = dlag[:, pl.ds((1 - core) * width, width)]


def input_gradient_body(g1, same, other, out):
    core = place()[2]
    own = same.shape[0]
    for source, at in ((same, core), (other, 1 - core)):
        lines = pl.ds(at * own, own)
        out[lines, :] = g1[lines, :] + source[...].astype(F32)


def table_gradient(cond_grad, who, mel, clips, speakers):
    lane = lax.broadcasted_iota(jnp.int32, (cond_grad.shape[0], speakers), 1)
    result = jnp.zeros((cond_grad.shape[0], speakers), F32)
    for clip in range(clips):
        column = cond_grad[:, mel + clip : mel + clip + 1]
        result = result + jnp.where(lane == who[clip], column, 0.0)
    return result


def square_body(rows, mel, clips, speakers, count, who, *refs):
    terms, (out, squares) = refs[:count], refs[-2:]
    where, total = sections(rows)
    start = where[6][0]
    value = terms[0][...]
    for term in terms[1:]:
        value = value + term[...].astype(F32)
    out[...] = value
    main = out[:start, :]
    amount = jnp.sum(main * main, keepdims=True)
    for half in range(2):
        block = out[start:, half * LANES : (half + 1) * LANES]
        lane = lax.broadcasted_iota(jnp.int32, block.shape, 1)
        plain = jnp.where((lane < mel) | (lane == mel + clips), block, 0.0)
        amount = amount + jnp.sum(plain * plain, keepdims=True)
        table = table_gradient(block, who, mel, clips, speakers)
        amount = amount + jnp.sum(table * table, keepdims=True)
    squares[...] = jnp.broadcast_to(amount, squares.shape)


def adamw(weight, mean, square, gradient, scale):
    clipped = gradient * scale
    new_mean = BETA_ONE * mean + (1.0 - BETA_ONE) * clipped
    new_square = BETA_TWO * square + (1.0 - BETA_TWO) * clipped * clipped
    fix_one = 1.0 - BETA_ONE**STEP
    fix_two = 1.0 - BETA_TWO**STEP
    update = new_mean / fix_one / (jnp.sqrt(new_square / fix_two) + ADAM_EPS)
    return weight - LEARN_RATE * (update + DECAY * weight), new_mean, new_square


def update_body(rows, mel, clips, who, *refs):
    grads = refs[0:2]
    squares = refs[2]
    old = [refs[3 + 3 * kind : 6 + 3 * kind] for kind in range(6)]
    norm = refs[21]
    new = [refs[22 + 5 * kind : 27 + 5 * kind] for kind in range(6)]
    where, total = sections(rows)
    chans = rows // 2
    grad_norm = jnp.sqrt(jnp.sum(squares[...], axis=0, keepdims=True)[:, 0:1])
    norm[...] = grad_norm
    scale = jnp.minimum(1.0, CLIP_NORM / grad_norm)

    def write(kind, index, gradient):
        weight, mean, square = (ref[index] for ref in old[kind])
        new_weight, new_mean, new_square = adamw(weight, mean, square, gradient, scale)
        for ref, value in zip(
            new[kind],
            (gradient, new_weight, new_mean, new_square, new_weight.astype(BF16)),
        ):
            ref[index] = value

    dil = new[0][0]
    for layer in range(2):
        for tap in range(2):
            for half in range(2):
                at, n = where[2 * tap + half]
                for tile in range(2):
                    dil[strided(layer, tap, half, tile, rows), :] = grads[layer][
                        at : at + n, tile * LANES : (tile + 1) * LANES
                    ]
    weight, mean, square = (ref[...] for ref in old[0])
    new_weight, new_mean, new_square = adamw(weight, mean, square, dil[...], scale)
    new[0][1][...] = new_weight
    new[0][2][...] = new_mean
    new[0][3][...] = new_square
    new[0][4][...] = new_weight.astype(BF16)
    for layer in range(2):
        for half in range(2):
            block = grads[layer][where[6][0] :, half * LANES : (half + 1) * LANES]
            eye = lax.broadcasted_iota(jnp.int32, (chans, chans), 0) == lax.broadcasted_iota(
                jnp.int32, (chans, chans), 1
            )
            column = block[:, mel + clips : mel + clips + 1]
            line = jnp.sum(jnp.where(eye, column, 0.0), axis=0, keepdims=True)
            write(1, (layer, slice(half, half + 1), slice(None)), line)
            write(2, (layer, half), block[:, :mel])
            speakers = old[3][0].shape[-1]
            write(3, (layer, half), table_gradient(block, who, mel, clips, speakers))
        for kind, section in ((4, 4), (5, 5)):
            at, n = where[section]
            write(kind, (layer,), grads[layer][at : at + n, :])


def on_device(
    x_input,
    mel_frames,
    sample_mask,
    clip_length_array,
    speaker_ids,
    cot_out,
    cot_skip,
    *states,
):
    parts = lax.axis_size("tm")
    held_rows, width = x_input.shape
    own, full = held_rows // 2, 2 * width
    wide = own + 2 * EDGE
    mel = mel_frames.shape[0]
    clips = clip_length_array.shape[0]
    hop = FIRST_DILATION // held_rows

    dil_shape = states[0].shape
    rows = dil_shape[2]
    views = (
        [dilated_view(s) for s in states[0:3]]
        + list(states[3:6])
        + [s.transpose(0, 2, 3, 1) for s in states[6:12]]
        + [s.transpose(0, 2, 1) for s in states[12:18]]
    )
    speakers = views[9].shape[-1]
    where, total = sections(rows)
    far = parts // NEAR
    taken = [views[k] for k in (0, 12, 15, 6, 9, 3)]
    packed_type = BF16 if rows % 32 == 0 else F32
    taken = [views[k] for k in (0, 12, 15, 6, 9, 3)]
    packed_type = BF16 if rows % 32 == 0 else F32
    pack_one, pack_two, kept, given, x_low = call(
        functools.partial(start_body, rows, mel, clips),
        (struct((total, 256), packed_type),) * 2
        + (struct((own, 3 * width)),) * 2
        + (struct(x_input.shape, BF16),),
        *taken,
        x_input,
        cot_out,
        cot_skip,
        scalars=(speaker_ids,),
        space=pl.ANY,
        grant=None,
        scratch=[pltpu.VMEM(v.shape, F32) for v in taken + [x_input]]
        + [pltpu.SemaphoreType.DMA((len(taken) + 7,))],
    )
    lag_same = shifted(x_low, "tm", hop)
    lag_other = swap_cores(lag_same)

    x_own, cot_own, skip_own, side, before, after, tail = call(
        join_body,
        (
            struct((own, full)),
            struct((own, full)),
            struct((own, full)),
            struct((own, LANES)),
            struct((EDGE, LANES + 2 * full)),
            struct((EDGE, LANES + 3 * full)),
            struct((EDGE, full)),
        ),
        kept,
        swap_cores(given),
        mel_frames,
        sample_mask[None, :],
    )
    before = shifted(before, BOTH, 1)
    x_wide, cot_wide, skip_wide, cond, marks = call(
        functools.partial(widen_body, mel, clips),
        (
            struct((wide, full)),
            struct((wide, full)),
            struct((wide, full), BF16),
            struct((wide, LANES), BF16),
            struct((wide, LANES)),
        ),
        x_own,
        cot_own,
        skip_own,
        side,
        before,
        shifted(after, BOTH, -1),
        scalars=(clip_length_array,),
    )
    group_one, stacked = along_all(pack_one.astype(BF16), (marks, lag_same))
    pack_two, _ = call(
        relay_body, (struct(pack_two.shape, BF16), TOKEN), pack_two.astype(BF16), unread=(stacked,)
    )
    group_two, stacked = along_all(pack_two, ())
    lag_wide = call(
        lag_body,
        struct((wide, full), BF16),
        lag_same,
        lag_other,
        before,
        shifted(tail, BOTH, 2 * hop + 1),
    )
    parts_one, _ = near_exchange(group_one, (stacked, lag_wide))
    parts_two, begun = near_exchange(group_two, ())
    w1_own, w1_oth = joined(parts_one, ())

    half = struct((own, width))
    wave = struct((own, full))
    broad = struct((wide, full))
    low_half = struct((own, width), BF16)
    low_full = struct((own, full), BF16)
    packed = struct((BLOCKS, ROWS, 256), BF16)

    def forward(weights, *earlier, unread=(), flops=1024):
        return call(
            functools.partial(first_body, own),
            (broad, wave, low_full, half, half, low_half, TOKEN),
            x_wide,
            lag_wide,
            cond,
            marks,
            weights,
            *earlier,
            unread=unread,
            flops=flops,
        )

    res, skip, lag1, ta_own, sb_own, hid_own, _ = forward(w1_own, unread=(begun,), flops=LONG)
    u2, s1, _, ta_oth, sb_oth, hid_oth, token = forward(w1_oth, res, skip)

    w2_own, w2_oth = joined(parts_two, (token,))

    def middle(weights, *earlier):
        return call(
            functools.partial(second_body, own),
            (wave, wave, wave, TOKEN if earlier else broad, packed),
            u2,
            s1,
            cond,
            marks,
            cot_wide,
            skip_wide,
            weights,
            *earlier,
        )

    gate_two = call(
        second_forward_body, (struct((wide, width)),) * 2, u2, cond, marks, w2_own
    )
    *sums, grad_oth = middle(w2_oth)
    mixed, skip_total, g2, _, grad_own = middle(w2_own, *sums, *gate_two)

    def totals(terms, unread=()):
        return call(
            functools.partial(square_body, rows, mel, clips, speakers, len(terms)),
            (struct((total, 256)), struct((8, LANES))),
            *terms,
            scalars=(speaker_ids,),
            unread=unread,
        )

    def backward(weights, tanh_a, sig_b, hidden, *earlier, unread):
        last = bool(earlier)
        return call(
            functools.partial(third_body, own, last),
            (wave, low_full if last else TOKEN, TOKEN if last else wave, packed),
            g2,
            x_wide,
            lag1,
            cond,
            marks,
            skip_wide,
            tanh_a,
            sig_b,
            hidden,
            weights,
            *earlier,
            unread=unread,
        )

    grads2, sent2, token = cores_summed(grad_own, grad_oth)
    now, _, lag_sum, grad_oth = backward(w1_oth, ta_oth, sb_oth, hid_oth, unread=(token,))
    grads2, sent2, token = near_summed(grads2, sent2, LONG)
    g1_part, dlag1, _, grad_own = backward(
        w1_own, ta_own, sb_own, hid_own, now, lag_sum, unread=()
    )
    grads1, sent1, _ = cores_summed(grad_own, grad_oth, (token,))
    kept, given = call(
        divide_body, (struct((own, 3 * width)),) * 2, mixed, skip_total, g1_part
    )
    mixed, skip_total, grad_input, token = call(
        finish_body, (struct((held_rows, width)),) * 3 + (TOKEN,), kept, swap_cores(given)
    )
    last_got = across(sent2, 0)
    grads1, sent1, _ = near_summed(grads1, sent1, unread=(last_got, token))
    terms2, _ = far_terms(grads2, last_got)
    terms1, token = far_terms(grads1, across(sent1, 0))
    same, other = call(push_body, (low_half,) * 2, dlag1, unread=(token,))
    same = shifted(same, "tm", -hop)
    other = crossed(other, -hop)
    grad_input = call(input_gradient_body, struct((held_rows, width)), grad_input, same, other)

    sum2, squares2 = totals(terms2)
    sum1, squares1 = totals(terms1, (same, other))
    squares = squares1[:1] + squares2[:1]
    squares = squares + swap_cores(squares)
    sent = jnp.broadcast_to(squares[None], (parts, 1, LANES))
    squares = lax.all_to_all(sent, "tm", split_axis=0, concat_axis=0, tiled=True)
    outs = [struct((1, 1))]
    for view in views[0::3]:
        outs += [struct(view.shape)] * 4 + [struct(view.shape, BF16)]
    updated = call(
        functools.partial(update_body, rows, mel, clips),
        tuple(outs),
        sum1,
        sum2,
        squares.reshape(parts, LANES),
        *views,
        scalars=(speaker_ids,),
    )
    grad_norm = updated[0].reshape(())
    backs = (
        [lambda v: dilated_back(v, dil_shape), lambda v: v]
        + [lambda v: v.transpose(0, 3, 1, 2)] * 2
        + [lambda v: v.transpose(0, 2, 1)] * 2
    )
    new = [
        [back(v) for v in updated[1 + 5 * kind : 6 + 5 * kind]] for kind, back in enumerate(backs)
    ]
    return (
        mixed,
        skip_total,
        grad_input,
        grad_norm,
        *[group[0] for group in new],
        *[value for group in new for value in group[1:4]],
        *[group[4] for group in new],
    )


def solution(mesh):
    rows = P("tm", "mp")
    dil = P(None, None, "tm", None, "mp")
    bias = P(None, None, ("mp", "tm"))
    wide = P(None, None, None, ("mp", "tm"))
    square = P(None, "mp", "tm")
    kinds = (dil, bias, wide, wide, square, square)
    thrice = tuple(kind for kind in kinds for _ in range(3))
    return jax.shard_map(
        on_device,
        mesh=mesh,
        in_specs=(rows, P(None, "tm"), P("tm"), P(), P(), rows, rows) + thrice,
        out_specs=(rows, rows, rows, P()) + kinds + thrice + kinds,
        check_vma=False,
    )
```

```python
import functools

import jax
import jax.numpy as jnp
from jax import lax
from jax.experimental import pallas as pl
from jax.experimental.pallas import tpu as pltpu
from jax.sharding import PartitionSpec as P

FIRST_DILATION = 512
STEP = 10
ROOT_HALF = 0.7071067811865476
BETA_ONE = 0.9
BETA_TWO = 0.999
ADAM_EPS = 1e-08
LEARN_RATE = 0.07
DECAY = 0.01
CLIP_NORM = 1.0

F32 = jnp.float32
BF16 = jnp.bfloat16
LANES = 128
EDGE = 8
BLOCKS = 16
NEAR = 4
VMEM_BYTES = 26 * 1024 * 1024
BOTH = ("tm", "mp")


def struct(shape, dtype=F32):
    return jax.ShapeDtypeStruct(shape, dtype)


def call(body, out_shape, *operands, scalars=(), scratch=(), space=pltpu.VMEM, unread=(), flops=1024, grant=VMEM_BYTES):
    specs = [pl.BlockSpec(memory_space=pltpu.SMEM)] * len(scalars)
    specs += [pl.BlockSpec(memory_space=space)] * len(operands)
    specs += [pl.BlockSpec(memory_space=pl.ANY)] * len(unread)
    return pl.pallas_call(
        body,
        out_shape=out_shape,
        in_specs=specs,
        scratch_shapes=list(scratch),
        compiler_params=pltpu.CompilerParams(vmem_limit_bytes=grant),
        cost_estimate=pl.CostEstimate(flops=flops, bytes_accessed=1024, transcendentals=0),
    )(*scalars, *operands, *unread)


def dot(left, right):
    return jnp.dot(left, right, preferred_element_type=F32)


def dot_right(left, right):
    return lax.dot_general(left, right, (((1,), (1,)), ((), ())), preferred_element_type=F32)


def dot_left(left, right):
    return lax.dot_general(left, right, (((0,), (0,)), ((), ())), preferred_element_type=F32)


def place():
    index = lax.axis_index("tm")
    core = lax.axis_index("mp")
    return index // NEAR, index % NEAR, core, 1 + core, 2 - core


def route(target):
    return [
        (index * 2 + core, target(index, core) * 2 + core)
        for index in range(lax.axis_size("tm"))
        for core in range(2)
    ]


def across(value, bit):
    return lax.ppermute(value, BOTH, route(lambda i, c: i ^ (1 + (c ^ bit))))


def along_far(value, distance):
    far = lax.axis_size("tm") // NEAR
    return lax.ppermute(
        value, BOTH, route(lambda i, c: (i // NEAR + distance) % far * NEAR + i % NEAR)
    )


def swap_cores(value):
    return lax.ppermute(value, "mp", [(0, 1), (1, 0)])


def shifted(value, axis, distance):
    devices = range(lax.axis_size(axis))
    pairs = [(i - distance, i) for i in devices if i - distance in devices]
    return lax.ppermute(value, axis, pairs)


def across_chips(value):
    pairs = []
    for index in range(1, lax.axis_size("tm")):
        pairs += [(index * 2 - 1, index * 2), (index * 2, index * 2 - 1)]
    return lax.ppermute(value, BOTH, pairs)


def sections(rows):
    found, at = [], 0
    for count in (rows,) * 6 + (rows // 2,):
        found.append((at, count))
        at += count
    return found, at


WHERE, ROWS = sections(32)


def dilated_view(array):
    layers, taps, rows, halves, width = array.shape
    tiles = width // LANES
    split = array.reshape(layers, taps, rows, halves, tiles, LANES)
    return split.transpose(0, 1, 2, 4, 3, 5).reshape(-1, LANES)


def dilated_back(array, shape):
    layers, taps, rows, halves, width = shape
    tiles = width // LANES
    split = array.reshape(layers, taps, rows, tiles, halves, LANES)
    return split.transpose(0, 1, 2, 4, 3, 5).reshape(shape)


def strided(layer, tap, half, tile, rows):
    return pl.ds((layer * 2 + tap) * rows * 4 + tile * 2 + half, rows, stride=4)


def start_body(rows, mel, clips, who, *refs):
    sources, (out_one, out_two, low), held, sems = refs[:7], refs[7:10], refs[10:17], refs[17]
    copies = [
        pltpu.make_async_copy(source, target, sems.at[index])
        for index, (source, target) in enumerate(zip(sources, held))
    ]
    for copy in copies:
        copy.start()
    dil, res, skip, mel_w, table, bias, samples = held
    where, total = sections(rows)
    chans = rows // 2
    speakers = table.shape[-1]
    lane = lax.broadcasted_iota(jnp.int32, (1, speakers), 1)
    hot = jnp.concatenate([(lane == who[k]).astype(F32) for k in range(clips)], axis=0).astype(BF16)
    eye = lax.broadcasted_iota(jnp.int32, (chans, chans), 0) == lax.broadcasted_iota(
        jnp.int32, (chans, chans), 1
    )

    def write(out, at, count, columns, value):
        out[at : at + count, columns] = value.astype(out.dtype)

    for copy in copies[:-1]:
        copy.wait()
    for layer, out in enumerate((out_one, out_two)):
        for tap in range(2):
            for half in range(2):
                at, count = where[2 * tap + half]
                for tile in range(2):
                    part = dil[strided(layer, tap, half, tile, rows), :]
                    write(out, at, count, slice(tile * LANES, (tile + 1) * LANES), part)
        for kind, source in ((4, res), (5, skip)):
            at, count = where[kind]
            write(out, at, count, slice(None), source[layer])
        at, count = where[6]
        for half in range(2):
            picked = dot_right(table[layer, half].astype(BF16), hot)
            line = jnp.broadcast_to(bias[layer, half : half + 1, :], (chans, chans))
            column = jnp.sum(jnp.where(eye, line, 0.0), axis=1, keepdims=True)
            blank = jnp.zeros((chans, LANES - mel - clips - 1), F32)
            row = jnp.concatenate([mel_w[layer, half], picked, column, blank], axis=1)
            columns = slice(half * LANES, (half + 1) * LANES)
            write(out, at, count, columns, row.astype(BF16).astype(F32))
    copies[-1].wait()
    low[...] = samples[...].astype(BF16)


def assemble_body(group, first, second, last, *refs):
    out = refs[-1]
    count = group.shape[0]
    far, near, _, first_bit, second_bit = place()
    for ref, mask in ((group, 0), (first, first_bit), (second, second_bit), (last, 3)):
        for back in range(count):
            out[lax.rem(far + count - back, count) * NEAR + (near ^ mask)] = ref[back]


def relay_body(value, *refs):
    out, token = refs[-2:]
    out[...] = value[...]
    token[...] = jnp.zeros_like(token)


TOKEN = struct((8, LANES))
LONG = 20_000_000_000


def stack_body(count, *refs):
    out, token = refs[-2:]
    for index in range(count):
        out[index] = refs[index][...]
    token[...] = jnp.zeros_like(token)


def along_all(pack, unread):
    far = lax.axis_size("tm") // NEAR
    got = [along_far(pack, distance) for distance in range(1, far)]
    return call(
        functools.partial(stack_body, far),
        (struct((far,) + pack.shape, BF16), TOKEN),
        pack,
        *got,
        unread=unread,
    )


def near_exchange(group, before_last):
    first = across(group, 0)
    second = across(group, 1)
    passed, token = call(
        relay_body, (struct(first.shape, BF16), TOKEN), first, unread=(second,) + before_last
    )
    return (group, first, second, across(passed, 1)), token


def joined(parts, before_end):
    count = NEAR * parts[0].shape[0]
    own = call(
        assemble_body, struct((count,) + parts[0].shape[1:], BF16), *parts, unread=before_end
    )
    if count != BLOCKS:
        own = to_canonical(own)
    return own, swap_cores(own)


def to_canonical(gathered):
    parts = gathered.shape[0]
    where, total = sections(BLOCKS * 32 // parts)
    return jnp.concatenate(
        [gathered[:, at : at + n, :].reshape(BLOCKS, -1, 256) for at, n in where], axis=1
    )


def from_canonical(packed, parts):
    where, total = sections(32)
    return jnp.concatenate(
        [packed[:, at : at + n, :].reshape(parts, -1, 256) for at, n in where], axis=1
    )


def piece(ref, kind):
    at, count = WHERE[kind]
    return ref[:, at : at + count, :].reshape(-1, 256)


def conditioning(ref, half):
    at, count = WHERE[6]
    return ref[:, at : at + count, half * LANES : (half + 1) * LANES].reshape(-1, LANES)


def slot(ordered, first, block):
    if not ordered:
        return block
    near = lax.axis_index("tm") % NEAR
    mask = (block % NEAR) ^ near
    group = jnp.where(mask == 3, 0, jnp.where(mask == 0, 3, jnp.where(mask == first, 2, 1)))
    return group * (BLOCKS // NEAR) + block // NEAR


def store(ref, slots, kind, value):
    at, count = WHERE[kind]
    value = value.astype(BF16)
    for block in range(BLOCKS):
        ref[slots[block], at : at + count, :] = value[block * count : (block + 1) * count]


def store_conditioning(ref, slots, half, value):
    at, count = WHERE[6]
    value = value.astype(BF16)
    for block in range(BLOCKS):
        ref[slots[block], at : at + count, half * LANES : (half + 1) * LANES] = value[
            block * count : (block + 1) * count
        ]


def order_body(own, other, own_out, other_out):
    parts = own.shape[0]
    far = parts // NEAR
    _, near, _, first, second = place()
    for source, out, bit, next_bit in (
        (own, own_out, first, second),
        (other, other_out, second, first),
    ):
        for group, mask in enumerate((3, next_bit, bit, 0)):
            for index in range(far):
                out[group * far + index] = source[index * NEAR + (near ^ mask)]


def first_sum_body(own, got, *refs):
    out, token = refs[-2:]
    half = out.shape[0]
    out[...] = own[:half] + got[:half]
    token[...] = jnp.zeros_like(token)


def second_sum_body(own, got, near_got, *refs):
    out, token = refs[-2:]
    count = out.shape[0]
    kept = slice(2 * count, 3 * count)
    out[...] = (
        own[kept].astype(F32) + got[kept].astype(F32) + near_got[:count].astype(F32)
    ).astype(BF16)
    token[...] = jnp.zeros_like(token)


def third_sum_body(own, got, near_got, last_got, *refs):
    far = place()[0]
    count = last_got.shape[0]
    token = refs[-1]
    token[...] = jnp.zeros_like(token)
    for distance, out in enumerate(refs[-count - 1 : -1]):
        index = lax.rem(far + distance, count)
        out[...] = (
            own[3 * count + index].astype(F32)
            + got[3 * count + index].astype(F32)
            + near_got[count + index].astype(F32)
            + last_got[index].astype(F32)
        ).astype(out.dtype)


def ordered(grads):
    parts = lax.axis_size("tm")
    return grads if parts == BLOCKS else from_canonical(grads, parts)


def cores_summed(own, other, unread=()):
    own, other = ordered(own), ordered(other)
    if own.shape[0] != BLOCKS:
        own, other = call(order_body, (struct(own.shape, BF16),) * 2, own, other)
    got = swap_cores(other)
    half = struct((own.shape[0] // 2,) + own.shape[1:], BF16)
    sent, token = call(first_sum_body, (half, TOKEN), own, got, unread=unread)
    return (own, got), sent, token


def near_summed(grads, sent, flops=1024, unread=()):
    near_got = across(sent, 1)
    shape = (grads[0].shape[0] // NEAR,) + grads[0].shape[1:]
    sent, token = call(
        second_sum_body,
        (struct(shape, BF16), TOKEN),
        *grads,
        near_got,
        flops=flops,
        unread=unread,
    )
    return grads + (near_got,), sent, token


def far_terms(grads, last_got, flops=1024):
    far, *shape = last_got.shape
    kept, *sends, token = call(
        third_sum_body,
        (struct(shape),) + (struct(shape, BF16),) * (far - 1) + (TOKEN,),
        *grads,
        last_got,
        flops=flops,
    )
    return [kept] + [along_far(value, k + 1) for k, value in enumerate(sends)], token


def gates(weights, lag, xin, cond):
    za = dot(lag, piece(weights, 0)) + dot(xin, piece(weights, 2))
    za = za + dot_right(cond, conditioning(weights, 0))
    zb = dot(lag, piece(weights, 1)) + dot(xin, piece(weights, 3))
    zb = zb + dot_right(cond, conditioning(weights, 1))
    return jnp.tanh(za), jax.nn.sigmoid(zb)


def gate_gradients(weights, res_grad, skip_grad, keep, tanh_a, sig_b):
    hidden_grad = dot(res_grad, piece(weights, 4)) + dot(skip_grad, piece(weights, 5))
    hidden_grad = hidden_grad * keep
    grad_a = (hidden_grad * sig_b * (1.0 - tanh_a * tanh_a)).astype(BF16)
    grad_b = (hidden_grad * tanh_a * sig_b * (1.0 - sig_b)).astype(BF16)
    return grad_a, grad_b


def weight_gradients(out, bit, lag, xin, cond, grad_a, grad_b, res_grad, skip_grad, hidden):
    slots = [slot(lax.axis_size("tm") == BLOCKS, bit, block) for block in range(BLOCKS)]
    store(out, slots, 0, dot_left(lag, grad_a))
    store(out, slots, 1, dot_left(lag, grad_b))
    store(out, slots, 2, dot_left(xin, grad_a))
    store(out, slots, 3, dot_left(xin, grad_b))
    store(out, slots, 4, dot_left(res_grad, hidden))
    store(out, slots, 5, dot_left(skip_grad, hidden))
    store_conditioning(out, slots, 0, dot_left(grad_a, cond))
    store_conditioning(out, slots, 1, dot_left(grad_b, cond))


def first_body(own, x, lag_raw, cond, marks, weights, *refs):
    earlier, (u2, s1, lag_out, ta, sb, hid, token) = refs[:-7], refs[-7:]
    token[...] = jnp.zeros_like(token)
    keep = marks[:, 0:1]
    xin = x[...].astype(BF16)
    lag = (lag_raw[...].astype(F32) * marks[:, 1:2]).astype(BF16)
    tanh_a, sig_b = gates(weights, lag, xin, cond[...])
    hidden = (keep * tanh_a * sig_b).astype(BF16)
    res = dot_right(hidden, piece(weights, 4))
    skip = dot_right(hidden[:own], piece(weights, 5))
    ta[...] = tanh_a[:own]
    sb[...] = sig_b[:own]
    hid[...] = hidden[:own]
    lag_out[...] = lag[:own]
    if len(earlier) == 2:
        u2[...] = (x[...] + (earlier[0][...] + res)) * ROOT_HALF
        s1[...] = earlier[1][...] + skip
    else:
        u2[...] = res
        s1[...] = skip


def second_input(u2, marks):
    xin = u2[...].astype(BF16)
    lag = (pltpu.roll(xin.astype(F32), 1, 0) * marks[:, 2:3]).astype(BF16)
    return xin, lag


def second_forward_body(u2, cond, marks, weights, ta, sb):
    xin, lag = second_input(u2, marks)
    ta[...], sb[...] = gates(weights, lag, xin, cond[...])


def second_body(own, u2, s1, cond, marks, cot, cot_skip, weights, *refs):
    last = len(refs) > 5
    earlier, (mixed, total, g2, lag_sum, grads) = refs[:-5], refs[-5:]
    rows = u2.shape[0]
    keep = marks[:, 0:1]
    xin, lag = second_input(u2, marks)
    res_grad = (cot[...] * ROOT_HALF).astype(BF16)
    skip_grad = cot_skip[...]
    if last:
        tanh_a, sig_b = earlier[4][...], earlier[5][...]
    else:
        tanh_a, sig_b = gates(weights, lag, xin, cond[...])
    hidden = (keep * tanh_a * sig_b).astype(BF16)[:own]
    grad_a, grad_b = gate_gradients(weights, res_grad, skip_grad, keep, tanh_a, sig_b)
    _, _, _, first_bit, second_bit = place()
    weight_gradients(
        grads,
        first_bit if last else second_bit,
        lag[:own],
        xin[:own],
        cond[:own, :],
        grad_a[:own],
        grad_b[:own],
        res_grad[:own],
        skip_grad[:own],
        hidden,
    )
    res = dot_right(hidden, piece(weights, 4))
    skip = dot_right(hidden, piece(weights, 5))
    lag_grad = dot_right(grad_a, piece(weights, 0)) + dot_right(grad_b, piece(weights, 1))
    now = dot_right(grad_a[:own], piece(weights, 2)) + dot_right(grad_b[:own], piece(weights, 3))
    if last:
        res, skip, now, lag_grad = (
            before[...] + value for before, value in zip(earlier, (res, skip, now, lag_grad))
        )
        mixed[...] = (u2[:own, :] + res) * ROOT_HALF
        total[...] = s1[...] + skip
        pushed = (lag_grad * marks[:, 2:3]).astype(BF16).astype(F32)
        g2[...] = cot[:own, :] * ROOT_HALF + now + pltpu.roll(pushed, rows - 1, 0)[:own]
    else:
        mixed[...] = res
        total[...] = skip
        g2[...] = now
        lag_sum[...] = lag_grad


def third_body(own, last, g2, x, lag, cond, marks, cot_skip, ta, sb, hid, weights, *refs):
    earlier, (g1, dlag, lag_sum, grads) = refs[:-4], refs[-4:]
    keep = marks[:own, 0:1]
    xin = x[:own, :].astype(BF16)
    res_grad = (g2[...] * ROOT_HALF).astype(BF16)
    skip_grad = cot_skip[:own, :]
    grad_a, grad_b = gate_gradients(weights, res_grad, skip_grad, keep, ta[...], sb[...])
    _, _, _, first_bit, second_bit = place()
    weight_gradients(
        grads,
        first_bit if last else second_bit,
        lag[...],
        xin,
        cond[:own, :],
        grad_a,
        grad_b,
        res_grad,
        skip_grad,
        hid[...],
    )
    lag_grad = dot_right(grad_a, piece(weights, 0)) + dot_right(grad_b, piece(weights, 1))
    now = dot_right(grad_a, piece(weights, 2)) + dot_right(grad_b, piece(weights, 3))
    if last:
        lag_sum[...] = jnp.zeros_like(lag_sum)
        g1[...] = g2[...] * ROOT_HALF + (earlier[0][...] + now)
        dlag[...] = ((earlier[1][...] + lag_grad) * marks[:own, 1:2]).astype(BF16)
    else:
        g1[...] = now
        lag_sum[...] = lag_grad


def part_body(x, cot, skip, lag, kept, given, held):
    core = place()[2]
    span, width = kept.shape[0], x.shape[1]
    beyond = x.shape[0] - span
    held[...] = lag[...].astype(F32)
    for index, ref in enumerate((x, cot, skip, held)):
        columns = slice(index * width, (index + 1) * width)
        kept[:, columns] = ref[pl.ds(core * beyond, span), :]
        given[:, columns] = ref[pl.ds((1 - core) * beyond, span), :]


def join_body(kept, got, mel, mask, inner, side, near_edge, edge_sent, held, lines):
    core = place()[2]
    span, width = kept.shape[0], kept.shape[1] // 4
    own, beyond = inner.shape[0], mel.shape[1] - span
    for index in range(4):
        for source, at in ((kept, core), (got, 1 - core)):
            held[:, pl.ds(index * 2 * width + at * width, width)] = source[
                :, index * width : (index + 1) * width
            ]
    blank = jnp.zeros((LANES - mel.shape[0] - 1, mel.shape[1]), F32)
    lines[...] = jnp.concatenate([mel[...], mask[...].astype(F32), blank], axis=0).T
    inner[...] = held[pl.ds(core * EDGE, own), :]
    side[...] = lines[pl.ds(core * own, own), :]
    for ref, at in ((near_edge, (1 - core) * own), (edge_sent, core * own)):
        ref[:, LANES:] = held[pl.ds(at, EDGE), :]
        ref[:, :LANES] = lines[pl.ds(core * beyond + at, EDGE), :]


def widen_body(
    mel, clips, lengths, inner, side, near_edge, edge, x_out, cot_out, skip_out, lag_out, cond, marks
):
    far, near, core = place()[:3]
    own, full = inner.shape[0], inner.shape[1] // 4
    wide = own + 2 * EDGE
    after = jnp.where(core == 0, near_edge[...], edge[...])
    before = jnp.where(core == 0, edge[...], near_edge[...])
    for index, ref in enumerate((x_out, cot_out, skip_out, lag_out)):
        at = LANES + index * full
        ref[...] = jnp.concatenate(
            [
                inner[:, index * full : (index + 1) * full],
                after[:, at : at + full],
                before[:, at : at + full],
            ],
            axis=0,
        ).astype(ref.dtype)
    side_wide = jnp.concatenate([side[...], after[:, :LANES], before[:, :LANES]], axis=0)
    lane = lax.broadcasted_iota(jnp.int32, (wide, LANES), 1)
    line = lax.broadcasted_iota(jnp.int32, (wide, LANES), 0)
    first = ((far * NEAR + near) * 2 + core) * own
    position = first + jnp.where(line < own + EDGE, line, line - wide)

    def segment(at):
        total = jnp.zeros((wide, LANES), jnp.int32)
        end = jnp.int32(0)
        for clip in range(clips):
            end = end + lengths[clip]
            total = total + (at >= end).astype(jnp.int32)
        return total

    here = segment(position)

    def valid(span):
        return ((position >= span) & (segment(position - span) == here)).astype(F32)

    hot = ((lane - mel) == here).astype(F32)
    value = jnp.where(lane < mel, side_wide, jnp.where(lane < mel + clips, hot, 0.0))
    cond[...] = jnp.where(lane == mel + clips, 1.0, value).astype(BF16)
    keep = side_wide[:, mel : mel + 1]
    marks[...] = jnp.where(
        lane == 0, keep, jnp.where(lane == 1, valid(FIRST_DILATION), valid(1))
    )


def divide_body(mixed, total, g1, push, *refs):
    core = place()[2]
    kept, given, held = refs[-3:]
    width = kept.shape[1] // 4
    held[...] = push[...].astype(F32)
    for index, ref in enumerate((mixed, total, g1, held)):
        columns = slice(index * width, (index + 1) * width)
        kept[:, columns] = ref[:, pl.ds(core * width, width)]
        given[:, columns] = ref[:, pl.ds((1 - core) * width, width)]


def finish_body(kept, got, *refs):
    core = place()[2]
    outs, token = refs[:-1], refs[-1]
    token[...] = jnp.zeros_like(token)
    own, width = kept.shape[0], kept.shape[1] // 4
    for index, ref in enumerate(outs):
        for source, at in ((kept, core), (got, 1 - core)):
            ref[pl.ds(at * own, own), :] = source[:, index * width : (index + 1) * width]


def push_body(push, *refs):
    refs[-1][...] = push[...].astype(BF16)


def input_gradient_body(g1, push, out):
    out[...] = g1[...] + push[...].astype(F32)


def table_gradient(cond_grad, who, mel, clips, speakers):
    lane = lax.broadcasted_iota(jnp.int32, (cond_grad.shape[0], speakers), 1)
    result = jnp.zeros((cond_grad.shape[0], speakers), F32)
    for clip in range(clips):
        column = cond_grad[:, mel + clip : mel + clip + 1]
        result = result + jnp.where(lane == who[clip], column, 0.0)
    return result


def square_body(rows, mel, clips, speakers, count, who, *refs):
    terms, (out, squares) = refs[:count], refs[-2:]
    where, total = sections(rows)
    start = where[6][0]
    value = terms[0][...]
    for term in terms[1:]:
        value = value + term[...].astype(F32)
    out[...] = value
    main = out[:start, :]
    amount = jnp.sum(main * main, keepdims=True)
    for half in range(2):
        block = out[start:, half * LANES : (half + 1) * LANES]
        lane = lax.broadcasted_iota(jnp.int32, block.shape, 1)
        plain = jnp.where((lane < mel) | (lane == mel + clips), block, 0.0)
        amount = amount + jnp.sum(plain * plain, keepdims=True)
        table = table_gradient(block, who, mel, clips, speakers)
        amount = amount + jnp.sum(table * table, keepdims=True)
    squares[...] = jnp.broadcast_to(amount, squares.shape)


def adamw(weight, mean, square, gradient, scale):
    clipped = gradient * scale
    new_mean = BETA_ONE * mean + (1.0 - BETA_ONE) * clipped
    new_square = BETA_TWO * square + (1.0 - BETA_TWO) * clipped * clipped
    fix_one = 1.0 - BETA_ONE**STEP
    fix_two = 1.0 - BETA_TWO**STEP
    update = new_mean / fix_one / (jnp.sqrt(new_square / fix_two) + ADAM_EPS)
    return weight - LEARN_RATE * (update + DECAY * weight), new_mean, new_square


def update_body(rows, mel, clips, who, *refs):
    grads = refs[0:2]
    squares = refs[2]
    old = [refs[3 + 3 * kind : 6 + 3 * kind] for kind in range(6)]
    norm = refs[21]
    new = [refs[22 + 5 * kind : 27 + 5 * kind] for kind in range(6)]
    where, total = sections(rows)
    chans = rows // 2
    grad_norm = jnp.sqrt(jnp.sum(squares[...], axis=0, keepdims=True)[:, 0:1])
    norm[...] = grad_norm
    scale = jnp.minimum(1.0, CLIP_NORM / grad_norm)

    def write(kind, index, gradient):
        weight, mean, square = (ref[index] for ref in old[kind])
        new_weight, new_mean, new_square = adamw(weight, mean, square, gradient, scale)
        for ref, value in zip(
            new[kind],
            (gradient, new_weight, new_mean, new_square, new_weight.astype(BF16)),
        ):
            ref[index] = value

    dil = new[0][0]
    for layer in range(2):
        for tap in range(2):
            for half in range(2):
                at, n = where[2 * tap + half]
                for tile in range(2):
                    dil[strided(layer, tap, half, tile, rows), :] = grads[layer][
                        at : at + n, tile * LANES : (tile + 1) * LANES
                    ]
    weight, mean, square = (ref[...] for ref in old[0])
    new_weight, new_mean, new_square = adamw(weight, mean, square, dil[...], scale)
    new[0][1][...] = new_weight
    new[0][2][...] = new_mean
    new[0][3][...] = new_square
    new[0][4][...] = new_weight.astype(BF16)
    for layer in range(2):
        for half in range(2):
            block = grads[layer][where[6][0] :, half * LANES : (half + 1) * LANES]
            eye = lax.broadcasted_iota(jnp.int32, (chans, chans), 0) == lax.broadcasted_iota(
                jnp.int32, (chans, chans), 1
            )
            column = block[:, mel + clips : mel + clips + 1]
            line = jnp.sum(jnp.where(eye, column, 0.0), axis=0, keepdims=True)
            write(1, (layer, slice(half, half + 1), slice(None)), line)
            write(2, (layer, half), block[:, :mel])
            speakers = old[3][0].shape[-1]
            write(3, (layer, half), table_gradient(block, who, mel, clips, speakers))
        for kind, section in ((4, 4), (5, 5)):
            at, n = where[section]
            write(kind, (layer,), grads[layer][at : at + n, :])


def on_device(
    x_input,
    mel_frames,
    sample_mask,
    clip_length_array,
    speaker_ids,
    cot_out,
    cot_skip,
    *states,
):
    parts = lax.axis_size("tm")
    held_rows, width = x_input.shape
    own, full = held_rows // 2, 2 * width
    wide = own + 2 * EDGE
    mel = mel_frames.shape[0]
    clips = clip_length_array.shape[0]
    hop = FIRST_DILATION // held_rows

    dil_shape = states[0].shape
    rows = dil_shape[2]
    views = (
        [dilated_view(s) for s in states[0:3]]
        + list(states[3:6])
        + [s.transpose(0, 2, 3, 1) for s in states[6:12]]
        + [s.transpose(0, 2, 1) for s in states[12:18]]
    )
    speakers = views[9].shape[-1]
    where, total = sections(rows)
    far = parts // NEAR
    taken = [views[k] for k in (0, 12, 15, 6, 9, 3)]
    packed_type = BF16 if rows % 32 == 0 else F32
    taken = [views[k] for k in (0, 12, 15, 6, 9, 3)]
    packed_type = BF16 if rows % 32 == 0 else F32
    taken.append(x_input)
    pack_one, pack_two, x_low = call(
        functools.partial(start_body, rows, mel, clips),
        (struct((total, 256), packed_type),) * 2 + (struct(x_input.shape, BF16),),
        *taken,
        scalars=(speaker_ids,),
        space=pl.ANY,
        grant=None,
        scratch=[pltpu.VMEM(v.shape, F32) for v in taken]
        + [pltpu.SemaphoreType.DMA((len(taken),))],
    )

    lag = shifted(x_low, "tm", hop)
    span = own + EDGE
    kept, given = call(
        part_body,
        (struct((span, 4 * width)),) * 2,
        x_input,
        cot_out,
        cot_skip,
        lag,
        scratch=[pltpu.VMEM(x_input.shape, F32)],
    )
    group_one, stacked = along_all(pack_one.astype(BF16), (lag,))
    joined_own = struct((own, 4 * full))
    edge = struct((EDGE, 4 * full + LANES))
    inner, side, near_edge, edge_sent = call(
        join_body,
        (joined_own, struct((own, LANES)), edge, edge),
        kept,
        swap_cores(given),
        mel_frames,
        sample_mask[None, :],
        scratch=[pltpu.VMEM((span, 4 * full), F32), pltpu.VMEM((held_rows, LANES), F32)],
    )
    x_wide, cot_wide, skip_wide, lag_wide, cond, marks = call(
        functools.partial(widen_body, mel, clips),
        (
            struct((wide, full)),
            struct((wide, full)),
            struct((wide, full), BF16),
            struct((wide, full), BF16),
            struct((wide, LANES), BF16),
            struct((wide, LANES)),
        ),
        inner,
        side,
        near_edge,
        across_chips(edge_sent),
        scalars=(clip_length_array,),
    )
    pack_two, _ = call(
        relay_body,
        (struct(pack_two.shape, BF16), TOKEN),
        pack_two.astype(BF16),
        unread=(stacked,),
        flops=LONG,
    )
    group_two, stacked = along_all(pack_two, ())
    parts_one, _ = near_exchange(group_one, (stacked, marks))
    parts_two, begun = near_exchange(group_two, ())
    w1_own, w1_oth = joined(parts_one, ())

    half = struct((own, width))
    wave = struct((own, full))
    broad = struct((wide, full))
    low_half = struct((own, width), BF16)
    low_full = struct((own, full), BF16)
    packed = struct((BLOCKS, ROWS, 256), BF16)

    def forward(weights, *earlier, unread=(), flops=1024):
        return call(
            functools.partial(first_body, own),
            (broad, wave, low_full, half, half, low_half, TOKEN),
            x_wide,
            lag_wide,
            cond,
            marks,
            weights,
            *earlier,
            unread=unread,
            flops=flops,
        )

    res, skip, lag1, ta_own, sb_own, hid_own, _ = forward(w1_own, unread=(begun,), flops=LONG)
    u2, s1, _, ta_oth, sb_oth, hid_oth, token = forward(w1_oth, res, skip)

    w2_own, w2_oth = joined(parts_two, (token,))

    def middle(weights, *earlier):
        return call(
            functools.partial(second_body, own),
            (wave, wave, wave, TOKEN if earlier else broad, packed),
            u2,
            s1,
            cond,
            marks,
            cot_wide,
            skip_wide,
            weights,
            *earlier,
        )

    gate_two = call(
        second_forward_body, (struct((wide, width)),) * 2, u2, cond, marks, w2_own
    )
    *sums, grad_oth = middle(w2_oth)
    mixed, skip_total, g2, _, grad_own = middle(w2_own, *sums, *gate_two)

    def totals(terms, unread=()):
        return call(
            functools.partial(square_body, rows, mel, clips, speakers, len(terms)),
            (struct((total, 256)), struct((8, LANES))),
            *terms,
            scalars=(speaker_ids,),
            unread=unread,
        )

    def backward(weights, tanh_a, sig_b, hidden, *earlier, unread):
        last = bool(earlier)
        return call(
            functools.partial(third_body, own, last),
            (wave, low_full if last else TOKEN, TOKEN if last else wave, packed),
            g2,
            x_wide,
            lag1,
            cond,
            marks,
            skip_wide,
            tanh_a,
            sig_b,
            hidden,
            weights,
            *earlier,
            unread=unread,
        )

    grads2, sent2, token = cores_summed(grad_own, grad_oth)
    now, _, lag_sum, grad_oth = backward(w1_oth, ta_oth, sb_oth, hid_oth, unread=(token,))
    g1_part, dlag1, token, grad_own = backward(
        w1_own, ta_own, sb_own, hid_own, now, lag_sum, unread=()
    )
    grads2, sent2, token = near_summed(grads2, sent2, LONG, (token,))
    grads1, sent1, _ = cores_summed(grad_own, grad_oth, (token,))
    last_got = across(sent2, 0)
    kept, given = call(
        divide_body,
        (struct((own, 4 * width)),) * 2,
        mixed,
        skip_total,
        g1_part,
        dlag1,
        scratch=[pltpu.VMEM((own, full), F32)],
    )
    mixed, skip_total, grad_input, push, token = call(
        finish_body, (struct((held_rows, width)),) * 4 + (TOKEN,), kept, swap_cores(given)
    )
    terms2, far_token = far_terms(grads2, last_got, LONG)
    grads1, sent1, _ = near_summed(grads1, sent1, unread=(token, far_token))
    terms1, token = far_terms(grads1, across(sent1, 0))
    push = call(push_body, struct((held_rows, width), BF16), push, unread=(token,))
    grad_input = call(
        input_gradient_body,
        struct((held_rows, width)),
        grad_input,
        shifted(push, "tm", -hop),
    )

    sum2, squares2 = totals(terms2)
    sum1, squares1 = totals(terms1)
    squares = squares1[:1] + squares2[:1]
    squares = squares + swap_cores(squares)
    sent = jnp.broadcast_to(squares[None], (parts, 1, LANES))
    squares = lax.all_to_all(sent, "tm", split_axis=0, concat_axis=0, tiled=True)
    outs = [struct((1, 1))]
    for view in views[0::3]:
        outs += [struct(view.shape)] * 4 + [struct(view.shape, BF16)]
    updated = call(
        functools.partial(update_body, rows, mel, clips),
        tuple(outs),
        sum1,
        sum2,
        squares.reshape(parts, LANES),
        *views,
        scalars=(speaker_ids,),
    )
    grad_norm = updated[0].reshape(())
    backs = (
        [lambda v: dilated_back(v, dil_shape), lambda v: v]
        + [lambda v: v.transpose(0, 3, 1, 2)] * 2
        + [lambda v: v.transpose(0, 2, 1)] * 2
    )
    new = [
        [back(v) for v in updated[1 + 5 * kind : 6 + 5 * kind]] for kind, back in enumerate(backs)
    ]
    return (
        mixed,
        skip_total,
        grad_input,
        grad_norm,
        *[group[0] for group in new],
        *[value for group in new for value in group[1:4]],
        *[group[4] for group in new],
    )


def solution(mesh):
    rows = P("tm", "mp")
    dil = P(None, None, "tm", None, "mp")
    bias = P(None, None, ("mp", "tm"))
    wide = P(None, None, None, ("mp", "tm"))
    square = P(None, "mp", "tm")
    kinds = (dil, bias, wide, wide, square, square)
    thrice = tuple(kind for kind in kinds for _ in range(3))
    return jax.shard_map(
        on_device,
        mesh=mesh,
        in_specs=(rows, P(None, "tm"), P("tm"), P(), P(), rows, rows) + thrice,
        out_specs=(rows, rows, rows, P()) + kinds + thrice + kinds,
        check_vma=False,
    )
```

```python
import functools

import jax
import jax.numpy as jnp
from jax import lax
from jax.experimental import pallas as pl
from jax.experimental.pallas import tpu as pltpu
from jax.sharding import PartitionSpec as P

FIRST_DILATION = 512
STEP = 10
ROOT_HALF = 0.7071067811865476
BETA_ONE = 0.9
BETA_TWO = 0.999
ADAM_EPS = 1e-08
LEARN_RATE = 0.07
DECAY = 0.01
CLIP_NORM = 1.0

F32 = jnp.float32
BF16 = jnp.bfloat16
LANES = 128
EDGE = 8
BLOCKS = 16
NEAR = 4
VMEM_BYTES = 26 * 1024 * 1024
BOTH = ("tm", "mp")


def struct(shape, dtype=F32):
    return jax.ShapeDtypeStruct(shape, dtype)


def call(body, out_shape, *operands, scalars=(), scratch=(), space=pltpu.VMEM, unread=(), flops=1024, grant=VMEM_BYTES):
    specs = [pl.BlockSpec(memory_space=pltpu.SMEM)] * len(scalars)
    specs += [pl.BlockSpec(memory_space=space)] * len(operands)
    specs += [pl.BlockSpec(memory_space=pl.ANY)] * len(unread)
    return pl.pallas_call(
        body,
        out_shape=out_shape,
        in_specs=specs,
        scratch_shapes=list(scratch),
        compiler_params=pltpu.CompilerParams(vmem_limit_bytes=grant),
        cost_estimate=pl.CostEstimate(flops=flops, bytes_accessed=1024, transcendentals=0),
    )(*scalars, *operands, *unread)


def dot(left, right):
    return jnp.dot(left, right, preferred_element_type=F32)


def dot_right(left, right):
    return lax.dot_general(left, right, (((1,), (1,)), ((), ())), preferred_element_type=F32)


def dot_left(left, right):
    return lax.dot_general(left, right, (((0,), (0,)), ((), ())), preferred_element_type=F32)


def place():
    index = lax.axis_index("tm")
    core = lax.axis_index("mp")
    return index // NEAR, index % NEAR, core, 1 + core, 2 - core


def route(target):
    return [
        (index * 2 + core, target(index, core) * 2 + core)
        for index in range(lax.axis_size("tm"))
        for core in range(2)
    ]


def across(value, bit):
    return lax.ppermute(value, BOTH, route(lambda i, c: i ^ (1 + (c ^ bit))))


def along_far(value, distance):
    far = lax.axis_size("tm") // NEAR
    return lax.ppermute(
        value, BOTH, route(lambda i, c: (i // NEAR + distance) % far * NEAR + i % NEAR)
    )


def swap_cores(value):
    return lax.ppermute(value, "mp", [(0, 1), (1, 0)])


def shifted(value, axis, distance):
    devices = range(lax.axis_size(axis))
    pairs = [(i - distance, i) for i in devices if i - distance in devices]
    return lax.ppermute(value, axis, pairs)


def across_chips(value):
    pairs = []
    for index in range(1, lax.axis_size("tm")):
        pairs += [(index * 2 - 1, index * 2), (index * 2, index * 2 - 1)]
    return lax.ppermute(value, BOTH, pairs)


def sections(rows):
    found, at = [], 0
    for count in (rows,) * 6 + (rows // 2,):
        found.append((at, count))
        at += count
    return found, at


WHERE, ROWS = sections(32)


def dilated_view(array):
    layers, taps, rows, halves, width = array.shape
    tiles = width // LANES
    split = array.reshape(layers, taps, rows, halves, tiles, LANES)
    return split.transpose(0, 1, 2, 4, 3, 5).reshape(-1, LANES)


def dilated_back(array, shape):
    layers, taps, rows, halves, width = shape
    tiles = width // LANES
    split = array.reshape(layers, taps, rows, tiles, halves, LANES)
    return split.transpose(0, 1, 2, 4, 3, 5).reshape(shape)


def strided(layer, tap, half, tile, rows):
    return pl.ds((layer * 2 + tap) * rows * 4 + tile * 2 + half, rows, stride=4)


def start_body(rows, mel, clips, who, *refs):
    sources, (out_one, out_two, low), held, sems = refs[:7], refs[7:10], refs[10:17], refs[17]
    copies = [
        pltpu.make_async_copy(source, target, sems.at[index])
        for index, (source, target) in enumerate(zip(sources, held))
    ]
    for copy in copies:
        copy.start()
    dil, res, skip, mel_w, table, bias, samples = held
    where, total = sections(rows)
    chans = rows // 2
    speakers = table.shape[-1]
    lane = lax.broadcasted_iota(jnp.int32, (1, speakers), 1)
    hot = jnp.concatenate([(lane == who[k]).astype(F32) for k in range(clips)], axis=0).astype(BF16)
    eye = lax.broadcasted_iota(jnp.int32, (chans, chans), 0) == lax.broadcasted_iota(
        jnp.int32, (chans, chans), 1
    )

    def write(out, at, count, columns, value):
        out[at : at + count, columns] = value.astype(out.dtype)

    for copy in copies[:-1]:
        copy.wait()
    for layer, out in enumerate((out_one, out_two)):
        for tap in range(2):
            for half in range(2):
                at, count = where[2 * tap + half]
                for tile in range(2):
                    part = dil[strided(layer, tap, half, tile, rows), :]
                    write(out, at, count, slice(tile * LANES, (tile + 1) * LANES), part)
        for kind, source in ((4, res), (5, skip)):
            at, count = where[kind]
            write(out, at, count, slice(None), source[layer])
        at, count = where[6]
        for half in range(2):
            picked = dot_right(table[layer, half].astype(BF16), hot)
            line = jnp.broadcast_to(bias[layer, half : half + 1, :], (chans, chans))
            column = jnp.sum(jnp.where(eye, line, 0.0), axis=1, keepdims=True)
            blank = jnp.zeros((chans, LANES - mel - clips - 1), F32)
            row = jnp.concatenate([mel_w[layer, half], picked, column, blank], axis=1)
            columns = slice(half * LANES, (half + 1) * LANES)
            write(out, at, count, columns, row.astype(BF16).astype(F32))
    copies[-1].wait()
    low[...] = samples[...].astype(BF16)


def assemble_body(group, first, second, last, *refs):
    out = refs[-1]
    count = group.shape[0]
    far, near, _, first_bit, second_bit = place()
    for ref, mask in ((group, 0), (first, first_bit), (second, second_bit), (last, 3)):
        for back in range(count):
            out[lax.rem(far + count - back, count) * NEAR + (near ^ mask)] = ref[back]


def relay_body(value, *refs):
    out, token = refs[-2:]
    out[...] = value[...]
    token[...] = jnp.zeros_like(token)


TOKEN = struct((8, LANES))
LONG = 20_000_000_000


def stack_body(count, *refs):
    out, token = refs[-2:]
    for index in range(count):
        out[index] = refs[index][...]
    token[...] = jnp.zeros_like(token)


def along_all(pack, unread):
    far = lax.axis_size("tm") // NEAR
    got = [along_far(pack, distance) for distance in range(1, far)]
    return call(
        functools.partial(stack_body, far),
        (struct((far,) + pack.shape, BF16), TOKEN),
        pack,
        *got,
        unread=unread,
    )


def near_exchange(group, before_last, flops=1024):
    first = across(group, 0)
    second = across(group, 1)
    passed, token = call(
        relay_body,
        (struct(first.shape, BF16), TOKEN),
        first,
        unread=(second,) + before_last,
        flops=flops,
    )
    return (group, first, second, across(passed, 1)), token


def joined(parts, before_end):
    count = NEAR * parts[0].shape[0]
    own = call(
        assemble_body, struct((count,) + parts[0].shape[1:], BF16), *parts, unread=before_end
    )
    if count != BLOCKS:
        own = to_canonical(own)
    return own, swap_cores(own)


def to_canonical(gathered):
    parts = gathered.shape[0]
    where, total = sections(BLOCKS * 32 // parts)
    return jnp.concatenate(
        [gathered[:, at : at + n, :].reshape(BLOCKS, -1, 256) for at, n in where], axis=1
    )


def from_canonical(packed, parts):
    where, total = sections(32)
    return jnp.concatenate(
        [packed[:, at : at + n, :].reshape(parts, -1, 256) for at, n in where], axis=1
    )


def piece(ref, kind):
    at, count = WHERE[kind]
    return ref[:, at : at + count, :].reshape(-1, 256)


def conditioning(ref, half):
    at, count = WHERE[6]
    return ref[:, at : at + count, half * LANES : (half + 1) * LANES].reshape(-1, LANES)


def slot(ordered, first, block):
    if not ordered:
        return block
    near = lax.axis_index("tm") % NEAR
    mask = (block % NEAR) ^ near
    group = jnp.where(mask == 3, 0, jnp.where(mask == 0, 3, jnp.where(mask == first, 2, 1)))
    return group * (BLOCKS // NEAR) + block // NEAR


def store(ref, slots, kind, value):
    at, count = WHERE[kind]
    value = value.astype(BF16)
    for block in range(BLOCKS):
        ref[slots[block], at : at + count, :] = value[block * count : (block + 1) * count]


def store_conditioning(ref, slots, half, value):
    at, count = WHERE[6]
    value = value.astype(BF16)
    for block in range(BLOCKS):
        ref[slots[block], at : at + count, half * LANES : (half + 1) * LANES] = value[
            block * count : (block + 1) * count
        ]


def order_body(own, other, own_out, other_out):
    parts = own.shape[0]
    far = parts // NEAR
    _, near, _, first, second = place()
    for source, out, bit, next_bit in (
        (own, own_out, first, second),
        (other, other_out, second, first),
    ):
        for group, mask in enumerate((3, next_bit, bit, 0)):
            for index in range(far):
                out[group * far + index] = source[index * NEAR + (near ^ mask)]


def first_sum_body(own, got, *refs):
    out, token = refs[-2:]
    half = out.shape[0]
    out[...] = own[:half] + got[:half]
    token[...] = jnp.zeros_like(token)


def second_sum_body(own, got, near_got, *refs):
    out, token = refs[-2:]
    count = out.shape[0]
    kept = slice(2 * count, 3 * count)
    out[...] = (
        own[kept].astype(F32) + got[kept].astype(F32) + near_got[:count].astype(F32)
    ).astype(BF16)
    token[...] = jnp.zeros_like(token)


def third_sum_body(own, got, near_got, last_got, *refs):
    far = place()[0]
    count = last_got.shape[0]
    token = refs[-1]
    token[...] = jnp.zeros_like(token)
    for distance, out in enumerate(refs[-count - 1 : -1]):
        index = lax.rem(far + distance, count)
        out[...] = (
            own[3 * count + index].astype(F32)
            + got[3 * count + index].astype(F32)
            + near_got[count + index].astype(F32)
            + last_got[index].astype(F32)
        ).astype(out.dtype)


def ordered(grads):
    parts = lax.axis_size("tm")
    return grads if parts == BLOCKS else from_canonical(grads, parts)


def cores_summed(own, other, unread=()):
    own, other = ordered(own), ordered(other)
    if own.shape[0] != BLOCKS:
        own, other = call(order_body, (struct(own.shape, BF16),) * 2, own, other)
    got = swap_cores(other)
    half = struct((own.shape[0] // 2,) + own.shape[1:], BF16)
    sent, token = call(first_sum_body, (half, TOKEN), own, got, unread=unread)
    return (own, got), sent, token


def near_summed(grads, sent, flops=1024, unread=()):
    near_got = across(sent, 1)
    shape = (grads[0].shape[0] // NEAR,) + grads[0].shape[1:]
    sent, token = call(
        second_sum_body,
        (struct(shape, BF16), TOKEN),
        *grads,
        near_got,
        flops=flops,
        unread=unread,
    )
    return grads + (near_got,), sent, token


def far_terms(grads, last_got, flops=1024):
    far, *shape = last_got.shape
    kept, *sends, token = call(
        third_sum_body,
        (struct(shape),) + (struct(shape, BF16),) * (far - 1) + (TOKEN,),
        *grads,
        last_got,
        flops=flops,
    )
    return [kept] + [along_far(value, k + 1) for k, value in enumerate(sends)], token


def gates(weights, lag, xin, cond):
    za = dot(lag, piece(weights, 0)) + dot(xin, piece(weights, 2))
    za = za + dot_right(cond, conditioning(weights, 0))
    zb = dot(lag, piece(weights, 1)) + dot(xin, piece(weights, 3))
    zb = zb + dot_right(cond, conditioning(weights, 1))
    return jnp.tanh(za), jax.nn.sigmoid(zb)


def gate_gradients(weights, res_grad, skip_grad, keep, tanh_a, sig_b):
    hidden_grad = dot(res_grad, piece(weights, 4)) + dot(skip_grad, piece(weights, 5))
    hidden_grad = hidden_grad * keep
    grad_a = (hidden_grad * sig_b * (1.0 - tanh_a * tanh_a)).astype(BF16)
    grad_b = (hidden_grad * tanh_a * sig_b * (1.0 - sig_b)).astype(BF16)
    return grad_a, grad_b


def weight_gradients(out, bit, lag, xin, cond, grad_a, grad_b, res_grad, skip_grad, hidden):
    slots = [slot(lax.axis_size("tm") == BLOCKS, bit, block) for block in range(BLOCKS)]
    store(out, slots, 0, dot_left(lag, grad_a))
    store(out, slots, 1, dot_left(lag, grad_b))
    store(out, slots, 2, dot_left(xin, grad_a))
    store(out, slots, 3, dot_left(xin, grad_b))
    store(out, slots, 4, dot_left(res_grad, hidden))
    store(out, slots, 5, dot_left(skip_grad, hidden))
    store_conditioning(out, slots, 0, dot_left(grad_a, cond))
    store_conditioning(out, slots, 1, dot_left(grad_b, cond))


def first_body(own, x, lag_raw, cond, marks, weights, *refs):
    earlier, (u2, s1, lag_out, ta, sb, hid, token) = refs[:-7], refs[-7:]
    token[...] = jnp.zeros_like(token)
    keep = marks[:, 0:1]
    xin = x[...].astype(BF16)
    lag = (lag_raw[...].astype(F32) * marks[:, 1:2]).astype(BF16)
    tanh_a, sig_b = gates(weights, lag, xin, cond[...])
    hidden = (keep * tanh_a * sig_b).astype(BF16)
    res = dot_right(hidden, piece(weights, 4))
    skip = dot_right(hidden[:own], piece(weights, 5))
    ta[...] = tanh_a[:own]
    sb[...] = sig_b[:own]
    hid[...] = hidden[:own]
    lag_out[...] = lag[:own]
    if len(earlier) == 2:
        u2[...] = (x[...] + (earlier[0][...] + res)) * ROOT_HALF
        s1[...] = earlier[1][...] + skip
    else:
        u2[...] = res
        s1[...] = skip


def second_input(u2, marks):
    xin = u2[...].astype(BF16)
    lag = (pltpu.roll(xin.astype(F32), 1, 0) * marks[:, 2:3]).astype(BF16)
    return xin, lag


def second_forward_body(u2, cond, marks, weights, ta, sb):
    xin, lag = second_input(u2, marks)
    ta[...], sb[...] = gates(weights, lag, xin, cond[...])


def second_body(own, u2, s1, cond, marks, cot, cot_skip, weights, *refs):
    last = len(refs) > 5
    earlier, (mixed, total, g2, lag_sum, grads) = refs[:-5], refs[-5:]
    rows = u2.shape[0]
    keep = marks[:, 0:1]
    xin, lag = second_input(u2, marks)
    res_grad = (cot[...] * ROOT_HALF).astype(BF16)
    skip_grad = cot_skip[...]
    if last:
        tanh_a, sig_b = earlier[4][...], earlier[5][...]
    else:
        tanh_a, sig_b = gates(weights, lag, xin, cond[...])
    hidden = (keep * tanh_a * sig_b).astype(BF16)[:own]
    grad_a, grad_b = gate_gradients(weights, res_grad, skip_grad, keep, tanh_a, sig_b)
    _, _, _, first_bit, second_bit = place()
    weight_gradients(
        grads,
        first_bit if last else second_bit,
        lag[:own],
        xin[:own],
        cond[:own, :],
        grad_a[:own],
        grad_b[:own],
        res_grad[:own],
        skip_grad[:own],
        hidden,
    )
    res = dot_right(hidden, piece(weights, 4))
    skip = dot_right(hidden, piece(weights, 5))
    lag_grad = dot_right(grad_a, piece(weights, 0)) + dot_right(grad_b, piece(weights, 1))
    now = dot_right(grad_a[:own], piece(weights, 2)) + dot_right(grad_b[:own], piece(weights, 3))
    if last:
        res, skip, now, lag_grad = (
            before[...] + value for before, value in zip(earlier, (res, skip, now, lag_grad))
        )
        mixed[...] = (u2[:own, :] + res) * ROOT_HALF
        total[...] = s1[...] + skip
        pushed = (lag_grad * marks[:, 2:3]).astype(BF16).astype(F32)
        g2[...] = cot[:own, :] * ROOT_HALF + now + pltpu.roll(pushed, rows - 1, 0)[:own]
    else:
        mixed[...] = res
        total[...] = skip
        g2[...] = now
        lag_sum[...] = lag_grad


def third_body(own, last, g2, x, lag, cond, marks, cot_skip, ta, sb, hid, weights, *refs):
    earlier, (g1, dlag, lag_sum, grads) = refs[:-4], refs[-4:]
    keep = marks[:own, 0:1]
    xin = x[:own, :].astype(BF16)
    res_grad = (g2[...] * ROOT_HALF).astype(BF16)
    skip_grad = cot_skip[:own, :]
    grad_a, grad_b = gate_gradients(weights, res_grad, skip_grad, keep, ta[...], sb[...])
    _, _, _, first_bit, second_bit = place()
    weight_gradients(
        grads,
        first_bit if last else second_bit,
        lag[...],
        xin,
        cond[:own, :],
        grad_a,
        grad_b,
        res_grad,
        skip_grad,
        hid[...],
    )
    lag_grad = dot_right(grad_a, piece(weights, 0)) + dot_right(grad_b, piece(weights, 1))
    now = dot_right(grad_a, piece(weights, 2)) + dot_right(grad_b, piece(weights, 3))
    if last:
        lag_sum[...] = jnp.zeros_like(lag_sum)
        g1[...] = g2[...] * ROOT_HALF + (earlier[0][...] + now)
        dlag[...] = ((earlier[1][...] + lag_grad) * marks[:own, 1:2]).astype(BF16)
    else:
        g1[...] = now
        lag_sum[...] = lag_grad


def part_body(x, cot, skip, lag, *refs):
    core = place()[2]
    kept, given, held = refs[-3:]
    span, width = kept.shape[0], x.shape[1]
    beyond = x.shape[0] - span
    held[...] = lag[...].astype(F32)
    for index, ref in enumerate((x, cot, skip, held)):
        columns = slice(index * width, (index + 1) * width)
        kept[:, columns] = ref[pl.ds(core * beyond, span), :]
        given[:, columns] = ref[pl.ds((1 - core) * beyond, span), :]


def join_body(kept, got, mel, mask, *refs):
    core = place()[2]
    inner, side, near_edge, edge_sent, held, lines = refs[-6:]
    span, width = kept.shape[0], kept.shape[1] // 4
    own, beyond = inner.shape[0], mel.shape[1] - span
    for index in range(4):
        for source, at in ((kept, core), (got, 1 - core)):
            held[:, pl.ds(index * 2 * width + at * width, width)] = source[
                :, index * width : (index + 1) * width
            ]
    blank = jnp.zeros((LANES - mel.shape[0] - 1, mel.shape[1]), F32)
    lines[...] = jnp.concatenate([mel[...], mask[...].astype(F32), blank], axis=0).T
    inner[...] = held[pl.ds(core * EDGE, own), :]
    side[...] = lines[pl.ds(core * own, own), :]
    for ref, at in ((near_edge, (1 - core) * own), (edge_sent, core * own)):
        ref[:, LANES:] = held[pl.ds(at, EDGE), :]
        ref[:, :LANES] = lines[pl.ds(core * beyond + at, EDGE), :]


def widen_body(
    mel, clips, lengths, inner, side, near_edge, edge, x_out, cot_out, skip_out, lag_out, cond, marks
):
    far, near, core = place()[:3]
    own, full = inner.shape[0], inner.shape[1] // 4
    wide = own + 2 * EDGE
    after = jnp.where(core == 0, near_edge[...], edge[...])
    before = jnp.where(core == 0, edge[...], near_edge[...])
    for index, ref in enumerate((x_out, cot_out, skip_out, lag_out)):
        at = LANES + index * full
        ref[...] = jnp.concatenate(
            [
                inner[:, index * full : (index + 1) * full],
                after[:, at : at + full],
                before[:, at : at + full],
            ],
            axis=0,
        ).astype(ref.dtype)
    side_wide = jnp.concatenate([side[...], after[:, :LANES], before[:, :LANES]], axis=0)
    lane = lax.broadcasted_iota(jnp.int32, (wide, LANES), 1)
    line = lax.broadcasted_iota(jnp.int32, (wide, LANES), 0)
    first = ((far * NEAR + near) * 2 + core) * own
    position = first + jnp.where(line < own + EDGE, line, line - wide)

    def segment(at):
        total = jnp.zeros((wide, LANES), jnp.int32)
        end = jnp.int32(0)
        for clip in range(clips):
            end = end + lengths[clip]
            total = total + (at >= end).astype(jnp.int32)
        return total

    here = segment(position)

    def valid(span):
        return ((position >= span) & (segment(position - span) == here)).astype(F32)

    hot = ((lane - mel) == here).astype(F32)
    value = jnp.where(lane < mel, side_wide, jnp.where(lane < mel + clips, hot, 0.0))
    cond[...] = jnp.where(lane == mel + clips, 1.0, value).astype(BF16)
    keep = side_wide[:, mel : mel + 1]
    marks[...] = jnp.where(
        lane == 0, keep, jnp.where(lane == 1, valid(FIRST_DILATION), valid(1))
    )


def divide_body(mixed, total, g1, push, *refs):
    core = place()[2]
    kept, given, held = refs[-3:]
    width = kept.shape[1] // 4
    held[...] = push[...].astype(F32)
    for index, ref in enumerate((mixed, total, g1, held)):
        columns = slice(index * width, (index + 1) * width)
        kept[:, columns] = ref[:, pl.ds(core * width, width)]
        given[:, columns] = ref[:, pl.ds((1 - core) * width, width)]


def finish_body(kept, got, *refs):
    core = place()[2]
    outs, token = refs[:-1], refs[-1]
    token[...] = jnp.zeros_like(token)
    own, width = kept.shape[0], kept.shape[1] // 4
    for index, ref in enumerate(outs):
        for source, at in ((kept, core), (got, 1 - core)):
            ref[pl.ds(at * own, own), :] = source[:, index * width : (index + 1) * width]


def push_body(push, *refs):
    refs[-1][...] = push[...].astype(BF16)


def input_gradient_body(g1, push, out):
    out[...] = g1[...] + push[...].astype(F32)


def table_gradient(cond_grad, who, mel, clips, speakers):
    lane = lax.broadcasted_iota(jnp.int32, (cond_grad.shape[0], speakers), 1)
    result = jnp.zeros((cond_grad.shape[0], speakers), F32)
    for clip in range(clips):
        column = cond_grad[:, mel + clip : mel + clip + 1]
        result = result + jnp.where(lane == who[clip], column, 0.0)
    return result


def square_body(rows, mel, clips, speakers, count, who, *refs):
    terms, (out, squares) = refs[:count], refs[-2:]
    where, total = sections(rows)
    start = where[6][0]
    value = terms[0][...]
    for term in terms[1:]:
        value = value + term[...].astype(F32)
    out[...] = value
    main = out[:start, :]
    amount = jnp.sum(main * main, keepdims=True)
    for half in range(2):
        block = out[start:, half * LANES : (half + 1) * LANES]
        lane = lax.broadcasted_iota(jnp.int32, block.shape, 1)
        plain = jnp.where((lane < mel) | (lane == mel + clips), block, 0.0)
        amount = amount + jnp.sum(plain * plain, keepdims=True)
        table = table_gradient(block, who, mel, clips, speakers)
        amount = amount + jnp.sum(table * table, keepdims=True)
    squares[...] = jnp.broadcast_to(amount, squares.shape)


def adamw(weight, mean, square, gradient, scale):
    clipped = gradient * scale
    new_mean = BETA_ONE * mean + (1.0 - BETA_ONE) * clipped
    new_square = BETA_TWO * square + (1.0 - BETA_TWO) * clipped * clipped
    fix_one = 1.0 - BETA_ONE**STEP
    fix_two = 1.0 - BETA_TWO**STEP
    update = new_mean / fix_one / (jnp.sqrt(new_square / fix_two) + ADAM_EPS)
    return weight - LEARN_RATE * (update + DECAY * weight), new_mean, new_square


def update_body(rows, mel, clips, who, *refs):
    grads = refs[0:2]
    squares = refs[2]
    old = [refs[3 + 3 * kind : 6 + 3 * kind] for kind in range(6)]
    norm = refs[21]
    new = [refs[22 + 5 * kind : 27 + 5 * kind] for kind in range(6)]
    where, total = sections(rows)
    chans = rows // 2
    grad_norm = jnp.sqrt(jnp.sum(squares[...], axis=0, keepdims=True)[:, 0:1])
    norm[...] = grad_norm
    scale = jnp.minimum(1.0, CLIP_NORM / grad_norm)

    def write(kind, index, gradient):
        weight, mean, square = (ref[index] for ref in old[kind])
        new_weight, new_mean, new_square = adamw(weight, mean, square, gradient, scale)
        for ref, value in zip(
            new[kind],
            (gradient, new_weight, new_mean, new_square, new_weight.astype(BF16)),
        ):
            ref[index] = value

    dil = new[0][0]
    for layer in range(2):
        for tap in range(2):
            for half in range(2):
                at, n = where[2 * tap + half]
                for tile in range(2):
                    dil[strided(layer, tap, half, tile, rows), :] = grads[layer][
                        at : at + n, tile * LANES : (tile + 1) * LANES
                    ]
    weight, mean, square = (ref[...] for ref in old[0])
    new_weight, new_mean, new_square = adamw(weight, mean, square, dil[...], scale)
    new[0][1][...] = new_weight
    new[0][2][...] = new_mean
    new[0][3][...] = new_square
    new[0][4][...] = new_weight.astype(BF16)
    for layer in range(2):
        for half in range(2):
            block = grads[layer][where[6][0] :, half * LANES : (half + 1) * LANES]
            eye = lax.broadcasted_iota(jnp.int32, (chans, chans), 0) == lax.broadcasted_iota(
                jnp.int32, (chans, chans), 1
            )
            column = block[:, mel + clips : mel + clips + 1]
            line = jnp.sum(jnp.where(eye, column, 0.0), axis=0, keepdims=True)
            write(1, (layer, slice(half, half + 1), slice(None)), line)
            write(2, (layer, half), block[:, :mel])
            speakers = old[3][0].shape[-1]
            write(3, (layer, half), table_gradient(block, who, mel, clips, speakers))
        for kind, section in ((4, 4), (5, 5)):
            at, n = where[section]
            write(kind, (layer,), grads[layer][at : at + n, :])


def on_device(
    x_input,
    mel_frames,
    sample_mask,
    clip_length_array,
    speaker_ids,
    cot_out,
    cot_skip,
    *states,
):
    parts = lax.axis_size("tm")
    held_rows, width = x_input.shape
    own, full = held_rows // 2, 2 * width
    wide = own + 2 * EDGE
    mel = mel_frames.shape[0]
    clips = clip_length_array.shape[0]
    hop = FIRST_DILATION // held_rows

    dil_shape = states[0].shape
    rows = dil_shape[2]
    views = (
        [dilated_view(s) for s in states[0:3]]
        + list(states[3:6])
        + [s.transpose(0, 2, 3, 1) for s in states[6:12]]
        + [s.transpose(0, 2, 1) for s in states[12:18]]
    )
    speakers = views[9].shape[-1]
    where, total = sections(rows)
    far = parts // NEAR
    taken = [views[k] for k in (0, 12, 15, 6, 9, 3)]
    packed_type = BF16 if rows % 32 == 0 else F32
    taken = [views[k] for k in (0, 12, 15, 6, 9, 3)]
    packed_type = BF16 if rows % 32 == 0 else F32
    taken.append(x_input)
    pack_one, pack_two, x_low = call(
        functools.partial(start_body, rows, mel, clips),
        (struct((total, 256), packed_type),) * 2 + (struct(x_input.shape, BF16),),
        *taken,
        scalars=(speaker_ids,),
        space=pl.ANY,
        grant=None,
        scratch=[pltpu.VMEM(v.shape, F32) for v in taken]
        + [pltpu.SemaphoreType.DMA((len(taken),))],
    )

    lag = shifted(x_low, "tm", hop)
    span = own + EDGE
    group_one, stacked = along_all(pack_one.astype(BF16), (lag,))
    group_two, stacked = along_all(pack_two.astype(BF16), (stacked,))
    kept, given = call(
        part_body,
        (struct((span, 4 * width)),) * 2,
        x_input,
        cot_out,
        cot_skip,
        lag,
        unread=(stacked,),
        scratch=[pltpu.VMEM(x_input.shape, F32)],
    )
    parts_one, relayed = near_exchange(group_one, (stacked,), LONG)
    joined_own = struct((own, 4 * full))
    edge = struct((EDGE, 4 * full + LANES))
    inner, side, near_edge, edge_sent = call(
        join_body,
        (joined_own, struct((own, LANES)), edge, edge),
        kept,
        swap_cores(given),
        mel_frames,
        sample_mask[None, :],
        unread=(relayed,),
        scratch=[pltpu.VMEM((span, 4 * full), F32), pltpu.VMEM((held_rows, LANES), F32)],
    )
    x_wide, cot_wide, skip_wide, lag_wide, cond, marks = call(
        functools.partial(widen_body, mel, clips),
        (
            struct((wide, full)),
            struct((wide, full)),
            struct((wide, full), BF16),
            struct((wide, full), BF16),
            struct((wide, LANES), BF16),
            struct((wide, LANES)),
        ),
        inner,
        side,
        near_edge,
        across_chips(edge_sent),
        scalars=(clip_length_array,),
    )
    parts_two, begun = near_exchange(group_two, (marks,))
    w1_own, w1_oth = joined(parts_one, (begun,))

    half = struct((own, width))
    wave = struct((own, full))
    broad = struct((wide, full))
    low_half = struct((own, width), BF16)
    low_full = struct((own, full), BF16)
    packed = struct((BLOCKS, ROWS, 256), BF16)

    def forward(weights, *earlier, unread=(), flops=1024):
        return call(
            functools.partial(first_body, own),
            (broad, wave, low_full, half, half, low_half, TOKEN),
            x_wide,
            lag_wide,
            cond,
            marks,
            weights,
            *earlier,
            unread=unread,
            flops=flops,
        )

    res, skip, lag1, ta_own, sb_own, hid_own, _ = forward(w1_own, unread=(begun,), flops=LONG)
    u2, s1, _, ta_oth, sb_oth, hid_oth, token = forward(w1_oth, res, skip)

    w2_own, w2_oth = joined(parts_two, (token,))

    def middle(weights, *earlier):
        return call(
            functools.partial(second_body, own),
            (wave, wave, wave, TOKEN if earlier else broad, packed),
            u2,
            s1,
            cond,
            marks,
            cot_wide,
            skip_wide,
            weights,
            *earlier,
        )

    gate_two = call(
        second_forward_body, (struct((wide, width)),) * 2, u2, cond, marks, w2_own
    )
    *sums, grad_oth = middle(w2_oth)
    mixed, skip_total, g2, _, grad_own = middle(w2_own, *sums, *gate_two)

    def totals(terms, unread=()):
        return call(
            functools.partial(square_body, rows, mel, clips, speakers, len(terms)),
            (struct((total, 256)), struct((8, LANES))),
            *terms,
            scalars=(speaker_ids,),
            unread=unread,
        )

    def backward(weights, tanh_a, sig_b, hidden, *earlier, unread):
        last = bool(earlier)
        return call(
            functools.partial(third_body, own, last),
            (wave, low_full if last else TOKEN, TOKEN if last else wave, packed),
            g2,
            x_wide,
            lag1,
            cond,
            marks,
            skip_wide,
            tanh_a,
            sig_b,
            hidden,
            weights,
            *earlier,
            unread=unread,
        )

    grads2, sent2, token = cores_summed(grad_own, grad_oth)
    now, _, lag_sum, grad_oth = backward(w1_oth, ta_oth, sb_oth, hid_oth, unread=(token,))
    g1_part, dlag1, token, grad_own = backward(
        w1_own, ta_own, sb_own, hid_own, now, lag_sum, unread=()
    )
    grads2, sent2, token = near_summed(grads2, sent2, LONG, (token,))
    grads1, sent1, _ = cores_summed(grad_own, grad_oth, (token,))
    last_got = across(sent2, 0)
    kept, given = call(
        divide_body,
        (struct((own, 4 * width)),) * 2,
        mixed,
        skip_total,
        g1_part,
        dlag1,
        scratch=[pltpu.VMEM((own, full), F32)],
    )
    mixed, skip_total, grad_input, push, token = call(
        finish_body, (struct((held_rows, width)),) * 4 + (TOKEN,), kept, swap_cores(given)
    )
    terms2, _ = far_terms(grads2, last_got, LONG)
    grads1, sent1, _ = near_summed(grads1, sent1, unread=(token, terms2[1], terms2[-1]))
    terms1, token = far_terms(grads1, across(sent1, 0))
    push = call(push_body, struct((held_rows, width), BF16), push, unread=(token,))
    grad_input = call(
        input_gradient_body,
        struct((held_rows, width)),
        grad_input,
        shifted(push, "tm", -hop),
    )

    sum2, squares2 = totals(terms2)
    sum1, squares1 = totals(terms1)
    squares = squares1[:1] + squares2[:1]
    squares = squares + swap_cores(squares)
    sent = jnp.broadcast_to(squares[None], (parts, 1, LANES))
    squares = lax.all_to_all(sent, "tm", split_axis=0, concat_axis=0, tiled=True)
    outs = [struct((1, 1))]
    for view in views[0::3]:
        outs += [struct(view.shape)] * 4 + [struct(view.shape, BF16)]
    updated = call(
        functools.partial(update_body, rows, mel, clips),
        tuple(outs),
        sum1,
        sum2,
        squares.reshape(parts, LANES),
        *views,
        scalars=(speaker_ids,),
    )
    grad_norm = updated[0].reshape(())
    backs = (
        [lambda v: dilated_back(v, dil_shape), lambda v: v]
        + [lambda v: v.transpose(0, 3, 1, 2)] * 2
        + [lambda v: v.transpose(0, 2, 1)] * 2
    )
    new = [
        [back(v) for v in updated[1 + 5 * kind : 6 + 5 * kind]] for kind, back in enumerate(backs)
    ]
    return (
        mixed,
        skip_total,
        grad_input,
        grad_norm,
        *[group[0] for group in new],
        *[value for group in new for value in group[1:4]],
        *[group[4] for group in new],
    )


def solution(mesh):
    rows = P("tm", "mp")
    dil = P(None, None, "tm", None, "mp")
    bias = P(None, None, ("mp", "tm"))
    wide = P(None, None, None, ("mp", "tm"))
    square = P(None, "mp", "tm")
    kinds = (dil, bias, wide, wide, square, square)
    thrice = tuple(kind for kind in kinds for _ in range(3))
    return jax.shard_map(
        on_device,
        mesh=mesh,
        in_specs=(rows, P(None, "tm"), P("tm"), P(), P(), rows, rows) + thrice,
        out_specs=(rows, rows, rows, P()) + kinds + thrice + kinds,
        check_vma=False,
    )
```

```python
import functools

import jax
import jax.numpy as jnp
from jax import lax
from jax.experimental import pallas as pl
from jax.experimental.pallas import tpu as pltpu
from jax.sharding import PartitionSpec as P

FIRST_DILATION = 512
STEP = 10
ROOT_HALF = 0.7071067811865476
BETA_ONE = 0.9
BETA_TWO = 0.999
ADAM_EPS = 1e-08
LEARN_RATE = 0.07
DECAY = 0.01
CLIP_NORM = 1.0

F32 = jnp.float32
BF16 = jnp.bfloat16
LANES = 128
EDGE = 8
BLOCKS = 16
NEAR = 4
VMEM_BYTES = 26 * 1024 * 1024
BOTH = ("tm", "mp")


def struct(shape, dtype=F32):
    return jax.ShapeDtypeStruct(shape, dtype)


def call(body, out_shape, *operands, scalars=(), scratch=(), space=pltpu.VMEM, unread=(), flops=1024, grant=VMEM_BYTES):
    specs = [pl.BlockSpec(memory_space=pltpu.SMEM)] * len(scalars)
    specs += [pl.BlockSpec(memory_space=space)] * len(operands)
    specs += [pl.BlockSpec(memory_space=pl.ANY)] * len(unread)
    return pl.pallas_call(
        body,
        out_shape=out_shape,
        in_specs=specs,
        scratch_shapes=list(scratch),
        compiler_params=pltpu.CompilerParams(vmem_limit_bytes=grant),
        cost_estimate=pl.CostEstimate(flops=flops, bytes_accessed=1024, transcendentals=0),
    )(*scalars, *operands, *unread)


def dot(left, right):
    return jnp.dot(left, right, preferred_element_type=F32)


def dot_right(left, right):
    return lax.dot_general(left, right, (((1,), (1,)), ((), ())), preferred_element_type=F32)


def dot_left(left, right):
    return lax.dot_general(left, right, (((0,), (0,)), ((), ())), preferred_element_type=F32)


def place():
    index = lax.axis_index("tm")
    core = lax.axis_index("mp")
    return index // NEAR, index % NEAR, core, 1 + core, 2 - core


def route(target):
    return [
        (index * 2 + core, target(index, core) * 2 + core)
        for index in range(lax.axis_size("tm"))
        for core in range(2)
    ]


def across(value, bit):
    return lax.ppermute(value, BOTH, route(lambda i, c: i ^ (1 + (c ^ bit))))


def along_far(value, distance):
    far = lax.axis_size("tm") // NEAR
    return lax.ppermute(
        value, BOTH, route(lambda i, c: (i // NEAR + distance) % far * NEAR + i % NEAR)
    )


def swap_cores(value):
    return lax.ppermute(value, "mp", [(0, 1), (1, 0)])


def shifted(value, axis, distance):
    devices = range(lax.axis_size(axis))
    pairs = [(i - distance, i) for i in devices if i - distance in devices]
    return lax.ppermute(value, axis, pairs)


def across_chips(value):
    pairs = []
    for index in range(1, lax.axis_size("tm")):
        pairs += [(index * 2 - 1, index * 2), (index * 2, index * 2 - 1)]
    return lax.ppermute(value, BOTH, pairs)


def sections(rows):
    found, at = [], 0
    for count in (rows,) * 6 + (rows // 2,):
        found.append((at, count))
        at += count
    return found, at


WHERE, ROWS = sections(32)


def dilated_view(array):
    layers, taps, rows, halves, width = array.shape
    tiles = width // LANES
    split = array.reshape(layers, taps, rows, halves, tiles, LANES)
    return split.transpose(0, 1, 2, 4, 3, 5).reshape(-1, LANES)


def dilated_back(array, shape):
    layers, taps, rows, halves, width = shape
    tiles = width // LANES
    split = array.reshape(layers, taps, rows, tiles, halves, LANES)
    return split.transpose(0, 1, 2, 4, 3, 5).reshape(shape)


def strided(layer, tap, half, tile, rows):
    return pl.ds((layer * 2 + tap) * rows * 4 + tile * 2 + half, rows, stride=4)


def start_body(rows, mel, clips, who, *refs):
    sources, (out_one, out_two, low), held, sems = refs[:7], refs[7:10], refs[10:17], refs[17]
    copies = [
        pltpu.make_async_copy(source, target, sems.at[index])
        for index, (source, target) in enumerate(zip(sources, held))
    ]
    for copy in copies:
        copy.start()
    dil, res, skip, mel_w, table, bias, samples = held
    where, total = sections(rows)
    chans = rows // 2
    speakers = table.shape[-1]
    lane = lax.broadcasted_iota(jnp.int32, (1, speakers), 1)
    hot = jnp.concatenate([(lane == who[k]).astype(F32) for k in range(clips)], axis=0).astype(BF16)
    eye = lax.broadcasted_iota(jnp.int32, (chans, chans), 0) == lax.broadcasted_iota(
        jnp.int32, (chans, chans), 1
    )

    def write(out, at, count, columns, value):
        out[at : at + count, columns] = value.astype(out.dtype)

    for copy in copies[:-1]:
        copy.wait()
    for layer, out in enumerate((out_one, out_two)):
        for tap in range(2):
            for half in range(2):
                at, count = where[2 * tap + half]
                for tile in range(2):
                    part = dil[strided(layer, tap, half, tile, rows), :]
                    write(out, at, count, slice(tile * LANES, (tile + 1) * LANES), part)
        for kind, source in ((4, res), (5, skip)):
            at, count = where[kind]
            write(out, at, count, slice(None), source[layer])
        at, count = where[6]
        for half in range(2):
            picked = dot_right(table[layer, half].astype(BF16), hot)
            line = jnp.broadcast_to(bias[layer, half : half + 1, :], (chans, chans))
            column = jnp.sum(jnp.where(eye, line, 0.0), axis=1, keepdims=True)
            blank = jnp.zeros((chans, LANES - mel - clips - 1), F32)
            row = jnp.concatenate([mel_w[layer, half], picked, column, blank], axis=1)
            columns = slice(half * LANES, (half + 1) * LANES)
            write(out, at, count, columns, row.astype(BF16).astype(F32))
    copies[-1].wait()
    low[...] = samples[...].astype(BF16)


def assemble_body(group, first, second, last, *refs):
    out = refs[-1]
    count = group.shape[0]
    far, near, _, first_bit, second_bit = place()
    for ref, mask in ((group, 0), (first, first_bit), (second, second_bit), (last, 3)):
        for back in range(count):
            out[lax.rem(far + count - back, count) * NEAR + (near ^ mask)] = ref[back]


def relay_body(value, *refs):
    out, token = refs[-2:]
    out[...] = value[...]
    token[...] = jnp.zeros_like(token)


TOKEN = struct((8, LANES))
LONG = 20_000_000_000


def stack_body(count, *refs):
    out, token = refs[-2:]
    for index in range(count):
        out[index] = refs[index][...]
    token[...] = jnp.zeros_like(token)


def along_all(pack, unread):
    far = lax.axis_size("tm") // NEAR
    got = [along_far(pack, distance) for distance in range(1, far)]
    return call(
        functools.partial(stack_body, far),
        (struct((far,) + pack.shape, BF16), TOKEN),
        pack,
        *got,
        unread=unread,
    )


def near_exchange(group, before_last, flops=1024):
    first = across(group, 0)
    second = across(group, 1)
    passed, token = call(
        relay_body,
        (struct(first.shape, BF16), TOKEN),
        first,
        unread=(second,) + before_last,
        flops=flops,
    )
    return (group, first, second, across(passed, 1)), token


def joined(parts, before_end):
    count = NEAR * parts[0].shape[0]
    own = call(
        assemble_body, struct((count,) + parts[0].shape[1:], BF16), *parts, unread=before_end
    )
    if count != BLOCKS:
        own = to_canonical(own)
    return own, swap_cores(own)


def to_canonical(gathered):
    parts = gathered.shape[0]
    where, total = sections(BLOCKS * 32 // parts)
    return jnp.concatenate(
        [gathered[:, at : at + n, :].reshape(BLOCKS, -1, 256) for at, n in where], axis=1
    )


def from_canonical(packed, parts):
    where, total = sections(32)
    return jnp.concatenate(
        [packed[:, at : at + n, :].reshape(parts, -1, 256) for at, n in where], axis=1
    )


def piece(ref, kind):
    at, count = WHERE[kind]
    return ref[:, at : at + count, :].reshape(-1, 256)


def conditioning(ref, half):
    at, count = WHERE[6]
    return ref[:, at : at + count, half * LANES : (half + 1) * LANES].reshape(-1, LANES)


def slot(ordered, first, block):
    if not ordered:
        return block
    near = lax.axis_index("tm") % NEAR
    mask = (block % NEAR) ^ near
    group = jnp.where(mask == 3, 0, jnp.where(mask == 0, 3, jnp.where(mask == first, 2, 1)))
    return group * (BLOCKS // NEAR) + block // NEAR


def store(ref, slots, kind, value):
    at, count = WHERE[kind]
    value = value.astype(BF16)
    for block in range(BLOCKS):
        ref[slots[block], at : at + count, :] = value[block * count : (block + 1) * count]


def store_conditioning(ref, slots, half, value):
    at, count = WHERE[6]
    value = value.astype(BF16)
    for block in range(BLOCKS):
        ref[slots[block], at : at + count, half * LANES : (half + 1) * LANES] = value[
            block * count : (block + 1) * count
        ]


def order_body(own, other, own_out, other_out):
    parts = own.shape[0]
    far = parts // NEAR
    _, near, _, first, second = place()
    for source, out, bit, next_bit in (
        (own, own_out, first, second),
        (other, other_out, second, first),
    ):
        for group, mask in enumerate((3, next_bit, bit, 0)):
            for index in range(far):
                out[group * far + index] = source[index * NEAR + (near ^ mask)]


def first_sum_body(own, got, *refs):
    out, token = refs[-2:]
    half = out.shape[0]
    out[...] = own[:half] + got[:half]
    token[...] = jnp.zeros_like(token)


def second_sum_body(own, got, near_got, *refs):
    out, token = refs[-2:]
    count = out.shape[0]
    kept = slice(2 * count, 3 * count)
    out[...] = (
        own[kept].astype(F32) + got[kept].astype(F32) + near_got[:count].astype(F32)
    ).astype(BF16)
    token[...] = jnp.zeros_like(token)


def third_sum_body(own, got, near_got, last_got, *refs):
    far = place()[0]
    count = last_got.shape[0]
    token = refs[-1]
    token[...] = jnp.zeros_like(token)
    for distance, out in enumerate(refs[-count - 1 : -1]):
        index = lax.rem(far + distance, count)
        out[...] = (
            own[3 * count + index].astype(F32)
            + got[3 * count + index].astype(F32)
            + near_got[count + index].astype(F32)
            + last_got[index].astype(F32)
        ).astype(out.dtype)


def ordered(grads):
    parts = lax.axis_size("tm")
    return grads if parts == BLOCKS else from_canonical(grads, parts)


def cores_summed(own, other, unread=()):
    own, other = ordered(own), ordered(other)
    if own.shape[0] != BLOCKS:
        own, other = call(order_body, (struct(own.shape, BF16),) * 2, own, other)
    got = swap_cores(other)
    half = struct((own.shape[0] // 2,) + own.shape[1:], BF16)
    sent, token = call(first_sum_body, (half, TOKEN), own, got, unread=unread)
    return (own, got), sent, token


def near_summed(grads, sent, flops=1024, unread=()):
    near_got = across(sent, 1)
    shape = (grads[0].shape[0] // NEAR,) + grads[0].shape[1:]
    sent, token = call(
        second_sum_body,
        (struct(shape, BF16), TOKEN),
        *grads,
        near_got,
        flops=flops,
        unread=unread,
    )
    return grads + (near_got,), sent, token


def far_terms(grads, last_got, flops=1024):
    far, *shape = last_got.shape
    kept, *sends, token = call(
        third_sum_body,
        (struct(shape),) + (struct(shape, BF16),) * (far - 1) + (TOKEN,),
        *grads,
        last_got,
        flops=flops,
    )
    return [kept] + [along_far(value, k + 1) for k, value in enumerate(sends)], token


def gates(weights, lag, xin, cond):
    za = dot(lag, piece(weights, 0)) + dot(xin, piece(weights, 2))
    za = za + dot_right(cond, conditioning(weights, 0))
    zb = dot(lag, piece(weights, 1)) + dot(xin, piece(weights, 3))
    zb = zb + dot_right(cond, conditioning(weights, 1))
    return jnp.tanh(za), jax.nn.sigmoid(zb)


def gate_gradients(weights, res_grad, skip_grad, keep, tanh_a, sig_b):
    hidden_grad = dot(res_grad, piece(weights, 4)) + dot(skip_grad, piece(weights, 5))
    hidden_grad = hidden_grad * keep
    grad_a = (hidden_grad * sig_b * (1.0 - tanh_a * tanh_a)).astype(BF16)
    grad_b = (hidden_grad * tanh_a * sig_b * (1.0 - sig_b)).astype(BF16)
    return grad_a, grad_b


def weight_gradients(out, bit, lag, xin, cond, grad_a, grad_b, res_grad, skip_grad, hidden):
    slots = [slot(lax.axis_size("tm") == BLOCKS, bit, block) for block in range(BLOCKS)]
    store(out, slots, 0, dot_left(lag, grad_a))
    store(out, slots, 1, dot_left(lag, grad_b))
    store(out, slots, 2, dot_left(xin, grad_a))
    store(out, slots, 3, dot_left(xin, grad_b))
    store(out, slots, 4, dot_left(res_grad, hidden))
    store(out, slots, 5, dot_left(skip_grad, hidden))
    store_conditioning(out, slots, 0, dot_left(grad_a, cond))
    store_conditioning(out, slots, 1, dot_left(grad_b, cond))


def first_body(own, x, lag_raw, cond, marks, weights, *refs):
    earlier, (u2, s1, lag_out, ta, sb, hid, token) = refs[:-7], refs[-7:]
    token[...] = jnp.zeros_like(token)
    keep = marks[:, 0:1]
    xin = x[...].astype(BF16)
    lag = (lag_raw[...].astype(F32) * marks[:, 1:2]).astype(BF16)
    tanh_a, sig_b = gates(weights, lag, xin, cond[...])
    hidden = (keep * tanh_a * sig_b).astype(BF16)
    res = dot_right(hidden, piece(weights, 4))
    skip = dot_right(hidden[:own], piece(weights, 5))
    ta[...] = tanh_a[:own]
    sb[...] = sig_b[:own]
    hid[...] = hidden[:own]
    lag_out[...] = lag[:own]
    if len(earlier) == 2:
        u2[...] = (x[...] + (earlier[0][...] + res)) * ROOT_HALF
        s1[...] = earlier[1][...] + skip
    else:
        u2[...] = res
        s1[...] = skip


def second_input(u2, marks):
    xin = u2[...].astype(BF16)
    lag = (pltpu.roll(xin.astype(F32), 1, 0) * marks[:, 2:3]).astype(BF16)
    return xin, lag


def second_forward_body(u2, cond, marks, weights, ta, sb):
    xin, lag = second_input(u2, marks)
    ta[...], sb[...] = gates(weights, lag, xin, cond[...])


def second_body(own, u2, s1, cond, marks, cot, cot_skip, weights, *refs):
    last = len(refs) > 5
    earlier, (mixed, total, g2, lag_sum, grads) = refs[:-5], refs[-5:]
    rows = u2.shape[0]
    keep = marks[:, 0:1]
    xin, lag = second_input(u2, marks)
    res_grad = (cot[...] * ROOT_HALF).astype(BF16)
    skip_grad = cot_skip[...]
    if last:
        tanh_a, sig_b = earlier[4][...], earlier[5][...]
    else:
        tanh_a, sig_b = gates(weights, lag, xin, cond[...])
    hidden = (keep * tanh_a * sig_b).astype(BF16)[:own]
    grad_a, grad_b = gate_gradients(weights, res_grad, skip_grad, keep, tanh_a, sig_b)
    _, _, _, first_bit, second_bit = place()
    weight_gradients(
        grads,
        first_bit if last else second_bit,
        lag[:own],
        xin[:own],
        cond[:own, :],
        grad_a[:own],
        grad_b[:own],
        res_grad[:own],
        skip_grad[:own],
        hidden,
    )
    res = dot_right(hidden, piece(weights, 4))
    skip = dot_right(hidden, piece(weights, 5))
    lag_grad = dot_right(grad_a, piece(weights, 0)) + dot_right(grad_b, piece(weights, 1))
    now = dot_right(grad_a[:own], piece(weights, 2)) + dot_right(grad_b[:own], piece(weights, 3))
    if last:
        res, skip, now, lag_grad = (
            before[...] + value for before, value in zip(earlier, (res, skip, now, lag_grad))
        )
        mixed[...] = (u2[:own, :] + res) * ROOT_HALF
        total[...] = s1[...] + skip
        pushed = (lag_grad * marks[:, 2:3]).astype(BF16).astype(F32)
        g2[...] = cot[:own, :] * ROOT_HALF + now + pltpu.roll(pushed, rows - 1, 0)[:own]
    else:
        mixed[...] = res
        total[...] = skip
        g2[...] = now
        lag_sum[...] = lag_grad


def third_body(own, last, g2, x, lag, cond, marks, cot_skip, ta, sb, hid, weights, *refs):
    earlier, (g1, dlag, lag_sum, grads) = refs[:-4], refs[-4:]
    keep = marks[:own, 0:1]
    xin = x[:own, :].astype(BF16)
    res_grad = (g2[...] * ROOT_HALF).astype(BF16)
    skip_grad = cot_skip[:own, :]
    grad_a, grad_b = gate_gradients(weights, res_grad, skip_grad, keep, ta[...], sb[...])
    _, _, _, first_bit, second_bit = place()
    weight_gradients(
        grads,
        first_bit if last else second_bit,
        lag[...],
        xin,
        cond[:own, :],
        grad_a,
        grad_b,
        res_grad,
        skip_grad,
        hid[...],
    )
    lag_grad = dot_right(grad_a, piece(weights, 0)) + dot_right(grad_b, piece(weights, 1))
    now = dot_right(grad_a, piece(weights, 2)) + dot_right(grad_b, piece(weights, 3))
    if last:
        lag_sum[...] = jnp.zeros_like(lag_sum)
        g1[...] = g2[...] * ROOT_HALF + (earlier[0][...] + now)
        dlag[...] = ((earlier[1][...] + lag_grad) * marks[:own, 1:2]).astype(BF16)
    else:
        g1[...] = now
        lag_sum[...] = lag_grad


def part_body(x, cot, skip, lag, *refs):
    core = place()[2]
    kept, given, held = refs[-3:]
    span, width = kept.shape[0], x.shape[1]
    beyond = x.shape[0] - span
    held[...] = lag[...].astype(F32)
    for index, ref in enumerate((x, cot, skip, held)):
        columns = slice(index * width, (index + 1) * width)
        kept[:, columns] = ref[pl.ds(core * beyond, span), :]
        given[:, columns] = ref[pl.ds((1 - core) * beyond, span), :]


def join_body(kept, got, mel, mask, *refs):
    core = place()[2]
    inner, side, near_edge, edge_sent, held, lines = refs[-6:]
    span, width = kept.shape[0], kept.shape[1] // 4
    own, beyond = inner.shape[0], mel.shape[1] - span
    for index in range(4):
        for source, at in ((kept, core), (got, 1 - core)):
            held[:, pl.ds(index * 2 * width + at * width, width)] = source[
                :, index * width : (index + 1) * width
            ]
    blank = jnp.zeros((LANES - mel.shape[0] - 1, mel.shape[1]), F32)
    lines[...] = jnp.concatenate([mel[...], mask[...].astype(F32), blank], axis=0).T
    inner[...] = held[pl.ds(core * EDGE, own), :]
    side[...] = lines[pl.ds(core * own, own), :]
    for ref, at in ((near_edge, (1 - core) * own), (edge_sent, core * own)):
        ref[:, LANES:] = held[pl.ds(at, EDGE), :]
        ref[:, :LANES] = lines[pl.ds(core * beyond + at, EDGE), :]


def widen_body(
    mel, clips, lengths, inner, side, near_edge, edge, *refs
):
    far, near, core = place()[:3]
    x_out, cot_out, skip_out, lag_out, cond, marks = refs[-6:]
    own, full = inner.shape[0], inner.shape[1] // 4
    wide = own + 2 * EDGE
    after = jnp.where(core == 0, near_edge[...], edge[...])
    before = jnp.where(core == 0, edge[...], near_edge[...])
    for index, ref in enumerate((x_out, cot_out, skip_out, lag_out)):
        at = LANES + index * full
        ref[...] = jnp.concatenate(
            [
                inner[:, index * full : (index + 1) * full],
                after[:, at : at + full],
                before[:, at : at + full],
            ],
            axis=0,
        ).astype(ref.dtype)
    side_wide = jnp.concatenate([side[...], after[:, :LANES], before[:, :LANES]], axis=0)
    lane = lax.broadcasted_iota(jnp.int32, (wide, LANES), 1)
    line = lax.broadcasted_iota(jnp.int32, (wide, LANES), 0)
    first = ((far * NEAR + near) * 2 + core) * own
    position = first + jnp.where(line < own + EDGE, line, line - wide)

    def segment(at):
        total = jnp.zeros((wide, LANES), jnp.int32)
        end = jnp.int32(0)
        for clip in range(clips):
            end = end + lengths[clip]
            total = total + (at >= end).astype(jnp.int32)
        return total

    here = segment(position)

    def valid(span):
        return ((position >= span) & (segment(position - span) == here)).astype(F32)

    hot = ((lane - mel) == here).astype(F32)
    value = jnp.where(lane < mel, side_wide, jnp.where(lane < mel + clips, hot, 0.0))
    cond[...] = jnp.where(lane == mel + clips, 1.0, value).astype(BF16)
    keep = side_wide[:, mel : mel + 1]
    marks[...] = jnp.where(
        lane == 0, keep, jnp.where(lane == 1, valid(FIRST_DILATION), valid(1))
    )


def divide_body(mixed, total, g1, push, *refs):
    core = place()[2]
    kept, given, held = refs[-3:]
    width = kept.shape[1] // 4
    held[...] = push[...].astype(F32)
    for index, ref in enumerate((mixed, total, g1, held)):
        columns = slice(index * width, (index + 1) * width)
        kept[:, columns] = ref[:, pl.ds(core * width, width)]
        given[:, columns] = ref[:, pl.ds((1 - core) * width, width)]


def finish_body(kept, got, *refs):
    core = place()[2]
    outs, token = refs[:-1], refs[-1]
    token[...] = jnp.zeros_like(token)
    own, width = kept.shape[0], kept.shape[1] // 4
    for index, ref in enumerate(outs):
        for source, at in ((kept, core), (got, 1 - core)):
            ref[pl.ds(at * own, own), :] = source[:, index * width : (index + 1) * width]


def push_body(push, *refs):
    refs[-1][...] = push[...].astype(BF16)


def input_gradient_body(g1, push, out):
    out[...] = g1[...] + push[...].astype(F32)


def table_gradient(cond_grad, who, mel, clips, speakers):
    lane = lax.broadcasted_iota(jnp.int32, (cond_grad.shape[0], speakers), 1)
    result = jnp.zeros((cond_grad.shape[0], speakers), F32)
    for clip in range(clips):
        column = cond_grad[:, mel + clip : mel + clip + 1]
        result = result + jnp.where(lane == who[clip], column, 0.0)
    return result


def square_body(rows, mel, clips, speakers, count, who, *refs):
    terms, (out, squares) = refs[:count], refs[-2:]
    where, total = sections(rows)
    start = where[6][0]
    value = terms[0][...]
    for term in terms[1:]:
        value = value + term[...].astype(F32)
    out[...] = value
    main = out[:start, :]
    amount = jnp.sum(main * main, keepdims=True)
    for half in range(2):
        block = out[start:, half * LANES : (half + 1) * LANES]
        lane = lax.broadcasted_iota(jnp.int32, block.shape, 1)
        plain = jnp.where((lane < mel) | (lane == mel + clips), block, 0.0)
        amount = amount + jnp.sum(plain * plain, keepdims=True)
        table = table_gradient(block, who, mel, clips, speakers)
        amount = amount + jnp.sum(table * table, keepdims=True)
    squares[...] = jnp.broadcast_to(amount, squares.shape)


def adamw(weight, mean, square, gradient, scale):
    clipped = gradient * scale
    new_mean = BETA_ONE * mean + (1.0 - BETA_ONE) * clipped
    new_square = BETA_TWO * square + (1.0 - BETA_TWO) * clipped * clipped
    fix_one = 1.0 - BETA_ONE**STEP
    fix_two = 1.0 - BETA_TWO**STEP
    update = new_mean / fix_one / (jnp.sqrt(new_square / fix_two) + ADAM_EPS)
    return weight - LEARN_RATE * (update + DECAY * weight), new_mean, new_square


def update_body(rows, mel, clips, who, *refs):
    grads = refs[0:2]
    squares = refs[2]
    old = [refs[3 + 3 * kind : 6 + 3 * kind] for kind in range(6)]
    norm = refs[21]
    new = [refs[22 + 5 * kind : 27 + 5 * kind] for kind in range(6)]
    where, total = sections(rows)
    chans = rows // 2
    grad_norm = jnp.sqrt(jnp.sum(squares[...], axis=0, keepdims=True)[:, 0:1])
    norm[...] = grad_norm
    scale = jnp.minimum(1.0, CLIP_NORM / grad_norm)

    def write(kind, index, gradient):
        weight, mean, square = (ref[index] for ref in old[kind])
        new_weight, new_mean, new_square = adamw(weight, mean, square, gradient, scale)
        for ref, value in zip(
            new[kind],
            (gradient, new_weight, new_mean, new_square, new_weight.astype(BF16)),
        ):
            ref[index] = value

    dil = new[0][0]
    for layer in range(2):
        for tap in range(2):
            for half in range(2):
                at, n = where[2 * tap + half]
                for tile in range(2):
                    dil[strided(layer, tap, half, tile, rows), :] = grads[layer][
                        at : at + n, tile * LANES : (tile + 1) * LANES
                    ]
    weight, mean, square = (ref[...] for ref in old[0])
    new_weight, new_mean, new_square = adamw(weight, mean, square, dil[...], scale)
    new[0][1][...] = new_weight
    new[0][2][...] = new_mean
    new[0][3][...] = new_square
    new[0][4][...] = new_weight.astype(BF16)
    for layer in range(2):
        for half in range(2):
            block = grads[layer][where[6][0] :, half * LANES : (half + 1) * LANES]
            eye = lax.broadcasted_iota(jnp.int32, (chans, chans), 0) == lax.broadcasted_iota(
                jnp.int32, (chans, chans), 1
            )
            column = block[:, mel + clips : mel + clips + 1]
            line = jnp.sum(jnp.where(eye, column, 0.0), axis=0, keepdims=True)
            write(1, (layer, slice(half, half + 1), slice(None)), line)
            write(2, (layer, half), block[:, :mel])
            speakers = old[3][0].shape[-1]
            write(3, (layer, half), table_gradient(block, who, mel, clips, speakers))
        for kind, section in ((4, 4), (5, 5)):
            at, n = where[section]
            write(kind, (layer,), grads[layer][at : at + n, :])


def on_device(
    x_input,
    mel_frames,
    sample_mask,
    clip_length_array,
    speaker_ids,
    cot_out,
    cot_skip,
    *states,
):
    parts = lax.axis_size("tm")
    held_rows, width = x_input.shape
    own, full = held_rows // 2, 2 * width
    wide = own + 2 * EDGE
    mel = mel_frames.shape[0]
    clips = clip_length_array.shape[0]
    hop = FIRST_DILATION // held_rows

    dil_shape = states[0].shape
    rows = dil_shape[2]
    views = (
        [dilated_view(s) for s in states[0:3]]
        + list(states[3:6])
        + [s.transpose(0, 2, 3, 1) for s in states[6:12]]
        + [s.transpose(0, 2, 1) for s in states[12:18]]
    )
    speakers = views[9].shape[-1]
    where, total = sections(rows)
    far = parts // NEAR
    taken = [views[k] for k in (0, 12, 15, 6, 9, 3)]
    packed_type = BF16 if rows % 32 == 0 else F32
    taken = [views[k] for k in (0, 12, 15, 6, 9, 3)]
    packed_type = BF16 if rows % 32 == 0 else F32
    taken.append(x_input)
    pack_one, pack_two, x_low = call(
        functools.partial(start_body, rows, mel, clips),
        (struct((total, 256), packed_type),) * 2 + (struct(x_input.shape, BF16),),
        *taken,
        scalars=(speaker_ids,),
        space=pl.ANY,
        grant=None,
        scratch=[pltpu.VMEM(v.shape, F32) for v in taken]
        + [pltpu.SemaphoreType.DMA((len(taken),))],
    )

    lag = shifted(x_low, "tm", hop)
    span = own + EDGE
    group_one, stacked = along_all(pack_one.astype(BF16), (lag,))
    group_two, stacked = along_all(pack_two.astype(BF16), (stacked,))
    kept, given = call(
        part_body,
        (struct((span, 4 * width)),) * 2,
        x_input,
        cot_out,
        cot_skip,
        lag,
        unread=(stacked,),
        scratch=[pltpu.VMEM(x_input.shape, F32)],
    )
    parts_one, relayed = near_exchange(group_one, (stacked,), LONG)
    parts_two, begun = near_exchange(group_two, (), LONG)
    joined_own = struct((own, 4 * full))
    edge = struct((EDGE, 4 * full + LANES))
    inner, side, near_edge, edge_sent = call(
        join_body,
        (joined_own, struct((own, LANES)), edge, edge),
        kept,
        swap_cores(given),
        mel_frames,
        sample_mask[None, :],
        unread=(relayed,),
        scratch=[pltpu.VMEM((span, 4 * full), F32), pltpu.VMEM((held_rows, LANES), F32)],
    )
    x_wide, cot_wide, skip_wide, lag_wide, cond, marks = call(
        functools.partial(widen_body, mel, clips),
        (
            struct((wide, full)),
            struct((wide, full)),
            struct((wide, full), BF16),
            struct((wide, full), BF16),
            struct((wide, LANES), BF16),
            struct((wide, LANES)),
        ),
        inner,
        side,
        near_edge,
        across_chips(edge_sent),
        scalars=(clip_length_array,),
        unread=(begun,),
    )
    w1_own, w1_oth = joined(parts_one, (marks,))

    half = struct((own, width))
    wave = struct((own, full))
    broad = struct((wide, full))
    low_half = struct((own, width), BF16)
    low_full = struct((own, full), BF16)
    packed = struct((BLOCKS, ROWS, 256), BF16)

    def forward(weights, *earlier, unread=(), flops=1024):
        return call(
            functools.partial(first_body, own),
            (broad, wave, low_full, half, half, low_half, TOKEN),
            x_wide,
            lag_wide,
            cond,
            marks,
            weights,
            *earlier,
            unread=unread,
            flops=flops,
        )

    res, skip, lag1, ta_own, sb_own, hid_own, _ = forward(w1_own, unread=(begun,), flops=LONG)
    u2, s1, _, ta_oth, sb_oth, hid_oth, token = forward(w1_oth, res, skip)

    w2_own, w2_oth = joined(parts_two, (token,))

    def middle(weights, *earlier):
        return call(
            functools.partial(second_body, own),
            (wave, wave, wave, TOKEN if earlier else broad, packed),
            u2,
            s1,
            cond,
            marks,
            cot_wide,
            skip_wide,
            weights,
            *earlier,
        )

    gate_two = call(
        second_forward_body, (struct((wide, width)),) * 2, u2, cond, marks, w2_own
    )
    *sums, grad_oth = middle(w2_oth)
    mixed, skip_total, g2, _, grad_own = middle(w2_own, *sums, *gate_two)

    def totals(terms, unread=()):
        return call(
            functools.partial(square_body, rows, mel, clips, speakers, len(terms)),
            (struct((total, 256)), struct((8, LANES))),
            *terms,
            scalars=(speaker_ids,),
            unread=unread,
        )

    def backward(weights, tanh_a, sig_b, hidden, *earlier, unread):
        last = bool(earlier)
        return call(
            functools.partial(third_body, own, last),
            (wave, low_full if last else TOKEN, TOKEN if last else wave, packed),
            g2,
            x_wide,
            lag1,
            cond,
            marks,
            skip_wide,
            tanh_a,
            sig_b,
            hidden,
            weights,
            *earlier,
            unread=unread,
        )

    grads2, sent2, token = cores_summed(grad_own, grad_oth)
    now, _, lag_sum, grad_oth = backward(w1_oth, ta_oth, sb_oth, hid_oth, unread=(token,))
    g1_part, dlag1, token, grad_own = backward(
        w1_own, ta_own, sb_own, hid_own, now, lag_sum, unread=()
    )
    grads2, sent2, token = near_summed(grads2, sent2, LONG, (token,))
    grads1, sent1, _ = cores_summed(grad_own, grad_oth, (token,))
    last_got = across(sent2, 0)
    terms2, _ = far_terms(grads2, last_got, LONG)
    kept, given = call(
        divide_body,
        (struct((own, 4 * width)),) * 2,
        mixed,
        skip_total,
        g1_part,
        dlag1,
        unread=(terms2[1], terms2[-1]),
        scratch=[pltpu.VMEM((own, full), F32)],
    )
    mixed, skip_total, grad_input, push, token = call(
        finish_body, (struct((held_rows, width)),) * 4 + (TOKEN,), kept, swap_cores(given)
    )
    grads1, sent1, _ = near_summed(grads1, sent1, unread=(terms2[1], terms2[-1]))
    terms1, token = far_terms(grads1, across(sent1, 0))
    push = call(push_body, struct((held_rows, width), BF16), push, unread=(token,))
    grad_input = call(
        input_gradient_body,
        struct((held_rows, width)),
        grad_input,
        shifted(push, "tm", -hop),
    )

    sum2, squares2 = totals(terms2)
    sum1, squares1 = totals(terms1)
    squares = squares1[:1] + squares2[:1]
    squares = squares + swap_cores(squares)
    sent = jnp.broadcast_to(squares[None], (parts, 1, LANES))
    squares = lax.all_to_all(sent, "tm", split_axis=0, concat_axis=0, tiled=True)
    outs = [struct((1, 1))]
    for view in views[0::3]:
        outs += [struct(view.shape)] * 4 + [struct(view.shape, BF16)]
    updated = call(
        functools.partial(update_body, rows, mel, clips),
        tuple(outs),
        sum1,
        sum2,
        squares.reshape(parts, LANES),
        *views,
        scalars=(speaker_ids,),
    )
    grad_norm = updated[0].reshape(())
    backs = (
        [lambda v: dilated_back(v, dil_shape), lambda v: v]
        + [lambda v: v.transpose(0, 3, 1, 2)] * 2
        + [lambda v: v.transpose(0, 2, 1)] * 2
    )
    new = [
        [back(v) for v in updated[1 + 5 * kind : 6 + 5 * kind]] for kind, back in enumerate(backs)
    ]
    return (
        mixed,
        skip_total,
        grad_input,
        grad_norm,
        *[group[0] for group in new],
        *[value for group in new for value in group[1:4]],
        *[group[4] for group in new],
    )


def solution(mesh):
    rows = P("tm", "mp")
    dil = P(None, None, "tm", None, "mp")
    bias = P(None, None, ("mp", "tm"))
    wide = P(None, None, None, ("mp", "tm"))
    square = P(None, "mp", "tm")
    kinds = (dil, bias, wide, wide, square, square)
    thrice = tuple(kind for kind in kinds for _ in range(3))
    return jax.shard_map(
        on_device,
        mesh=mesh,
        in_specs=(rows, P(None, "tm"), P("tm"), P(), P(), rows, rows) + thrice,
        out_specs=(rows, rows, rows, P()) + kinds + thrice + kinds,
        check_vma=False,
    )
```

```python
import functools

import jax
import jax.numpy as jnp
from jax import lax
from jax.experimental import pallas as pl
from jax.experimental.pallas import tpu as pltpu
from jax.sharding import PartitionSpec as P

FIRST_DILATION = 512
STEP = 10
ROOT_HALF = 0.7071067811865476
BETA_ONE = 0.9
BETA_TWO = 0.999
ADAM_EPS = 1e-08
LEARN_RATE = 0.07
DECAY = 0.01
CLIP_NORM = 1.0

F32 = jnp.float32
BF16 = jnp.bfloat16
LANES = 128
EDGE = 8
BLOCKS = 16
NEAR = 4
VMEM_BYTES = 26 * 1024 * 1024
BOTH = ("tm", "mp")


def struct(shape, dtype=F32):
    return jax.ShapeDtypeStruct(shape, dtype)


def call(body, out_shape, *operands, scalars=(), scratch=(), space=pltpu.VMEM, unread=(), flops=1024, grant=VMEM_BYTES):
    specs = [pl.BlockSpec(memory_space=pltpu.SMEM)] * len(scalars)
    specs += [pl.BlockSpec(memory_space=space)] * len(operands)
    specs += [pl.BlockSpec(memory_space=pl.ANY)] * len(unread)
    return pl.pallas_call(
        body,
        out_shape=out_shape,
        in_specs=specs,
        scratch_shapes=list(scratch),
        compiler_params=pltpu.CompilerParams(vmem_limit_bytes=grant),
        cost_estimate=pl.CostEstimate(flops=flops, bytes_accessed=1024, transcendentals=0),
    )(*scalars, *operands, *unread)


def dot(left, right):
    return jnp.dot(left, right, preferred_element_type=F32)


def dot_right(left, right):
    return lax.dot_general(left, right, (((1,), (1,)), ((), ())), preferred_element_type=F32)


def dot_left(left, right):
    return lax.dot_general(left, right, (((0,), (0,)), ((), ())), preferred_element_type=F32)


def place():
    index = lax.axis_index("tm")
    core = lax.axis_index("mp")
    return index // NEAR, index % NEAR, core, 1 + core, 2 - core


def route(target):
    return [
        (index * 2 + core, target(index, core) * 2 + core)
        for index in range(lax.axis_size("tm"))
        for core in range(2)
    ]


def across(value, bit):
    return lax.ppermute(value, BOTH, route(lambda i, c: i ^ (1 + (c ^ bit))))


def along_far(value, distance):
    far = lax.axis_size("tm") // NEAR
    return lax.ppermute(
        value, BOTH, route(lambda i, c: (i // NEAR + distance) % far * NEAR + i % NEAR)
    )


def swap_cores(value):
    return lax.ppermute(value, "mp", [(0, 1), (1, 0)])


def shifted(value, axis, distance):
    devices = range(lax.axis_size(axis))
    pairs = [(i - distance, i) for i in devices if i - distance in devices]
    return lax.ppermute(value, axis, pairs)


def across_chips(value):
    pairs = []
    for index in range(1, lax.axis_size("tm")):
        pairs += [(index * 2 - 1, index * 2), (index * 2, index * 2 - 1)]
    return lax.ppermute(value, BOTH, pairs)


def sections(rows):
    found, at = [], 0
    for count in (rows,) * 6 + (rows // 2,):
        found.append((at, count))
        at += count
    return found, at


WHERE, ROWS = sections(32)


def dilated_view(array):
    layers, taps, rows, halves, width = array.shape
    tiles = width // LANES
    split = array.reshape(layers, taps, rows, halves, tiles, LANES)
    return split.transpose(0, 1, 2, 4, 3, 5).reshape(-1, LANES)


def dilated_back(array, shape):
    layers, taps, rows, halves, width = shape
    tiles = width // LANES
    split = array.reshape(layers, taps, rows, tiles, halves, LANES)
    return split.transpose(0, 1, 2, 4, 3, 5).reshape(shape)


def strided(layer, tap, half, tile, rows):
    return pl.ds((layer * 2 + tap) * rows * 4 + tile * 2 + half, rows, stride=4)


def start_body(rows, mel, clips, who, *refs):
    sources, (out_one, out_two, low), held, sems = refs[:7], refs[7:10], refs[10:17], refs[17]
    copies = [
        pltpu.make_async_copy(source, target, sems.at[index])
        for index, (source, target) in enumerate(zip(sources, held))
    ]
    for copy in copies:
        copy.start()
    dil, res, skip, mel_w, table, bias, samples = held
    where, total = sections(rows)
    chans = rows // 2
    speakers = table.shape[-1]
    lane = lax.broadcasted_iota(jnp.int32, (1, speakers), 1)
    hot = jnp.concatenate([(lane == who[k]).astype(F32) for k in range(clips)], axis=0).astype(BF16)
    eye = lax.broadcasted_iota(jnp.int32, (chans, chans), 0) == lax.broadcasted_iota(
        jnp.int32, (chans, chans), 1
    )

    def write(out, at, count, columns, value):
        out[at : at + count, columns] = value.astype(out.dtype)

    for copy in copies[:-1]:
        copy.wait()
    for layer, out in enumerate((out_one, out_two)):
        for tap in range(2):
            for half in range(2):
                at, count = where[2 * tap + half]
                for tile in range(2):
                    part = dil[strided(layer, tap, half, tile, rows), :]
                    write(out, at, count, slice(tile * LANES, (tile + 1) * LANES), part)
        for kind, source in ((4, res), (5, skip)):
            at, count = where[kind]
            write(out, at, count, slice(None), source[layer])
        at, count = where[6]
        for half in range(2):
            picked = dot_right(table[layer, half].astype(BF16), hot)
            line = jnp.broadcast_to(bias[layer, half : half + 1, :], (chans, chans))
            column = jnp.sum(jnp.where(eye, line, 0.0), axis=1, keepdims=True)
            blank = jnp.zeros((chans, LANES - mel - clips - 1), F32)
            row = jnp.concatenate([mel_w[layer, half], picked, column, blank], axis=1)
            columns = slice(half * LANES, (half + 1) * LANES)
            write(out, at, count, columns, row.astype(BF16).astype(F32))
    copies[-1].wait()
    low[...] = samples[...].astype(BF16)


def assemble_body(group, first, second, last, *refs):
    out = refs[-1]
    count = group.shape[0]
    far, near, _, first_bit, second_bit = place()
    for ref, mask in ((group, 0), (first, first_bit), (second, second_bit), (last, 3)):
        for back in range(count):
            out[lax.rem(far + count - back, count) * NEAR + (near ^ mask)] = ref[back]


def relay_body(value, *refs):
    out, token = refs[-2:]
    out[...] = value[...]
    token[...] = jnp.zeros_like(token)


TOKEN = struct((8, LANES))
LONG = 20_000_000_000


def stack_body(count, *refs):
    out, token = refs[-2:]
    for index in range(count):
        out[index] = refs[index][...]
    token[...] = jnp.zeros_like(token)


def along_all(pack, unread):
    far = lax.axis_size("tm") // NEAR
    got = [along_far(pack, distance) for distance in range(1, far)]
    held, _ = call(relay_body, (struct(pack.shape, BF16), TOKEN), pack)
    return call(
        functools.partial(stack_body, far),
        (struct((far,) + pack.shape, BF16), TOKEN),
        held,
        *got,
        unread=unread,
    )


def near_exchange(group, before_last, flops=1024):
    first = across(group, 0)
    second = across(group, 1)
    passed, token = call(
        relay_body,
        (struct(first.shape, BF16), TOKEN),
        first,
        unread=(second,) + before_last,
        flops=flops,
    )
    return (group, first, second, across(passed, 1)), token


def joined(parts, before_end):
    count = NEAR * parts[0].shape[0]
    own = call(
        assemble_body, struct((count,) + parts[0].shape[1:], BF16), *parts, unread=before_end
    )
    if count != BLOCKS:
        own = to_canonical(own)
    return own, swap_cores(own)


def to_canonical(gathered):
    parts = gathered.shape[0]
    where, total = sections(BLOCKS * 32 // parts)
    return jnp.concatenate(
        [gathered[:, at : at + n, :].reshape(BLOCKS, -1, 256) for at, n in where], axis=1
    )


def from_canonical(packed, parts):
    where, total = sections(32)
    return jnp.concatenate(
        [packed[:, at : at + n, :].reshape(parts, -1, 256) for at, n in where], axis=1
    )


def piece(ref, kind):
    at, count = WHERE[kind]
    return ref[:, at : at + count, :].reshape(-1, 256)


def conditioning(ref, half):
    at, count = WHERE[6]
    return ref[:, at : at + count, half * LANES : (half + 1) * LANES].reshape(-1, LANES)


def slot(ordered, first, block):
    if not ordered:
        return block
    near = lax.axis_index("tm") % NEAR
    mask = (block % NEAR) ^ near
    group = jnp.where(mask == 3, 0, jnp.where(mask == 0, 3, jnp.where(mask == first, 2, 1)))
    return group * (BLOCKS // NEAR) + block // NEAR


def store(ref, slots, kind, value):
    at, count = WHERE[kind]
    value = value.astype(BF16)
    for block in range(BLOCKS):
        ref[slots[block], at : at + count, :] = value[block * count : (block + 1) * count]


def store_conditioning(ref, slots, half, value):
    at, count = WHERE[6]
    value = value.astype(BF16)
    for block in range(BLOCKS):
        ref[slots[block], at : at + count, half * LANES : (half + 1) * LANES] = value[
            block * count : (block + 1) * count
        ]


def order_body(own, other, own_out, other_out):
    parts = own.shape[0]
    far = parts // NEAR
    _, near, _, first, second = place()
    for source, out, bit, next_bit in (
        (own, own_out, first, second),
        (other, other_out, second, first),
    ):
        for group, mask in enumerate((3, next_bit, bit, 0)):
            for index in range(far):
                out[group * far + index] = source[index * NEAR + (near ^ mask)]


def first_sum_body(own, got, *refs):
    out, token = refs[-2:]
    half = out.shape[0]
    out[...] = own[:half] + got[:half]
    token[...] = jnp.zeros_like(token)


def second_sum_body(own, got, near_got, *refs):
    out, token = refs[-2:]
    count = out.shape[0]
    kept = slice(2 * count, 3 * count)
    out[...] = (
        own[kept].astype(F32) + got[kept].astype(F32) + near_got[:count].astype(F32)
    ).astype(BF16)
    token[...] = jnp.zeros_like(token)


def third_sum_body(own, got, near_got, last_got, *refs):
    far = place()[0]
    count = last_got.shape[0]
    token = refs[-1]
    token[...] = jnp.zeros_like(token)
    for distance, out in enumerate(refs[-count - 1 : -1]):
        index = lax.rem(far + distance, count)
        out[...] = (
            own[3 * count + index].astype(F32)
            + got[3 * count + index].astype(F32)
            + near_got[count + index].astype(F32)
            + last_got[index].astype(F32)
        ).astype(out.dtype)


def ordered(grads):
    parts = lax.axis_size("tm")
    return grads if parts == BLOCKS else from_canonical(grads, parts)


def cores_summed(own, other, unread=()):
    own, other = ordered(own), ordered(other)
    if own.shape[0] != BLOCKS:
        own, other = call(order_body, (struct(own.shape, BF16),) * 2, own, other)
    got = swap_cores(other)
    half = struct((own.shape[0] // 2,) + own.shape[1:], BF16)
    sent, token = call(first_sum_body, (half, TOKEN), own, got, unread=unread)
    return (own, got), sent, token


def near_summed(grads, sent, flops=1024, unread=()):
    near_got = across(sent, 1)
    shape = (grads[0].shape[0] // NEAR,) + grads[0].shape[1:]
    sent, token = call(
        second_sum_body,
        (struct(shape, BF16), TOKEN),
        *grads,
        near_got,
        flops=flops,
        unread=unread,
    )
    return grads + (near_got,), sent, token


def far_terms(grads, last_got, flops=1024, unread=()):
    far, *shape = last_got.shape
    kept, *sends, token = call(
        third_sum_body,
        (struct(shape),) + (struct(shape, BF16),) * (far - 1) + (TOKEN,),
        *grads,
        last_got,
        flops=flops,
        unread=unread,
    )
    return [kept] + [along_far(value, k + 1) for k, value in enumerate(sends)], token


def gates(weights, lag, xin, cond):
    za = dot(lag, piece(weights, 0)) + dot(xin, piece(weights, 2))
    za = za + dot_right(cond, conditioning(weights, 0))
    zb = dot(lag, piece(weights, 1)) + dot(xin, piece(weights, 3))
    zb = zb + dot_right(cond, conditioning(weights, 1))
    return jnp.tanh(za), jax.nn.sigmoid(zb)


def gate_gradients(weights, res_grad, skip_grad, keep, tanh_a, sig_b):
    hidden_grad = dot(res_grad, piece(weights, 4)) + dot(skip_grad, piece(weights, 5))
    hidden_grad = hidden_grad * keep
    grad_a = (hidden_grad * sig_b * (1.0 - tanh_a * tanh_a)).astype(BF16)
    grad_b = (hidden_grad * tanh_a * sig_b * (1.0 - sig_b)).astype(BF16)
    return grad_a, grad_b


def weight_gradients(out, bit, lag, xin, cond, grad_a, grad_b, res_grad, skip_grad, hidden):
    slots = [slot(lax.axis_size("tm") == BLOCKS, bit, block) for block in range(BLOCKS)]
    store(out, slots, 0, dot_left(lag, grad_a))
    store(out, slots, 1, dot_left(lag, grad_b))
    store(out, slots, 2, dot_left(xin, grad_a))
    store(out, slots, 3, dot_left(xin, grad_b))
    store(out, slots, 4, dot_left(res_grad, hidden))
    store(out, slots, 5, dot_left(skip_grad, hidden))
    store_conditioning(out, slots, 0, dot_left(grad_a, cond))
    store_conditioning(out, slots, 1, dot_left(grad_b, cond))


def first_body(own, x, lag_raw, cond, marks, weights, *refs):
    earlier, (u2, s1, lag_out, ta, sb, hid, token) = refs[:-7], refs[-7:]
    token[...] = jnp.zeros_like(token)
    keep = marks[:, 0:1]
    xin = x[...].astype(BF16)
    lag = (lag_raw[...].astype(F32) * marks[:, 1:2]).astype(BF16)
    tanh_a, sig_b = gates(weights, lag, xin, cond[...])
    hidden = (keep * tanh_a * sig_b).astype(BF16)
    res = dot_right(hidden, piece(weights, 4))
    skip = dot_right(hidden[:own], piece(weights, 5))
    ta[...] = tanh_a[:own]
    sb[...] = sig_b[:own]
    hid[...] = hidden[:own]
    lag_out[...] = lag[:own]
    if len(earlier) == 2:
        u2[...] = (x[...] + (earlier[0][...] + res)) * ROOT_HALF
        s1[...] = earlier[1][...] + skip
    else:
        u2[...] = res
        s1[...] = skip


def second_input(u2, marks):
    xin = u2[...].astype(BF16)
    lag = (pltpu.roll(xin.astype(F32), 1, 0) * marks[:, 2:3]).astype(BF16)
    return xin, lag


def second_forward_body(u2, cond, marks, weights, ta, sb):
    xin, lag = second_input(u2, marks)
    ta[...], sb[...] = gates(weights, lag, xin, cond[...])


def second_body(own, u2, s1, cond, marks, cot, cot_skip, weights, *refs):
    last = len(refs) > 5
    earlier, (mixed, total, g2, lag_sum, grads) = refs[:-5], refs[-5:]
    rows = u2.shape[0]
    keep = marks[:, 0:1]
    xin, lag = second_input(u2, marks)
    res_grad = (cot[...] * ROOT_HALF).astype(BF16)
    skip_grad = cot_skip[...]
    if last:
        tanh_a, sig_b = earlier[4][...], earlier[5][...]
    else:
        tanh_a, sig_b = gates(weights, lag, xin, cond[...])
    hidden = (keep * tanh_a * sig_b).astype(BF16)[:own]
    grad_a, grad_b = gate_gradients(weights, res_grad, skip_grad, keep, tanh_a, sig_b)
    _, _, _, first_bit, second_bit = place()
    weight_gradients(
        grads,
        first_bit if last else second_bit,
        lag[:own],
        xin[:own],
        cond[:own, :],
        grad_a[:own],
        grad_b[:own],
        res_grad[:own],
        skip_grad[:own],
        hidden,
    )
    res = dot_right(hidden, piece(weights, 4))
    skip = dot_right(hidden, piece(weights, 5))
    lag_grad = dot_right(grad_a, piece(weights, 0)) + dot_right(grad_b, piece(weights, 1))
    now = dot_right(grad_a[:own], piece(weights, 2)) + dot_right(grad_b[:own], piece(weights, 3))
    if last:
        res, skip, now, lag_grad = (
            before[...] + value for before, value in zip(earlier, (res, skip, now, lag_grad))
        )
        mixed[...] = (u2[:own, :] + res) * ROOT_HALF
        total[...] = s1[...] + skip
        pushed = (lag_grad * marks[:, 2:3]).astype(BF16).astype(F32)
        g2[...] = cot[:own, :] * ROOT_HALF + now + pltpu.roll(pushed, rows - 1, 0)[:own]
    else:
        mixed[...] = res
        total[...] = skip
        g2[...] = now
        lag_sum[...] = lag_grad


def third_body(own, last, g2, x, lag, cond, marks, cot_skip, ta, sb, hid, weights, *refs):
    earlier, (g1, dlag, lag_sum, grads) = refs[:-4], refs[-4:]
    keep = marks[:own, 0:1]
    xin = x[:own, :].astype(BF16)
    res_grad = (g2[...] * ROOT_HALF).astype(BF16)
    skip_grad = cot_skip[:own, :]
    grad_a, grad_b = gate_gradients(weights, res_grad, skip_grad, keep, ta[...], sb[...])
    _, _, _, first_bit, second_bit = place()
    weight_gradients(
        grads,
        first_bit if last else second_bit,
        lag[...],
        xin,
        cond[:own, :],
        grad_a,
        grad_b,
        res_grad,
        skip_grad,
        hid[...],
    )
    lag_grad = dot_right(grad_a, piece(weights, 0)) + dot_right(grad_b, piece(weights, 1))
    now = dot_right(grad_a, piece(weights, 2)) + dot_right(grad_b, piece(weights, 3))
    if last:
        lag_sum[...] = jnp.zeros_like(lag_sum)
        g1[...] = g2[...] * ROOT_HALF + (earlier[0][...] + now)
        dlag[...] = ((earlier[1][...] + lag_grad) * marks[:own, 1:2]).astype(BF16)
    else:
        g1[...] = now
        lag_sum[...] = lag_grad


def part_body(x, cot, skip, lag, *refs):
    core = place()[2]
    kept, given, held = refs[-3:]
    span, width = kept.shape[0], x.shape[1]
    beyond = x.shape[0] - span
    held[...] = lag[...].astype(F32)
    for index, ref in enumerate((x, cot, skip, held)):
        columns = slice(index * width, (index + 1) * width)
        kept[:, columns] = ref[pl.ds(core * beyond, span), :]
        given[:, columns] = ref[pl.ds((1 - core) * beyond, span), :]


def join_body(kept, got, mel, mask, *refs):
    core = place()[2]
    inner, side, near_edge, edge_sent, held, lines = refs[-6:]
    span, width = kept.shape[0], kept.shape[1] // 4
    own, beyond = inner.shape[0], mel.shape[1] - span
    for index in range(4):
        for source, at in ((kept, core), (got, 1 - core)):
            held[:, pl.ds(index * 2 * width + at * width, width)] = source[
                :, index * width : (index + 1) * width
            ]
    blank = jnp.zeros((LANES - mel.shape[0] - 1, mel.shape[1]), F32)
    lines[...] = jnp.concatenate([mel[...], mask[...].astype(F32), blank], axis=0).T
    inner[...] = held[pl.ds(core * EDGE, own), :]
    side[...] = lines[pl.ds(core * own, own), :]
    for ref, at in ((near_edge, (1 - core) * own), (edge_sent, core * own)):
        ref[:, LANES:] = held[pl.ds(at, EDGE), :]
        ref[:, :LANES] = lines[pl.ds(core * beyond + at, EDGE), :]


def widen_body(
    mel, clips, lengths, inner, side, near_edge, edge, *refs
):
    far, near, core = place()[:3]
    x_out, cot_out, skip_out, lag_out, cond, marks = refs[-6:]
    own, full = inner.shape[0], inner.shape[1] // 4
    wide = own + 2 * EDGE
    after = jnp.where(core == 0, near_edge[...], edge[...])
    before = jnp.where(core == 0, edge[...], near_edge[...])
    for index, ref in enumerate((x_out, cot_out, skip_out, lag_out)):
        at = LANES + index * full
        ref[...] = jnp.concatenate(
            [
                inner[:, index * full : (index + 1) * full],
                after[:, at : at + full],
                before[:, at : at + full],
            ],
            axis=0,
        ).astype(ref.dtype)
    side_wide = jnp.concatenate([side[...], after[:, :LANES], before[:, :LANES]], axis=0)
    lane = lax.broadcasted_iota(jnp.int32, (wide, LANES), 1)
    line = lax.broadcasted_iota(jnp.int32, (wide, LANES), 0)
    first = ((far * NEAR + near) * 2 + core) * own
    position = first + jnp.where(line < own + EDGE, line, line - wide)

    def segment(at):
        total = jnp.zeros((wide, LANES), jnp.int32)
        end = jnp.int32(0)
        for clip in range(clips):
            end = end + lengths[clip]
            total = total + (at >= end).astype(jnp.int32)
        return total

    here = segment(position)

    def valid(span):
        return ((position >= span) & (segment(position - span) == here)).astype(F32)

    hot = ((lane - mel) == here).astype(F32)
    value = jnp.where(lane < mel, side_wide, jnp.where(lane < mel + clips, hot, 0.0))
    cond[...] = jnp.where(lane == mel + clips, 1.0, value).astype(BF16)
    keep = side_wide[:, mel : mel + 1]
    marks[...] = jnp.where(
        lane == 0, keep, jnp.where(lane == 1, valid(FIRST_DILATION), valid(1))
    )


def divide_body(mixed, total, g1, push, *refs):
    core = place()[2]
    kept, given, held = refs[-3:]
    width = kept.shape[1] // 4
    held[...] = push[...].astype(F32)
    for index, ref in enumerate((mixed, total, g1, held)):
        columns = slice(index * width, (index + 1) * width)
        kept[:, columns] = ref[:, pl.ds(core * width, width)]
        given[:, columns] = ref[:, pl.ds((1 - core) * width, width)]


def finish_body(kept, got, *refs):
    core = place()[2]
    outs, token = refs[:-1], refs[-1]
    token[...] = jnp.zeros_like(token)
    own, width = kept.shape[0], kept.shape[1] // 4
    for index, ref in enumerate(outs):
        for source, at in ((kept, core), (got, 1 - core)):
            ref[pl.ds(at * own, own), :] = source[:, index * width : (index + 1) * width]


def push_body(push, *refs):
    refs[-1][...] = push[...].astype(BF16)


def table_gradient(cond_grad, who, mel, clips, speakers):
    lane = lax.broadcasted_iota(jnp.int32, (cond_grad.shape[0], speakers), 1)
    result = jnp.zeros((cond_grad.shape[0], speakers), F32)
    for clip in range(clips):
        column = cond_grad[:, mel + clip : mel + clip + 1]
        result = result + jnp.where(lane == who[clip], column, 0.0)
    return result


def square_body(rows, mel, clips, speakers, count, who, *refs):
    terms, (out, squares) = refs[:count], refs[-2:]
    where, total = sections(rows)
    start = where[6][0]
    value = terms[0][...]
    for term in terms[1:]:
        value = value + term[...].astype(F32)
    out[...] = value
    main = out[:start, :]
    amount = jnp.sum(main * main, keepdims=True)
    for half in range(2):
        block = out[start:, half * LANES : (half + 1) * LANES]
        lane = lax.broadcasted_iota(jnp.int32, block.shape, 1)
        plain = jnp.where((lane < mel) | (lane == mel + clips), block, 0.0)
        amount = amount + jnp.sum(plain * plain, keepdims=True)
        table = table_gradient(block, who, mel, clips, speakers)
        amount = amount + jnp.sum(table * table, keepdims=True)
    squares[...] = jnp.broadcast_to(amount, squares.shape)


def add_body(left, right, out):
    out[...] = left[...] + right[...]


def spread_body(left, right, out):
    total = left[0:1, :] + right[0:1, :]
    out[...] = jnp.broadcast_to(total[None], out.shape)


def adamw(weight, mean, square, gradient, scale):
    clipped = gradient * scale
    new_mean = BETA_ONE * mean + (1.0 - BETA_ONE) * clipped
    new_square = BETA_TWO * square + (1.0 - BETA_TWO) * clipped * clipped
    fix_one = 1.0 - BETA_ONE**STEP
    fix_two = 1.0 - BETA_TWO**STEP
    update = new_mean / fix_one / (jnp.sqrt(new_square / fix_two) + ADAM_EPS)
    return weight - LEARN_RATE * (update + DECAY * weight), new_mean, new_square


def update_body(rows, mel, clips, who, *refs):
    grads = refs[0:2]
    squares = refs[2]
    old = [refs[3 + 3 * kind : 6 + 3 * kind] for kind in range(6)]
    part, push, norm, grad_input = refs[21:25]
    new = [refs[25 + 5 * kind : 30 + 5 * kind] for kind in range(6)]
    grad_input[...] = part[...] + push[...].astype(F32)
    where, total = sections(rows)
    chans = rows // 2
    grad_norm = jnp.sqrt(jnp.sum(squares[...], axis=0, keepdims=True)[:, 0:1])
    norm[...] = grad_norm
    scale = jnp.minimum(1.0, CLIP_NORM / grad_norm)

    def write(kind, index, gradient):
        weight, mean, square = (ref[index] for ref in old[kind])
        new_weight, new_mean, new_square = adamw(weight, mean, square, gradient, scale)
        for ref, value in zip(
            new[kind],
            (gradient, new_weight, new_mean, new_square, new_weight.astype(BF16)),
        ):
            ref[index] = value

    dil = new[0][0]
    for layer in range(2):
        for tap in range(2):
            for half in range(2):
                at, n = where[2 * tap + half]
                for tile in range(2):
                    dil[strided(layer, tap, half, tile, rows), :] = grads[layer][
                        at : at + n, tile * LANES : (tile + 1) * LANES
                    ]
    weight, mean, square = (ref[...] for ref in old[0])
    new_weight, new_mean, new_square = adamw(weight, mean, square, dil[...], scale)
    new[0][1][...] = new_weight
    new[0][2][...] = new_mean
    new[0][3][...] = new_square
    new[0][4][...] = new_weight.astype(BF16)
    for layer in range(2):
        for half in range(2):
            block = grads[layer][where[6][0] :, half * LANES : (half + 1) * LANES]
            eye = lax.broadcasted_iota(jnp.int32, (chans, chans), 0) == lax.broadcasted_iota(
                jnp.int32, (chans, chans), 1
            )
            column = block[:, mel + clips : mel + clips + 1]
            line = jnp.sum(jnp.where(eye, column, 0.0), axis=0, keepdims=True)
            write(1, (layer, slice(half, half + 1), slice(None)), line)
            write(2, (layer, half), block[:, :mel])
            speakers = old[3][0].shape[-1]
            write(3, (layer, half), table_gradient(block, who, mel, clips, speakers))
        for kind, section in ((4, 4), (5, 5)):
            at, n = where[section]
            write(kind, (layer,), grads[layer][at : at + n, :])


def on_device(
    x_input,
    mel_frames,
    sample_mask,
    clip_length_array,
    speaker_ids,
    cot_out,
    cot_skip,
    *states,
):
    parts = lax.axis_size("tm")
    held_rows, width = x_input.shape
    own, full = held_rows // 2, 2 * width
    wide = own + 2 * EDGE
    mel = mel_frames.shape[0]
    clips = clip_length_array.shape[0]
    hop = FIRST_DILATION // held_rows

    dil_shape = states[0].shape
    rows = dil_shape[2]
    views = (
        [dilated_view(s) for s in states[0:3]]
        + list(states[3:6])
        + [s.transpose(0, 2, 3, 1) for s in states[6:12]]
        + [s.transpose(0, 2, 1) for s in states[12:18]]
    )
    speakers = views[9].shape[-1]
    where, total = sections(rows)
    far = parts // NEAR
    taken = [views[k] for k in (0, 12, 15, 6, 9, 3)]
    packed_type = BF16 if rows % 32 == 0 else F32
    taken = [views[k] for k in (0, 12, 15, 6, 9, 3)]
    packed_type = BF16 if rows % 32 == 0 else F32
    taken.append(x_input)
    pack_one, pack_two, x_low = call(
        functools.partial(start_body, rows, mel, clips),
        (struct((total, 256), packed_type),) * 2 + (struct(x_input.shape, BF16),),
        *taken,
        scalars=(speaker_ids,),
        space=pl.ANY,
        grant=None,
        scratch=[pltpu.VMEM(v.shape, F32) for v in taken]
        + [pltpu.SemaphoreType.DMA((len(taken),))],
    )

    lag = shifted(x_low, "tm", hop)
    span = own + EDGE
    group_one, stacked = along_all(pack_one.astype(BF16), (lag,))
    group_two, stacked = along_all(pack_two.astype(BF16), (stacked,))
    kept, given = call(
        part_body,
        (struct((span, 4 * width)),) * 2,
        x_input,
        cot_out,
        cot_skip,
        lag,
        unread=(stacked,),
        scratch=[pltpu.VMEM(x_input.shape, F32)],
    )
    parts_one, relayed = near_exchange(group_one, (stacked,), LONG)
    parts_two, begun = near_exchange(group_two, (), LONG)
    joined_own = struct((own, 4 * full))
    edge = struct((EDGE, 4 * full + LANES))
    inner, side, near_edge, edge_sent = call(
        join_body,
        (joined_own, struct((own, LANES)), edge, edge),
        kept,
        swap_cores(given),
        mel_frames,
        sample_mask[None, :],
        unread=(relayed,),
        scratch=[pltpu.VMEM((span, 4 * full), F32), pltpu.VMEM((held_rows, LANES), F32)],
    )
    x_wide, cot_wide, skip_wide, lag_wide, cond, marks = call(
        functools.partial(widen_body, mel, clips),
        (
            struct((wide, full)),
            struct((wide, full)),
            struct((wide, full), BF16),
            struct((wide, full), BF16),
            struct((wide, LANES), BF16),
            struct((wide, LANES)),
        ),
        inner,
        side,
        near_edge,
        across_chips(edge_sent),
        scalars=(clip_length_array,),
        unread=(begun,),
    )
    w1_own, w1_oth = joined(parts_one, (marks,))

    half = struct((own, width))
    wave = struct((own, full))
    broad = struct((wide, full))
    low_half = struct((own, width), BF16)
    low_full = struct((own, full), BF16)
    packed = struct((BLOCKS, ROWS, 256), BF16)

    def forward(weights, *earlier, unread=(), flops=1024):
        return call(
            functools.partial(first_body, own),
            (broad, wave, low_full, half, half, low_half, TOKEN),
            x_wide,
            lag_wide,
            cond,
            marks,
            weights,
            *earlier,
            unread=unread,
            flops=flops,
        )

    res, skip, lag1, ta_own, sb_own, hid_own, _ = forward(w1_own, unread=(begun,), flops=LONG)
    u2, s1, _, ta_oth, sb_oth, hid_oth, token = forward(w1_oth, res, skip)

    w2_own, w2_oth = joined(parts_two, (token,))

    def middle(weights, *earlier):
        return call(
            functools.partial(second_body, own),
            (wave, wave, wave, TOKEN if earlier else broad, packed),
            u2,
            s1,
            cond,
            marks,
            cot_wide,
            skip_wide,
            weights,
            *earlier,
        )

    gate_two = call(
        second_forward_body, (struct((wide, width)),) * 2, u2, cond, marks, w2_own
    )
    *sums, grad_oth = middle(w2_oth)
    mixed, skip_total, g2, _, grad_own = middle(w2_own, *sums, *gate_two)

    def totals(terms, unread=()):
        return call(
            functools.partial(square_body, rows, mel, clips, speakers, len(terms)),
            (struct((total, 256)), struct((8, LANES))),
            *terms,
            scalars=(speaker_ids,),
            unread=unread,
        )

    def backward(weights, tanh_a, sig_b, hidden, *earlier, unread):
        last = bool(earlier)
        return call(
            functools.partial(third_body, own, last),
            (wave, low_full if last else TOKEN, TOKEN if last else wave, packed),
            g2,
            x_wide,
            lag1,
            cond,
            marks,
            skip_wide,
            tanh_a,
            sig_b,
            hidden,
            weights,
            *earlier,
            unread=unread,
        )

    grads2, sent2, token = cores_summed(grad_own, grad_oth)
    now, _, lag_sum, grad_oth = backward(w1_oth, ta_oth, sb_oth, hid_oth, unread=(token,))
    g1_part, dlag1, backed, grad_own = backward(
        w1_own, ta_own, sb_own, hid_own, now, lag_sum, unread=()
    )
    kept, given = call(
        divide_body,
        (struct((own, 4 * width)),) * 2,
        mixed,
        skip_total,
        g1_part,
        dlag1,
        scratch=[pltpu.VMEM((own, full), F32)],
    )
    mixed, skip_total, grad_input, push, token = call(
        finish_body, (struct((held_rows, width)),) * 4 + (TOKEN,), kept, swap_cores(given)
    )
    grads2, sent2, summed = near_summed(grads2, sent2, LONG, (backed,))
    grads1, sent1, _ = cores_summed(grad_own, grad_oth, (summed, token))
    last_got = across(sent2, 0)
    terms2, _ = far_terms(grads2, last_got, LONG)
    grads1, sent1, _ = near_summed(grads1, sent1, unread=(terms2[1], terms2[-1]))
    terms1, _ = far_terms(grads1, across(sent1, 0), unread=tuple(terms2[1:]))
    sum2, squares2 = totals(terms2)
    push = call(push_body, struct((held_rows, width), BF16), push)
    push = shifted(push, "tm", -hop)
    sum1, squares1 = totals(terms1, (push,))
    squares = call(add_body, TOKEN, squares1, squares2)
    sent = call(spread_body, struct((parts, 1, LANES)), squares, swap_cores(squares))
    squares = lax.all_to_all(sent, "tm", split_axis=0, concat_axis=0, tiled=True)
    outs = [struct((1, 1)), struct((held_rows, width))]
    for view in views[0::3]:
        outs += [struct(view.shape)] * 4 + [struct(view.shape, BF16)]
    updated = call(
        functools.partial(update_body, rows, mel, clips),
        tuple(outs),
        sum1,
        sum2,
        squares.reshape(parts, LANES),
        *views,
        grad_input,
        push,
        scalars=(speaker_ids,),
    )
    grad_norm, grad_input = updated[0].reshape(()), updated[1]
    backs = (
        [lambda v: dilated_back(v, dil_shape), lambda v: v]
        + [lambda v: v.transpose(0, 3, 1, 2)] * 2
        + [lambda v: v.transpose(0, 2, 1)] * 2
    )
    new = [
        [back(v) for v in updated[2 + 5 * kind : 7 + 5 * kind]] for kind, back in enumerate(backs)
    ]
    return (
        mixed,
        skip_total,
        grad_input,
        grad_norm,
        *[group[0] for group in new],
        *[value for group in new for value in group[1:4]],
        *[group[4] for group in new],
    )


def solution(mesh):
    rows = P("tm", "mp")
    dil = P(None, None, "tm", None, "mp")
    bias = P(None, None, ("mp", "tm"))
    wide = P(None, None, None, ("mp", "tm"))
    square = P(None, "mp", "tm")
    kinds = (dil, bias, wide, wide, square, square)
    thrice = tuple(kind for kind in kinds for _ in range(3))
    return jax.shard_map(
        on_device,
        mesh=mesh,
        in_specs=(rows, P(None, "tm"), P("tm"), P(), P(), rows, rows) + thrice,
        out_specs=(rows, rows, rows, P()) + kinds + thrice + kinds,
        check_vma=False,
    )
```

```python
import functools

import jax
import jax.numpy as jnp
from jax import lax
from jax.experimental import pallas as pl
from jax.experimental.pallas import tpu as pltpu
from jax.sharding import PartitionSpec as P

FIRST_DILATION = 512
STEP = 10
ROOT_HALF = 0.7071067811865476
BETA_ONE = 0.9
BETA_TWO = 0.999
ADAM_EPS = 1e-08
LEARN_RATE = 0.07
DECAY = 0.01
CLIP_NORM = 1.0

F32 = jnp.float32
BF16 = jnp.bfloat16
LANES = 128
EDGE = 8
BLOCKS = 16
NEAR = 4
VMEM_BYTES = 26 * 1024 * 1024
BOTH = ("tm", "mp")


def struct(shape, dtype=F32):
    return jax.ShapeDtypeStruct(shape, dtype)


def call(body, out_shape, *operands, scalars=(), scratch=(), space=pltpu.VMEM, unread=(), flops=1024, grant=VMEM_BYTES):
    specs = [pl.BlockSpec(memory_space=pltpu.SMEM)] * len(scalars)
    specs += [pl.BlockSpec(memory_space=space)] * len(operands)
    specs += [pl.BlockSpec(memory_space=pl.ANY)] * len(unread)
    return pl.pallas_call(
        body,
        out_shape=out_shape,
        in_specs=specs,
        scratch_shapes=list(scratch),
        compiler_params=pltpu.CompilerParams(vmem_limit_bytes=grant),
        cost_estimate=pl.CostEstimate(flops=flops, bytes_accessed=1024, transcendentals=0),
    )(*scalars, *operands, *unread)


def dot(left, right):
    return jnp.dot(left, right, preferred_element_type=F32)


def dot_right(left, right):
    return lax.dot_general(left, right, (((1,), (1,)), ((), ())), preferred_element_type=F32)


def dot_left(left, right):
    return lax.dot_general(left, right, (((0,), (0,)), ((), ())), preferred_element_type=F32)


def place():
    index = lax.axis_index("tm")
    core = lax.axis_index("mp")
    return index // NEAR, index % NEAR, core, 1 + core, 2 - core


def route(target):
    return [
        (index * 2 + core, target(index, core) * 2 + core)
        for index in range(lax.axis_size("tm"))
        for core in range(2)
    ]


def across(value, bit):
    return lax.ppermute(value, BOTH, route(lambda i, c: i ^ (1 + (c ^ bit))))


def along_far(value, distance):
    far = lax.axis_size("tm") // NEAR
    return lax.ppermute(
        value, BOTH, route(lambda i, c: (i // NEAR + distance) % far * NEAR + i % NEAR)
    )


def swap_cores(value):
    return lax.ppermute(value, "mp", [(0, 1), (1, 0)])


def shifted(value, axis, distance):
    devices = range(lax.axis_size(axis))
    pairs = [(i - distance, i) for i in devices if i - distance in devices]
    return lax.ppermute(value, axis, pairs)


def across_chips(value):
    pairs = []
    for index in range(1, lax.axis_size("tm")):
        pairs += [(index * 2 - 1, index * 2), (index * 2, index * 2 - 1)]
    return lax.ppermute(value, BOTH, pairs)


def sections(rows):
    found, at = [], 0
    for count in (rows,) * 6 + (rows // 2,):
        found.append((at, count))
        at += count
    return found, at


WHERE, ROWS = sections(32)


def dilated_view(array):
    layers, taps, rows, halves, width = array.shape
    tiles = width // LANES
    split = array.reshape(layers, taps, rows, halves, tiles, LANES)
    return split.transpose(0, 1, 2, 4, 3, 5).reshape(-1, LANES)


def dilated_back(array, shape):
    layers, taps, rows, halves, width = shape
    tiles = width // LANES
    split = array.reshape(layers, taps, rows, tiles, halves, LANES)
    return split.transpose(0, 1, 2, 4, 3, 5).reshape(shape)


def strided(layer, tap, half, tile, rows):
    return pl.ds((layer * 2 + tap) * rows * 4 + tile * 2 + half, rows, stride=4)


def start_body(rows, mel, clips, who, *refs):
    sources, (out_one, out_two, low), held, sems = refs[:7], refs[7:10], refs[10:17], refs[17]
    copies = [
        pltpu.make_async_copy(source, target, sems.at[index])
        for index, (source, target) in enumerate(zip(sources, held))
    ]
    for copy in copies:
        copy.start()
    dil, res, skip, mel_w, table, bias, samples = held
    where, total = sections(rows)
    chans = rows // 2
    speakers = table.shape[-1]
    lane = lax.broadcasted_iota(jnp.int32, (1, speakers), 1)
    hot = jnp.concatenate([(lane == who[k]).astype(F32) for k in range(clips)], axis=0).astype(BF16)
    eye = lax.broadcasted_iota(jnp.int32, (chans, chans), 0) == lax.broadcasted_iota(
        jnp.int32, (chans, chans), 1
    )

    def write(out, at, count, columns, value):
        out[at : at + count, columns] = value.astype(out.dtype)

    for copy in copies[:-1]:
        copy.wait()
    for layer, out in enumerate((out_one, out_two)):
        for tap in range(2):
            for half in range(2):
                at, count = where[2 * tap + half]
                for tile in range(2):
                    part = dil[strided(layer, tap, half, tile, rows), :]
                    write(out, at, count, slice(tile * LANES, (tile + 1) * LANES), part)
        for kind, source in ((4, res), (5, skip)):
            at, count = where[kind]
            write(out, at, count, slice(None), source[layer])
        at, count = where[6]
        for half in range(2):
            picked = dot_right(table[layer, half].astype(BF16), hot)
            line = jnp.broadcast_to(bias[layer, half : half + 1, :], (chans, chans))
            column = jnp.sum(jnp.where(eye, line, 0.0), axis=1, keepdims=True)
            blank = jnp.zeros((chans, LANES - mel - clips - 1), F32)
            row = jnp.concatenate([mel_w[layer, half], picked, column, blank], axis=1)
            columns = slice(half * LANES, (half + 1) * LANES)
            write(out, at, count, columns, row.astype(BF16).astype(F32))
    copies[-1].wait()
    low[...] = samples[...].astype(BF16)


def assemble_body(group, first, second, last, *refs):
    out = refs[-1]
    count = group.shape[0]
    far, near, _, first_bit, second_bit = place()
    for ref, mask in ((group, 0), (first, first_bit), (second, second_bit), (last, 3)):
        for back in range(count):
            out[lax.rem(far + count - back, count) * NEAR + (near ^ mask)] = ref[back]


def relay_body(value, *refs):
    out, token = refs[-2:]
    out[...] = value[...]
    token[...] = jnp.zeros_like(token)


TOKEN = struct((8, LANES))
LONG = 20_000_000_000


def stack_body(count, *refs):
    out, token = refs[-2:]
    for index in range(count):
        out[index] = refs[index][...]
    token[...] = jnp.zeros_like(token)


def along_all(pack, unread):
    far = lax.axis_size("tm") // NEAR
    got = [along_far(pack, distance) for distance in range(1, far)]
    held, _ = call(relay_body, (struct(pack.shape, BF16), TOKEN), pack)
    return call(
        functools.partial(stack_body, far),
        (struct((far,) + pack.shape, BF16), TOKEN),
        held,
        *got,
        unread=unread,
    )


def near_exchange(group, before_last, flops=1024):
    first = across(group, 0)
    second = across(group, 1)
    passed, token = call(
        relay_body,
        (struct(first.shape, BF16), TOKEN),
        first,
        unread=(second,) + before_last,
        flops=flops,
    )
    return (group, first, second, across(passed, 1)), token


def joined(parts, before_end):
    count = NEAR * parts[0].shape[0]
    own = call(
        assemble_body, struct((count,) + parts[0].shape[1:], BF16), *parts, unread=before_end
    )
    if count != BLOCKS:
        own = to_canonical(own)
    return own, swap_cores(own)


def to_canonical(gathered):
    parts = gathered.shape[0]
    where, total = sections(BLOCKS * 32 // parts)
    return jnp.concatenate(
        [gathered[:, at : at + n, :].reshape(BLOCKS, -1, 256) for at, n in where], axis=1
    )


def from_canonical(packed, parts):
    where, total = sections(32)
    return jnp.concatenate(
        [packed[:, at : at + n, :].reshape(parts, -1, 256) for at, n in where], axis=1
    )


def piece(ref, kind):
    at, count = WHERE[kind]
    return ref[:, at : at + count, :].reshape(-1, 256)


def conditioning(ref, half):
    at, count = WHERE[6]
    return ref[:, at : at + count, half * LANES : (half + 1) * LANES].reshape(-1, LANES)


def slot(ordered, first, block):
    if not ordered:
        return block
    near = lax.axis_index("tm") % NEAR
    mask = (block % NEAR) ^ near
    group = jnp.where(mask == 3, 0, jnp.where(mask == 0, 3, jnp.where(mask == first, 2, 1)))
    return group * (BLOCKS // NEAR) + block // NEAR


def store(ref, slots, kind, value):
    at, count = WHERE[kind]
    value = value.astype(BF16)
    for block in range(BLOCKS):
        ref[slots[block], at : at + count, :] = value[block * count : (block + 1) * count]


def store_conditioning(ref, slots, half, value):
    at, count = WHERE[6]
    value = value.astype(BF16)
    for block in range(BLOCKS):
        ref[slots[block], at : at + count, half * LANES : (half + 1) * LANES] = value[
            block * count : (block + 1) * count
        ]


def order_body(own, other, own_out, other_out):
    parts = own.shape[0]
    far = parts // NEAR
    _, near, _, first, second = place()
    for source, out, bit, next_bit in (
        (own, own_out, first, second),
        (other, other_out, second, first),
    ):
        for group, mask in enumerate((3, next_bit, bit, 0)):
            for index in range(far):
                out[group * far + index] = source[index * NEAR + (near ^ mask)]


def first_sum_body(own, got, *refs):
    out, token = refs[-2:]
    half = out.shape[0]
    out[...] = own[:half] + got[:half]
    token[...] = jnp.zeros_like(token)


def second_sum_body(own, got, near_got, *refs):
    out, token = refs[-2:]
    count = out.shape[0]
    kept = slice(2 * count, 3 * count)
    out[...] = (
        own[kept].astype(F32) + got[kept].astype(F32) + near_got[:count].astype(F32)
    ).astype(BF16)
    token[...] = jnp.zeros_like(token)


def third_sum_body(own, got, near_got, last_got, *refs):
    far = place()[0]
    count = last_got.shape[0]
    token = refs[-1]
    token[...] = jnp.zeros_like(token)
    for distance, out in enumerate(refs[-count - 1 : -1]):
        index = lax.rem(far + distance, count)
        out[...] = (
            own[3 * count + index].astype(F32)
            + got[3 * count + index].astype(F32)
            + near_got[count + index].astype(F32)
            + last_got[index].astype(F32)
        ).astype(out.dtype)


def ordered(grads):
    parts = lax.axis_size("tm")
    return grads if parts == BLOCKS else from_canonical(grads, parts)


def cores_summed(own, other, unread=()):
    own, other = ordered(own), ordered(other)
    if own.shape[0] != BLOCKS:
        own, other = call(order_body, (struct(own.shape, BF16),) * 2, own, other)
    got = swap_cores(other)
    half = struct((own.shape[0] // 2,) + own.shape[1:], BF16)
    sent, token = call(first_sum_body, (half, TOKEN), own, got, unread=unread)
    return (own, got), sent, token


def near_summed(grads, sent, flops=1024, unread=()):
    near_got = across(sent, 1)
    shape = (grads[0].shape[0] // NEAR,) + grads[0].shape[1:]
    sent, token = call(
        second_sum_body,
        (struct(shape, BF16), TOKEN),
        *grads,
        near_got,
        flops=flops,
        unread=unread,
    )
    return grads + (near_got,), sent, token


def far_terms(grads, last_got, flops=1024, unread=()):
    far, *shape = last_got.shape
    kept, *sends, token = call(
        third_sum_body,
        (struct(shape),) + (struct(shape, BF16),) * (far - 1) + (TOKEN,),
        *grads,
        last_got,
        flops=flops,
        unread=unread,
    )
    return [kept] + [along_far(value, k + 1) for k, value in enumerate(sends)], token


def gates(weights, lag, xin, cond):
    za = dot(lag, piece(weights, 0)) + dot(xin, piece(weights, 2))
    za = za + dot_right(cond, conditioning(weights, 0))
    zb = dot(lag, piece(weights, 1)) + dot(xin, piece(weights, 3))
    zb = zb + dot_right(cond, conditioning(weights, 1))
    return jnp.tanh(za), jax.nn.sigmoid(zb)


def gate_gradients(weights, res_grad, skip_grad, keep, tanh_a, sig_b):
    hidden_grad = dot(res_grad, piece(weights, 4)) + dot(skip_grad, piece(weights, 5))
    hidden_grad = hidden_grad * keep
    grad_a = (hidden_grad * sig_b * (1.0 - tanh_a * tanh_a)).astype(BF16)
    grad_b = (hidden_grad * tanh_a * sig_b * (1.0 - sig_b)).astype(BF16)
    return grad_a, grad_b


def weight_gradients(out, bit, lag, xin, cond, grad_a, grad_b, res_grad, skip_grad, hidden):
    slots = [slot(lax.axis_size("tm") == BLOCKS, bit, block) for block in range(BLOCKS)]
    store(out, slots, 0, dot_left(lag, grad_a))
    store(out, slots, 1, dot_left(lag, grad_b))
    store(out, slots, 2, dot_left(xin, grad_a))
    store(out, slots, 3, dot_left(xin, grad_b))
    store(out, slots, 4, dot_left(res_grad, hidden))
    store(out, slots, 5, dot_left(skip_grad, hidden))
    store_conditioning(out, slots, 0, dot_left(grad_a, cond))
    store_conditioning(out, slots, 1, dot_left(grad_b, cond))


def first_body(own, x, lag_raw, cond, marks, weights, *refs):
    earlier, (u2, s1, lag_out, ta, sb, hid, token) = refs[:-7], refs[-7:]
    token[...] = jnp.zeros_like(token)
    keep = marks[:, 0:1]
    xin = x[...].astype(BF16)
    lag = (lag_raw[...].astype(F32) * marks[:, 1:2]).astype(BF16)
    tanh_a, sig_b = gates(weights, lag, xin, cond[...])
    hidden = (keep * tanh_a * sig_b).astype(BF16)
    res = dot_right(hidden, piece(weights, 4))
    skip = dot_right(hidden[:own], piece(weights, 5))
    ta[...] = tanh_a[:own]
    sb[...] = sig_b[:own]
    hid[...] = hidden[:own]
    lag_out[...] = lag[:own]
    if len(earlier) == 2:
        u2[...] = (x[...] + (earlier[0][...] + res)) * ROOT_HALF
        s1[...] = earlier[1][...] + skip
    else:
        u2[...] = res
        s1[...] = skip


def second_input(u2, marks):
    xin = u2[...].astype(BF16)
    lag = (pltpu.roll(xin.astype(F32), 1, 0) * marks[:, 2:3]).astype(BF16)
    return xin, lag


def second_forward_body(u2, cond, marks, weights, ta, sb):
    xin, lag = second_input(u2, marks)
    ta[...], sb[...] = gates(weights, lag, xin, cond[...])


def second_body(own, u2, s1, cond, marks, cot, cot_skip, weights, *refs):
    last = len(refs) > 5
    earlier, (mixed, total, g2, lag_sum, grads) = refs[:-5], refs[-5:]
    rows = u2.shape[0]
    keep = marks[:, 0:1]
    xin, lag = second_input(u2, marks)
    res_grad = (cot[...] * ROOT_HALF).astype(BF16)
    skip_grad = cot_skip[...]
    if last:
        tanh_a, sig_b = earlier[4][...], earlier[5][...]
    else:
        tanh_a, sig_b = gates(weights, lag, xin, cond[...])
    hidden = (keep * tanh_a * sig_b).astype(BF16)[:own]
    grad_a, grad_b = gate_gradients(weights, res_grad, skip_grad, keep, tanh_a, sig_b)
    _, _, _, first_bit, second_bit = place()
    weight_gradients(
        grads,
        first_bit if last else second_bit,
        lag[:own],
        xin[:own],
        cond[:own, :],
        grad_a[:own],
        grad_b[:own],
        res_grad[:own],
        skip_grad[:own],
        hidden,
    )
    res = dot_right(hidden, piece(weights, 4))
    skip = dot_right(hidden, piece(weights, 5))
    lag_grad = dot_right(grad_a, piece(weights, 0)) + dot_right(grad_b, piece(weights, 1))
    now = dot_right(grad_a[:own], piece(weights, 2)) + dot_right(grad_b[:own], piece(weights, 3))
    if last:
        res, skip, now, lag_grad = (
            before[...] + value for before, value in zip(earlier, (res, skip, now, lag_grad))
        )
        mixed[...] = (u2[:own, :] + res) * ROOT_HALF
        total[...] = s1[...] + skip
        pushed = (lag_grad * marks[:, 2:3]).astype(BF16).astype(F32)
        g2[...] = cot[:own, :] * ROOT_HALF + now + pltpu.roll(pushed, rows - 1, 0)[:own]
    else:
        mixed[...] = res
        total[...] = skip
        g2[...] = now
        lag_sum[...] = lag_grad


def third_body(own, last, g2, x, lag, cond, marks, cot_skip, ta, sb, hid, weights, *refs):
    earlier, (g1, dlag, lag_sum, grads) = refs[:-4], refs[-4:]
    keep = marks[:own, 0:1]
    xin = x[:own, :].astype(BF16)
    res_grad = (g2[...] * ROOT_HALF).astype(BF16)
    skip_grad = cot_skip[:own, :]
    grad_a, grad_b = gate_gradients(weights, res_grad, skip_grad, keep, ta[...], sb[...])
    _, _, _, first_bit, second_bit = place()
    weight_gradients(
        grads,
        first_bit if last else second_bit,
        lag[...],
        xin,
        cond[:own, :],
        grad_a,
        grad_b,
        res_grad,
        skip_grad,
        hid[...],
    )
    lag_grad = dot_right(grad_a, piece(weights, 0)) + dot_right(grad_b, piece(weights, 1))
    now = dot_right(grad_a, piece(weights, 2)) + dot_right(grad_b, piece(weights, 3))
    if last:
        lag_sum[...] = jnp.zeros_like(lag_sum)
        g1[...] = g2[...] * ROOT_HALF + (earlier[0][...] + now)
        dlag[...] = ((earlier[1][...] + lag_grad) * marks[:own, 1:2]).astype(BF16)
    else:
        g1[...] = now
        lag_sum[...] = lag_grad


def part_body(x, cot, skip, lag, *refs):
    core = place()[2]
    kept, given, held = refs[-3:]
    span, width = kept.shape[0], x.shape[1]
    beyond = x.shape[0] - span
    held[...] = lag[...].astype(F32)
    for index, ref in enumerate((x, cot, skip, held)):
        columns = slice(index * width, (index + 1) * width)
        kept[:, columns] = ref[pl.ds(core * beyond, span), :]
        given[:, columns] = ref[pl.ds((1 - core) * beyond, span), :]


def join_body(kept, got, mel, mask, *refs):
    core = place()[2]
    inner, side, near_edge, edge_sent, held, lines = refs[-6:]
    span, width = kept.shape[0], kept.shape[1] // 4
    own, beyond = inner.shape[0], mel.shape[1] - span
    for index in range(4):
        for source, at in ((kept, core), (got, 1 - core)):
            held[:, pl.ds(index * 2 * width + at * width, width)] = source[
                :, index * width : (index + 1) * width
            ]
    blank = jnp.zeros((LANES - mel.shape[0] - 1, mel.shape[1]), F32)
    lines[...] = jnp.concatenate([mel[...], mask[...].astype(F32), blank], axis=0).T
    inner[...] = held[pl.ds(core * EDGE, own), :]
    side[...] = lines[pl.ds(core * own, own), :]
    for ref, at in ((near_edge, (1 - core) * own), (edge_sent, core * own)):
        ref[:, LANES:] = held[pl.ds(at, EDGE), :]
        ref[:, :LANES] = lines[pl.ds(core * beyond + at, EDGE), :]


def widen_body(
    mel, clips, lengths, inner, side, near_edge, edge, *refs
):
    far, near, core = place()[:3]
    x_out, cot_out, skip_out, lag_out, cond, marks = refs[-6:]
    own, full = inner.shape[0], inner.shape[1] // 4
    wide = own + 2 * EDGE
    after = jnp.where(core == 0, near_edge[...], edge[...])
    before = jnp.where(core == 0, edge[...], near_edge[...])
    for index, ref in enumerate((x_out, cot_out, skip_out, lag_out)):
        at = LANES + index * full
        ref[...] = jnp.concatenate(
            [
                inner[:, index * full : (index + 1) * full],
                after[:, at : at + full],
                before[:, at : at + full],
            ],
            axis=0,
        ).astype(ref.dtype)
    side_wide = jnp.concatenate([side[...], after[:, :LANES], before[:, :LANES]], axis=0)
    lane = lax.broadcasted_iota(jnp.int32, (wide, LANES), 1)
    line = lax.broadcasted_iota(jnp.int32, (wide, LANES), 0)
    first = ((far * NEAR + near) * 2 + core) * own
    position = first + jnp.where(line < own + EDGE, line, line - wide)

    def segment(at):
        total = jnp.zeros((wide, LANES), jnp.int32)
        end = jnp.int32(0)
        for clip in range(clips):
            end = end + lengths[clip]
            total = total + (at >= end).astype(jnp.int32)
        return total

    here = segment(position)

    def valid(span):
        return ((position >= span) & (segment(position - span) == here)).astype(F32)

    hot = ((lane - mel) == here).astype(F32)
    value = jnp.where(lane < mel, side_wide, jnp.where(lane < mel + clips, hot, 0.0))
    cond[...] = jnp.where(lane == mel + clips, 1.0, value).astype(BF16)
    keep = side_wide[:, mel : mel + 1]
    marks[...] = jnp.where(
        lane == 0, keep, jnp.where(lane == 1, valid(FIRST_DILATION), valid(1))
    )


def divide_body(mixed, total, g1, push, *refs):
    core = place()[2]
    kept, given, held = refs[-3:]
    width = kept.shape[1] // 4
    held[...] = push[...].astype(F32)
    for index, ref in enumerate((mixed, total, g1, held)):
        columns = slice(index * width, (index + 1) * width)
        kept[:, columns] = ref[:, pl.ds(core * width, width)]
        given[:, columns] = ref[:, pl.ds((1 - core) * width, width)]


def finish_body(kept, got, *refs):
    core = place()[2]
    outs, token = refs[:-1], refs[-1]
    token[...] = jnp.zeros_like(token)
    own, width = kept.shape[0], kept.shape[1] // 4
    for index, ref in enumerate(outs):
        for source, at in ((kept, core), (got, 1 - core)):
            ref[pl.ds(at * own, own), :] = source[:, index * width : (index + 1) * width]


def push_body(push, *refs):
    refs[-1][...] = push[...].astype(BF16)


def table_gradient(cond_grad, who, mel, clips, speakers):
    lane = lax.broadcasted_iota(jnp.int32, (cond_grad.shape[0], speakers), 1)
    result = jnp.zeros((cond_grad.shape[0], speakers), F32)
    for clip in range(clips):
        column = cond_grad[:, mel + clip : mel + clip + 1]
        result = result + jnp.where(lane == who[clip], column, 0.0)
    return result


def square_body(rows, mel, clips, speakers, count, who, *refs):
    terms, (out, squares) = refs[:count], refs[-2:]
    where, total = sections(rows)
    start = where[6][0]
    value = terms[0][...]
    for term in terms[1:]:
        value = value + term[...].astype(F32)
    out[...] = value
    main = out[:start, :]
    amount = jnp.sum(main * main, keepdims=True)
    for half in range(2):
        block = out[start:, half * LANES : (half + 1) * LANES]
        lane = lax.broadcasted_iota(jnp.int32, block.shape, 1)
        plain = jnp.where((lane < mel) | (lane == mel + clips), block, 0.0)
        amount = amount + jnp.sum(plain * plain, keepdims=True)
        table = table_gradient(block, who, mel, clips, speakers)
        amount = amount + jnp.sum(table * table, keepdims=True)
    squares[...] = jnp.broadcast_to(amount, squares.shape)


def add_body(left, right, out):
    out[...] = left[...] + right[...]


def spread_body(left, right, out):
    total = left[0:1, :] + right[0:1, :]
    out[...] = jnp.broadcast_to(total[None], out.shape)


def adamw(weight, mean, square, gradient, scale):
    clipped = gradient * scale
    new_mean = BETA_ONE * mean + (1.0 - BETA_ONE) * clipped
    new_square = BETA_TWO * square + (1.0 - BETA_TWO) * clipped * clipped
    fix_one = 1.0 - BETA_ONE**STEP
    fix_two = 1.0 - BETA_TWO**STEP
    update = new_mean / fix_one / (jnp.sqrt(new_square / fix_two) + ADAM_EPS)
    return weight - LEARN_RATE * (update + DECAY * weight), new_mean, new_square


def update_body(rows, mel, clips, who, *refs):
    grads = refs[0:2]
    squares = refs[2]
    old = [refs[3 + 3 * kind : 6 + 3 * kind] for kind in range(6)]
    part, push, norm, grad_input = refs[21:25]
    new = [refs[25 + 5 * kind : 30 + 5 * kind] for kind in range(6)]
    grad_input[...] = part[...] + push[...].astype(F32)
    where, total = sections(rows)
    chans = rows // 2
    grad_norm = jnp.sqrt(jnp.sum(squares[...], axis=0, keepdims=True)[:, 0:1])
    norm[...] = grad_norm
    scale = jnp.minimum(1.0, CLIP_NORM / grad_norm)

    def write(kind, index, gradient):
        weight, mean, square = (ref[index] for ref in old[kind])
        new_weight, new_mean, new_square = adamw(weight, mean, square, gradient, scale)
        for ref, value in zip(
            new[kind],
            (gradient, new_weight, new_mean, new_square, new_weight.astype(BF16)),
        ):
            ref[index] = value

    dil = new[0][0]
    for layer in range(2):
        for tap in range(2):
            for half in range(2):
                at, n = where[2 * tap + half]
                for tile in range(2):
                    dil[strided(layer, tap, half, tile, rows), :] = grads[layer][
                        at : at + n, tile * LANES : (tile + 1) * LANES
                    ]
    weight, mean, square = (ref[...] for ref in old[0])
    new_weight, new_mean, new_square = adamw(weight, mean, square, dil[...], scale)
    new[0][1][...] = new_weight
    new[0][2][...] = new_mean
    new[0][3][...] = new_square
    new[0][4][...] = new_weight.astype(BF16)
    for layer in range(2):
        for half in range(2):
            block = grads[layer][where[6][0] :, half * LANES : (half + 1) * LANES]
            eye = lax.broadcasted_iota(jnp.int32, (chans, chans), 0) == lax.broadcasted_iota(
                jnp.int32, (chans, chans), 1
            )
            column = block[:, mel + clips : mel + clips + 1]
            line = jnp.sum(jnp.where(eye, column, 0.0), axis=0, keepdims=True)
            write(1, (layer, slice(half, half + 1), slice(None)), line)
            write(2, (layer, half), block[:, :mel])
            speakers = old[3][0].shape[-1]
            write(3, (layer, half), table_gradient(block, who, mel, clips, speakers))
        for kind, section in ((4, 4), (5, 5)):
            at, n = where[section]
            write(kind, (layer,), grads[layer][at : at + n, :])


def on_device(
    x_input,
    mel_frames,
    sample_mask,
    clip_length_array,
    speaker_ids,
    cot_out,
    cot_skip,
    *states,
):
    parts = lax.axis_size("tm")
    held_rows, width = x_input.shape
    own, full = held_rows // 2, 2 * width
    wide = own + 2 * EDGE
    mel = mel_frames.shape[0]
    clips = clip_length_array.shape[0]
    hop = FIRST_DILATION // held_rows

    dil_shape = states[0].shape
    rows = dil_shape[2]
    views = (
        [dilated_view(s) for s in states[0:3]]
        + list(states[3:6])
        + [s.transpose(0, 2, 3, 1) for s in states[6:12]]
        + [s.transpose(0, 2, 1) for s in states[12:18]]
    )
    speakers = views[9].shape[-1]
    where, total = sections(rows)
    far = parts // NEAR
    taken = [views[k] for k in (0, 12, 15, 6, 9, 3)]
    packed_type = BF16 if rows % 32 == 0 else F32
    taken = [views[k] for k in (0, 12, 15, 6, 9, 3)]
    packed_type = BF16 if rows % 32 == 0 else F32
    taken.append(x_input)
    pack_one, pack_two, x_low = call(
        functools.partial(start_body, rows, mel, clips),
        (struct((total, 256), packed_type),) * 2 + (struct(x_input.shape, BF16),),
        *taken,
        scalars=(speaker_ids,),
        space=pl.ANY,
        grant=None,
        scratch=[pltpu.VMEM(v.shape, F32) for v in taken]
        + [pltpu.SemaphoreType.DMA((len(taken),))],
    )

    lag = shifted(x_low, "tm", hop)
    span = own + EDGE
    group_one, stacked = along_all(pack_one.astype(BF16), (lag,))
    group_two, stacked = along_all(pack_two.astype(BF16), (stacked,))
    kept, given = call(
        part_body,
        (struct((span, 4 * width)),) * 2,
        x_input,
        cot_out,
        cot_skip,
        lag,
        unread=(stacked,),
        scratch=[pltpu.VMEM(x_input.shape, F32)],
    )
    parts_one, relayed = near_exchange(group_one, (stacked,), LONG)
    parts_two, begun = near_exchange(group_two, (), LONG)
    joined_own = struct((own, 4 * full))
    edge = struct((EDGE, 4 * full + LANES))
    inner, side, near_edge, edge_sent = call(
        join_body,
        (joined_own, struct((own, LANES)), edge, edge),
        kept,
        swap_cores(given),
        mel_frames,
        sample_mask[None, :],
        unread=(relayed,),
        scratch=[pltpu.VMEM((span, 4 * full), F32), pltpu.VMEM((held_rows, LANES), F32)],
    )
    x_wide, cot_wide, skip_wide, lag_wide, cond, marks = call(
        functools.partial(widen_body, mel, clips),
        (
            struct((wide, full)),
            struct((wide, full)),
            struct((wide, full), BF16),
            struct((wide, full), BF16),
            struct((wide, LANES), BF16),
            struct((wide, LANES)),
        ),
        inner,
        side,
        near_edge,
        across_chips(edge_sent),
        scalars=(clip_length_array,),
        unread=(begun,),
    )
    w1_own, w1_oth = joined(parts_one, (marks,))

    half = struct((own, width))
    wave = struct((own, full))
    broad = struct((wide, full))
    low_half = struct((own, width), BF16)
    low_full = struct((own, full), BF16)
    packed = struct((BLOCKS, ROWS, 256), BF16)

    def forward(weights, *earlier, unread=(), flops=1024):
        return call(
            functools.partial(first_body, own),
            (broad, wave, low_full, half, half, low_half, TOKEN),
            x_wide,
            lag_wide,
            cond,
            marks,
            weights,
            *earlier,
            unread=unread,
            flops=flops,
        )

    res, skip, lag1, ta_own, sb_own, hid_own, _ = forward(w1_own, unread=(begun,), flops=LONG)
    u2, s1, _, ta_oth, sb_oth, hid_oth, token = forward(w1_oth, res, skip)

    w2_own, w2_oth = joined(parts_two, (token,))

    def middle(weights, *earlier):
        return call(
            functools.partial(second_body, own),
            (wave, wave, wave, TOKEN if earlier else broad, packed),
            u2,
            s1,
            cond,
            marks,
            cot_wide,
            skip_wide,
            weights,
            *earlier,
        )

    gate_two = call(
        second_forward_body, (struct((wide, width)),) * 2, u2, cond, marks, w2_own
    )
    *sums, grad_oth = middle(w2_oth)
    mixed, skip_total, g2, _, grad_own = middle(w2_own, *sums, *gate_two)

    def totals(terms, unread=()):
        return call(
            functools.partial(square_body, rows, mel, clips, speakers, len(terms)),
            (struct((total, 256)), struct((8, LANES))),
            *terms,
            scalars=(speaker_ids,),
            unread=unread,
        )

    def backward(weights, tanh_a, sig_b, hidden, *earlier, unread):
        last = bool(earlier)
        return call(
            functools.partial(third_body, own, last),
            (wave, low_full if last else TOKEN, TOKEN if last else wave, packed),
            g2,
            x_wide,
            lag1,
            cond,
            marks,
            skip_wide,
            tanh_a,
            sig_b,
            hidden,
            weights,
            *earlier,
            unread=unread,
        )

    grads2, sent2, token = cores_summed(grad_own, grad_oth)
    now, _, lag_sum, grad_oth = backward(w1_oth, ta_oth, sb_oth, hid_oth, unread=(token,))
    g1_part, dlag1, backed, grad_own = backward(
        w1_own, ta_own, sb_own, hid_own, now, lag_sum, unread=()
    )
    kept, given = call(
        divide_body,
        (struct((own, 4 * width)),) * 2,
        mixed,
        skip_total,
        g1_part,
        dlag1,
        scratch=[pltpu.VMEM((own, full), F32)],
    )
    mixed, skip_total, grad_input, push, token = call(
        finish_body, (struct((held_rows, width)),) * 4 + (TOKEN,), kept, swap_cores(given)
    )
    grads2, sent2, summed = near_summed(grads2, sent2, LONG, (backed,))
    grads1, sent1, _ = cores_summed(grad_own, grad_oth, (summed, token))
    last_got = across(sent2, 0)
    terms2, _ = far_terms(grads2, last_got, LONG)
    grads1, sent1, _ = near_summed(grads1, sent1, unread=(terms2[1], terms2[-1]))
    terms1, _ = far_terms(grads1, across(sent1, 0))
    sum2, squares2 = totals(terms2)
    push = call(push_body, struct((held_rows, width), BF16), push)
    push = shifted(push, "tm", -hop)
    sum1, squares1 = totals(terms1, (push,))
    squares = call(add_body, TOKEN, squares1, squares2)
    sent = call(spread_body, struct((parts, 1, LANES)), squares, swap_cores(squares))
    squares = lax.all_to_all(sent, "tm", split_axis=0, concat_axis=0, tiled=True)
    outs = [struct((1, 1)), struct((held_rows, width))]
    for view in views[0::3]:
        outs += [struct(view.shape)] * 4 + [struct(view.shape, BF16)]
    updated = call(
        functools.partial(update_body, rows, mel, clips),
        tuple(outs),
        sum1,
        sum2,
        squares.reshape(parts, LANES),
        *views,
        grad_input,
        push,
        scalars=(speaker_ids,),
    )
    grad_norm, grad_input = updated[0].reshape(()), updated[1]
    backs = (
        [lambda v: dilated_back(v, dil_shape), lambda v: v]
        + [lambda v: v.transpose(0, 3, 1, 2)] * 2
        + [lambda v: v.transpose(0, 2, 1)] * 2
    )
    new = [
        [back(v) for v in updated[2 + 5 * kind : 7 + 5 * kind]] for kind, back in enumerate(backs)
    ]
    return (
        mixed,
        skip_total,
        grad_input,
        grad_norm,
        *[group[0] for group in new],
        *[value for group in new for value in group[1:4]],
        *[group[4] for group in new],
    )


def solution(mesh):
    rows = P("tm", "mp")
    dil = P(None, None, "tm", None, "mp")
    bias = P(None, None, ("mp", "tm"))
    wide = P(None, None, None, ("mp", "tm"))
    square = P(None, "mp", "tm")
    kinds = (dil, bias, wide, wide, square, square)
    thrice = tuple(kind for kind in kinds for _ in range(3))
    return jax.shard_map(
        on_device,
        mesh=mesh,
        in_specs=(rows, P(None, "tm"), P("tm"), P(), P(), rows, rows) + thrice,
        out_specs=(rows, rows, rows, P()) + kinds + thrice + kinds,
        check_vma=False,
    )
```

```python
import functools

import jax
import jax.numpy as jnp
from jax import lax
from jax.experimental import pallas as pl
from jax.experimental.pallas import tpu as pltpu
from jax.sharding import PartitionSpec as P

FIRST_DILATION = 512
STEP = 10
ROOT_HALF = 0.7071067811865476
BETA_ONE = 0.9
BETA_TWO = 0.999
ADAM_EPS = 1e-08
LEARN_RATE = 0.07
DECAY = 0.01
CLIP_NORM = 1.0

F32 = jnp.float32
BF16 = jnp.bfloat16
LANES = 128
EDGE = 8
BLOCKS = 16
NEAR = 4
VMEM_BYTES = 26 * 1024 * 1024
BOTH = ("tm", "mp")


def struct(shape, dtype=F32):
    return jax.ShapeDtypeStruct(shape, dtype)


def call(body, out_shape, *operands, scalars=(), scratch=(), space=pltpu.VMEM, unread=(), flops=1024, grant=VMEM_BYTES):
    specs = [pl.BlockSpec(memory_space=pltpu.SMEM)] * len(scalars)
    specs += [pl.BlockSpec(memory_space=space)] * len(operands)
    specs += [pl.BlockSpec(memory_space=pl.ANY)] * len(unread)
    return pl.pallas_call(
        body,
        out_shape=out_shape,
        in_specs=specs,
        scratch_shapes=list(scratch),
        compiler_params=pltpu.CompilerParams(vmem_limit_bytes=grant),
        cost_estimate=pl.CostEstimate(flops=flops, bytes_accessed=1024, transcendentals=0),
    )(*scalars, *operands, *unread)


def dot(left, right):
    return jnp.dot(left, right, preferred_element_type=F32)


def dot_right(left, right):
    return lax.dot_general(left, right, (((1,), (1,)), ((), ())), preferred_element_type=F32)


def dot_left(left, right):
    return lax.dot_general(left, right, (((0,), (0,)), ((), ())), preferred_element_type=F32)


def place():
    index = lax.axis_index("tm")
    core = lax.axis_index("mp")
    return index // NEAR, index % NEAR, core, 1 + core, 2 - core


def route(target):
    return [
        (index * 2 + core, target(index, core) * 2 + core)
        for index in range(lax.axis_size("tm"))
        for core in range(2)
    ]


def across(value, bit):
    return lax.ppermute(value, BOTH, route(lambda i, c: i ^ (1 + (c ^ bit))))


def along_far(value, distance):
    far = lax.axis_size("tm") // NEAR
    return lax.ppermute(
        value, BOTH, route(lambda i, c: (i // NEAR + distance) % far * NEAR + i % NEAR)
    )


def swap_cores(value):
    return lax.ppermute(value, "mp", [(0, 1), (1, 0)])


def shifted(value, axis, distance):
    devices = range(lax.axis_size(axis))
    pairs = [(i - distance, i) for i in devices if i - distance in devices]
    return lax.ppermute(value, axis, pairs)


def across_chips(value):
    pairs = []
    for index in range(1, lax.axis_size("tm")):
        pairs += [(index * 2 - 1, index * 2), (index * 2, index * 2 - 1)]
    return lax.ppermute(value, BOTH, pairs)


def sections(rows):
    found, at = [], 0
    for count in (rows,) * 6 + (rows // 2,):
        found.append((at, count))
        at += count
    return found, at


WHERE, ROWS = sections(32)


def dilated_view(array):
    layers, taps, rows, halves, width = array.shape
    tiles = width // LANES
    split = array.reshape(layers, taps, rows, halves, tiles, LANES)
    return split.transpose(0, 1, 2, 4, 3, 5).reshape(-1, LANES)


def dilated_back(array, shape):
    layers, taps, rows, halves, width = shape
    tiles = width // LANES
    split = array.reshape(layers, taps, rows, tiles, halves, LANES)
    return split.transpose(0, 1, 2, 4, 3, 5).reshape(shape)


def strided(layer, tap, half, tile, rows):
    return pl.ds((layer * 2 + tap) * rows * 4 + tile * 2 + half, rows, stride=4)


def start_body(rows, mel, clips, who, *refs):
    sources, (out_one, out_two, low), held, sems = refs[:7], refs[7:10], refs[10:17], refs[17]
    copies = [
        pltpu.make_async_copy(source, target, sems.at[index])
        for index, (source, target) in enumerate(zip(sources, held))
    ]
    for copy in copies:
        copy.start()
    dil, res, skip, mel_w, table, bias, samples = held
    where, total = sections(rows)
    chans = rows // 2
    speakers = table.shape[-1]
    lane = lax.broadcasted_iota(jnp.int32, (1, speakers), 1)
    hot = jnp.concatenate([(lane == who[k]).astype(F32) for k in range(clips)], axis=0).astype(BF16)
    eye = lax.broadcasted_iota(jnp.int32, (chans, chans), 0) == lax.broadcasted_iota(
        jnp.int32, (chans, chans), 1
    )

    def write(out, at, count, columns, value):
        out[at : at + count, columns] = value.astype(out.dtype)

    for copy in copies[:-1]:
        copy.wait()
    for layer, out in enumerate((out_one, out_two)):
        for tap in range(2):
            for half in range(2):
                at, count = where[2 * tap + half]
                for tile in range(2):
                    part = dil[strided(layer, tap, half, tile, rows), :]
                    write(out, at, count, slice(tile * LANES, (tile + 1) * LANES), part)
        for kind, source in ((4, res), (5, skip)):
            at, count = where[kind]
            write(out, at, count, slice(None), source[layer])
        at, count = where[6]
        for half in range(2):
            picked = dot_right(table[layer, half].astype(BF16), hot)
            line = jnp.broadcast_to(bias[layer, half : half + 1, :], (chans, chans))
            column = jnp.sum(jnp.where(eye, line, 0.0), axis=1, keepdims=True)
            blank = jnp.zeros((chans, LANES - mel - clips - 1), F32)
            row = jnp.concatenate([mel_w[layer, half], picked, column, blank], axis=1)
            columns = slice(half * LANES, (half + 1) * LANES)
            write(out, at, count, columns, row.astype(BF16).astype(F32))
    copies[-1].wait()
    low[...] = samples[...].astype(BF16)


def assemble_body(group, first, second, last, *refs):
    out = refs[-1]
    count = group.shape[0]
    far, near, _, first_bit, second_bit = place()
    for ref, mask in ((group, 0), (first, first_bit), (second, second_bit), (last, 3)):
        for back in range(count):
            out[lax.rem(far + count - back, count) * NEAR + (near ^ mask)] = ref[back]


def relay_body(value, *refs):
    out, token = refs[-2:]
    out[...] = value[...]
    token[...] = jnp.zeros_like(token)


TOKEN = struct((8, LANES))
LONG = 20_000_000_000


def stack_body(count, *refs):
    out, token = refs[-2:]
    for index in range(count):
        out[index] = refs[index][...]
    token[...] = jnp.zeros_like(token)


def along_all(pack, unread):
    far = lax.axis_size("tm") // NEAR
    got = [along_far(pack, distance) for distance in range(1, far)]
    held, _ = call(relay_body, (struct(pack.shape, BF16), TOKEN), pack)
    return call(
        functools.partial(stack_body, far),
        (struct((far,) + pack.shape, BF16), TOKEN),
        held,
        *got,
        unread=unread,
    )


def near_exchange(group, before_last, flops=1024):
    first = across(group, 0)
    second = across(group, 1)
    passed, token = call(
        relay_body,
        (struct(first.shape, BF16), TOKEN),
        first,
        unread=(second,) + before_last,
        flops=flops,
    )
    return (group, first, second, across(passed, 1)), token


def joined(parts, before_end):
    count = NEAR * parts[0].shape[0]
    own = call(
        assemble_body, struct((count,) + parts[0].shape[1:], BF16), *parts, unread=before_end
    )
    if count != BLOCKS:
        own = to_canonical(own)
    return own, swap_cores(own)


def to_canonical(gathered):
    parts = gathered.shape[0]
    where, total = sections(BLOCKS * 32 // parts)
    return jnp.concatenate(
        [gathered[:, at : at + n, :].reshape(BLOCKS, -1, 256) for at, n in where], axis=1
    )


def from_canonical(packed, parts):
    where, total = sections(32)
    return jnp.concatenate(
        [packed[:, at : at + n, :].reshape(parts, -1, 256) for at, n in where], axis=1
    )


def piece(ref, kind):
    at, count = WHERE[kind]
    return ref[:, at : at + count, :].reshape(-1, 256)


def conditioning(ref, half):
    at, count = WHERE[6]
    return ref[:, at : at + count, half * LANES : (half + 1) * LANES].reshape(-1, LANES)


def slot(ordered, first, block):
    if not ordered:
        return block
    near = lax.axis_index("tm") % NEAR
    mask = (block % NEAR) ^ near
    group = jnp.where(mask == 3, 0, jnp.where(mask == 0, 3, jnp.where(mask == first, 2, 1)))
    return group * (BLOCKS // NEAR) + block // NEAR


def store(ref, slots, kind, value):
    at, count = WHERE[kind]
    value = value.astype(BF16)
    for block in range(BLOCKS):
        ref[slots[block], at : at + count, :] = value[block * count : (block + 1) * count]


def store_conditioning(ref, slots, half, value):
    at, count = WHERE[6]
    value = value.astype(BF16)
    for block in range(BLOCKS):
        ref[slots[block], at : at + count, half * LANES : (half + 1) * LANES] = value[
            block * count : (block + 1) * count
        ]


def order_body(own, other, own_out, other_out):
    parts = own.shape[0]
    far = parts // NEAR
    _, near, _, first, second = place()
    for source, out, bit, next_bit in (
        (own, own_out, first, second),
        (other, other_out, second, first),
    ):
        for group, mask in enumerate((3, next_bit, bit, 0)):
            for index in range(far):
                out[group * far + index] = source[index * NEAR + (near ^ mask)]


def first_sum_body(own, got, *refs):
    out, token = refs[-2:]
    half = out.shape[0]
    out[...] = own[:half] + got[:half]
    token[...] = jnp.zeros_like(token)


def second_sum_body(own, got, near_got, *refs):
    out, token = refs[-2:]
    count = out.shape[0]
    kept = slice(2 * count, 3 * count)
    out[...] = (
        own[kept].astype(F32) + got[kept].astype(F32) + near_got[:count].astype(F32)
    ).astype(BF16)
    token[...] = jnp.zeros_like(token)


def third_sum_body(own, got, near_got, last_got, *refs):
    far = place()[0]
    count = last_got.shape[0]
    token = refs[-1]
    token[...] = jnp.zeros_like(token)
    for distance, out in enumerate(refs[-count - 1 : -1]):
        index = lax.rem(far + distance, count)
        out[...] = (
            own[3 * count + index].astype(F32)
            + got[3 * count + index].astype(F32)
            + near_got[count + index].astype(F32)
            + last_got[index].astype(F32)
        ).astype(out.dtype)


def ordered(grads):
    parts = lax.axis_size("tm")
    return grads if parts == BLOCKS else from_canonical(grads, parts)


def cores_summed(own, other, unread=()):
    own, other = ordered(own), ordered(other)
    if own.shape[0] != BLOCKS:
        own, other = call(order_body, (struct(own.shape, BF16),) * 2, own, other)
    got = swap_cores(other)
    half = struct((own.shape[0] // 2,) + own.shape[1:], BF16)
    sent, token = call(first_sum_body, (half, TOKEN), own, got, unread=unread)
    return (own, got), sent, token


def near_summed(grads, sent, flops=1024, unread=()):
    near_got = across(sent, 1)
    shape = (grads[0].shape[0] // NEAR,) + grads[0].shape[1:]
    sent, token = call(
        second_sum_body,
        (struct(shape, BF16), TOKEN),
        *grads,
        near_got,
        flops=flops,
        unread=unread,
    )
    return grads + (near_got,), sent, token


def far_terms(grads, last_got, flops=1024, unread=()):
    far, *shape = last_got.shape
    kept, *sends, token = call(
        third_sum_body,
        (struct(shape),) + (struct(shape, BF16),) * (far - 1) + (TOKEN,),
        *grads,
        last_got,
        flops=flops,
        unread=unread,
    )
    return [kept] + [along_far(value, k + 1) for k, value in enumerate(sends)], token


def gates(weights, lag, xin, cond):
    za = dot(lag, piece(weights, 0)) + dot(xin, piece(weights, 2))
    za = za + dot_right(cond, conditioning(weights, 0))
    zb = dot(lag, piece(weights, 1)) + dot(xin, piece(weights, 3))
    zb = zb + dot_right(cond, conditioning(weights, 1))
    return jnp.tanh(za), jax.nn.sigmoid(zb)


def gate_gradients(weights, res_grad, skip_grad, keep, tanh_a, sig_b):
    hidden_grad = dot(res_grad, piece(weights, 4)) + dot(skip_grad, piece(weights, 5))
    hidden_grad = hidden_grad * keep
    grad_a = (hidden_grad * sig_b * (1.0 - tanh_a * tanh_a)).astype(BF16)
    grad_b = (hidden_grad * tanh_a * sig_b * (1.0 - sig_b)).astype(BF16)
    return grad_a, grad_b


def weight_gradients(out, bit, lag, xin, cond, grad_a, grad_b, res_grad, skip_grad, hidden):
    slots = [slot(lax.axis_size("tm") == BLOCKS, bit, block) for block in range(BLOCKS)]
    store(out, slots, 0, dot_left(lag, grad_a))
    store(out, slots, 1, dot_left(lag, grad_b))
    store(out, slots, 2, dot_left(xin, grad_a))
    store(out, slots, 3, dot_left(xin, grad_b))
    store(out, slots, 4, dot_left(res_grad, hidden))
    store(out, slots, 5, dot_left(skip_grad, hidden))
    store_conditioning(out, slots, 0, dot_left(grad_a, cond))
    store_conditioning(out, slots, 1, dot_left(grad_b, cond))


def first_body(own, x, lag_raw, cond, marks, weights, *refs):
    earlier, (u2, s1, lag_out, ta, sb, hid, token) = refs[:-7], refs[-7:]
    token[...] = jnp.zeros_like(token)
    keep = marks[:, 0:1]
    xin = x[...].astype(BF16)
    lag = (lag_raw[...].astype(F32) * marks[:, 1:2]).astype(BF16)
    tanh_a, sig_b = gates(weights, lag, xin, cond[...])
    hidden = (keep * tanh_a * sig_b).astype(BF16)
    res = dot_right(hidden, piece(weights, 4))
    skip = dot_right(hidden[:own], piece(weights, 5))
    ta[...] = tanh_a[:own]
    sb[...] = sig_b[:own]
    hid[...] = hidden[:own]
    lag_out[...] = lag[:own]
    if len(earlier) == 2:
        u2[...] = (x[...] + (earlier[0][...] + res)) * ROOT_HALF
        s1[...] = earlier[1][...] + skip
    else:
        u2[...] = res
        s1[...] = skip


def second_input(u2, marks):
    xin = u2[...].astype(BF16)
    lag = (pltpu.roll(xin.astype(F32), 1, 0) * marks[:, 2:3]).astype(BF16)
    return xin, lag


def second_forward_body(u2, cond, marks, weights, ta, sb):
    xin, lag = second_input(u2, marks)
    ta[...], sb[...] = gates(weights, lag, xin, cond[...])


def second_body(own, u2, s1, cond, marks, cot, cot_skip, weights, *refs):
    last = len(refs) > 5
    earlier, (mixed, total, g2, lag_sum, grads) = refs[:-5], refs[-5:]
    rows = u2.shape[0]
    keep = marks[:, 0:1]
    xin, lag = second_input(u2, marks)
    res_grad = (cot[...] * ROOT_HALF).astype(BF16)
    skip_grad = cot_skip[...]
    if last:
        tanh_a, sig_b = earlier[4][...], earlier[5][...]
    else:
        tanh_a, sig_b = gates(weights, lag, xin, cond[...])
    hidden = (keep * tanh_a * sig_b).astype(BF16)[:own]
    grad_a, grad_b = gate_gradients(weights, res_grad, skip_grad, keep, tanh_a, sig_b)
    _, _, _, first_bit, second_bit = place()
    weight_gradients(
        grads,
        first_bit if last else second_bit,
        lag[:own],
        xin[:own],
        cond[:own, :],
        grad_a[:own],
        grad_b[:own],
        res_grad[:own],
        skip_grad[:own],
        hidden,
    )
    res = dot_right(hidden, piece(weights, 4))
    skip = dot_right(hidden, piece(weights, 5))
    lag_grad = dot_right(grad_a, piece(weights, 0)) + dot_right(grad_b, piece(weights, 1))
    now = dot_right(grad_a[:own], piece(weights, 2)) + dot_right(grad_b[:own], piece(weights, 3))
    if last:
        res, skip, now, lag_grad = (
            before[...] + value for before, value in zip(earlier, (res, skip, now, lag_grad))
        )
        mixed[...] = (u2[:own, :] + res) * ROOT_HALF
        total[...] = s1[...] + skip
        pushed = (lag_grad * marks[:, 2:3]).astype(BF16).astype(F32)
        g2[...] = cot[:own, :] * ROOT_HALF + now + pltpu.roll(pushed, rows - 1, 0)[:own]
    else:
        mixed[...] = res
        total[...] = skip
        g2[...] = now
        lag_sum[...] = lag_grad


def third_body(own, last, g2, x, lag, cond, marks, cot_skip, ta, sb, hid, weights, *refs):
    earlier, (g1, dlag, lag_sum, grads) = refs[:-4], refs[-4:]
    keep = marks[:own, 0:1]
    xin = x[:own, :].astype(BF16)
    res_grad = (g2[...] * ROOT_HALF).astype(BF16)
    skip_grad = cot_skip[:own, :]
    grad_a, grad_b = gate_gradients(weights, res_grad, skip_grad, keep, ta[...], sb[...])
    _, _, _, first_bit, second_bit = place()
    weight_gradients(
        grads,
        first_bit if last else second_bit,
        lag[...],
        xin,
        cond[:own, :],
        grad_a,
        grad_b,
        res_grad,
        skip_grad,
        hid[...],
    )
    lag_grad = dot_right(grad_a, piece(weights, 0)) + dot_right(grad_b, piece(weights, 1))
    now = dot_right(grad_a, piece(weights, 2)) + dot_right(grad_b, piece(weights, 3))
    if last:
        lag_sum[...] = jnp.zeros_like(lag_sum)
        g1[...] = g2[...] * ROOT_HALF + (earlier[0][...] + now)
        dlag[...] = ((earlier[1][...] + lag_grad) * marks[:own, 1:2]).astype(BF16)
    else:
        g1[...] = now
        lag_sum[...] = lag_grad


def part_body(x, cot, skip, lag, *refs):
    core = place()[2]
    kept, given, held = refs[-3:]
    span, width = kept.shape[0], x.shape[1]
    beyond = x.shape[0] - span
    held[...] = lag[...].astype(F32)
    for index, ref in enumerate((x, cot, skip, held)):
        columns = slice(index * width, (index + 1) * width)
        kept[:, columns] = ref[pl.ds(core * beyond, span), :]
        given[:, columns] = ref[pl.ds((1 - core) * beyond, span), :]


def join_body(kept, got, mel, mask, *refs):
    core = place()[2]
    inner, side, near_edge, edge_sent, held, lines = refs[-6:]
    span, width = kept.shape[0], kept.shape[1] // 4
    own, beyond = inner.shape[0], mel.shape[1] - span
    for index in range(4):
        for source, at in ((kept, core), (got, 1 - core)):
            held[:, pl.ds(index * 2 * width + at * width, width)] = source[
                :, index * width : (index + 1) * width
            ]
    blank = jnp.zeros((LANES - mel.shape[0] - 1, mel.shape[1]), F32)
    lines[...] = jnp.concatenate([mel[...], mask[...].astype(F32), blank], axis=0).T
    inner[...] = held[pl.ds(core * EDGE, own), :]
    side[...] = lines[pl.ds(core * own, own), :]
    for ref, at in ((near_edge, (1 - core) * own), (edge_sent, core * own)):
        ref[:, LANES:] = held[pl.ds(at, EDGE), :]
        ref[:, :LANES] = lines[pl.ds(core * beyond + at, EDGE), :]


def widen_body(
    mel, clips, lengths, inner, side, near_edge, edge, *refs
):
    far, near, core = place()[:3]
    x_out, cot_out, skip_out, lag_out, cond, marks = refs[-6:]
    own, full = inner.shape[0], inner.shape[1] // 4
    wide = own + 2 * EDGE
    after = jnp.where(core == 0, near_edge[...], edge[...])
    before = jnp.where(core == 0, edge[...], near_edge[...])
    for index, ref in enumerate((x_out, cot_out, skip_out, lag_out)):
        at = LANES + index * full
        ref[...] = jnp.concatenate(
            [
                inner[:, index * full : (index + 1) * full],
                after[:, at : at + full],
                before[:, at : at + full],
            ],
            axis=0,
        ).astype(ref.dtype)
    side_wide = jnp.concatenate([side[...], after[:, :LANES], before[:, :LANES]], axis=0)
    lane = lax.broadcasted_iota(jnp.int32, (wide, LANES), 1)
    line = lax.broadcasted_iota(jnp.int32, (wide, LANES), 0)
    first = ((far * NEAR + near) * 2 + core) * own
    position = first + jnp.where(line < own + EDGE, line, line - wide)

    def segment(at):
        total = jnp.zeros((wide, LANES), jnp.int32)
        end = jnp.int32(0)
        for clip in range(clips):
            end = end + lengths[clip]
            total = total + (at >= end).astype(jnp.int32)
        return total

    here = segment(position)

    def valid(span):
        return ((position >= span) & (segment(position - span) == here)).astype(F32)

    hot = ((lane - mel) == here).astype(F32)
    value = jnp.where(lane < mel, side_wide, jnp.where(lane < mel + clips, hot, 0.0))
    cond[...] = jnp.where(lane == mel + clips, 1.0, value).astype(BF16)
    keep = side_wide[:, mel : mel + 1]
    marks[...] = jnp.where(
        lane == 0, keep, jnp.where(lane == 1, valid(FIRST_DILATION), valid(1))
    )


def divide_body(mixed, total, g1, push, *refs):
    core = place()[2]
    kept, given, held = refs[-3:]
    width = kept.shape[1] // 4
    held[...] = push[...].astype(F32)
    for index, ref in enumerate((mixed, total, g1, held)):
        columns = slice(index * width, (index + 1) * width)
        kept[:, columns] = ref[:, pl.ds(core * width, width)]
        given[:, columns] = ref[:, pl.ds((1 - core) * width, width)]


def finish_body(kept, got, *refs):
    core = place()[2]
    outs, token = refs[:-1], refs[-1]
    token[...] = jnp.zeros_like(token)
    own, width = kept.shape[0], kept.shape[1] // 4
    for index, ref in enumerate(outs):
        for source, at in ((kept, core), (got, 1 - core)):
            ref[pl.ds(at * own, own), :] = source[:, index * width : (index + 1) * width]


def push_body(push, *refs):
    refs[-1][...] = push[...].astype(BF16)


def table_gradient(cond_grad, who, mel, clips, speakers):
    lane = lax.broadcasted_iota(jnp.int32, (cond_grad.shape[0], speakers), 1)
    result = jnp.zeros((cond_grad.shape[0], speakers), F32)
    for clip in range(clips):
        column = cond_grad[:, mel + clip : mel + clip + 1]
        result = result + jnp.where(lane == who[clip], column, 0.0)
    return result


def square_body(rows, mel, clips, speakers, count, who, *refs):
    terms, (out, squares) = refs[:count], refs[-2:]
    where, total = sections(rows)
    start = where[6][0]
    value = terms[0][...]
    for term in terms[1:]:
        value = value + term[...].astype(F32)
    out[...] = value
    main = out[:start, :]
    amount = jnp.sum(main * main, keepdims=True)
    for half in range(2):
        block = out[start:, half * LANES : (half + 1) * LANES]
        lane = lax.broadcasted_iota(jnp.int32, block.shape, 1)
        plain = jnp.where((lane < mel) | (lane == mel + clips), block, 0.0)
        amount = amount + jnp.sum(plain * plain, keepdims=True)
        table = table_gradient(block, who, mel, clips, speakers)
        amount = amount + jnp.sum(table * table, keepdims=True)
    squares[...] = jnp.broadcast_to(amount, squares.shape)


def add_body(left, right, out):
    out[...] = left[...] + right[...]


def spread_body(left, right, out):
    total = left[0:1, :] + right[0:1, :]
    out[...] = jnp.broadcast_to(total[None], out.shape)


def adamw(weight, mean, square, gradient, scale):
    clipped = gradient * scale
    new_mean = BETA_ONE * mean + (1.0 - BETA_ONE) * clipped
    new_square = BETA_TWO * square + (1.0 - BETA_TWO) * clipped * clipped
    fix_one = 1.0 - BETA_ONE**STEP
    fix_two = 1.0 - BETA_TWO**STEP
    update = new_mean / fix_one / (jnp.sqrt(new_square / fix_two) + ADAM_EPS)
    return weight - LEARN_RATE * (update + DECAY * weight), new_mean, new_square


def update_body(rows, mel, clips, who, *refs):
    grads = refs[0:2]
    squares = refs[2]
    old = [refs[3 + 3 * kind : 6 + 3 * kind] for kind in range(6)]
    part, push, norm, grad_input = refs[21:25]
    new = [refs[25 + 5 * kind : 30 + 5 * kind] for kind in range(6)]
    grad_input[...] = part[...] + push[...].astype(F32)
    where, total = sections(rows)
    chans = rows // 2
    grad_norm = jnp.sqrt(jnp.sum(squares[...], axis=0, keepdims=True)[:, 0:1])
    norm[...] = grad_norm
    scale = jnp.minimum(1.0, CLIP_NORM / grad_norm)

    def write(kind, index, gradient):
        weight, mean, square = (ref[index] for ref in old[kind])
        new_weight, new_mean, new_square = adamw(weight, mean, square, gradient, scale)
        for ref, value in zip(
            new[kind],
            (gradient, new_weight, new_mean, new_square, new_weight.astype(BF16)),
        ):
            ref[index] = value

    dil = new[0][0]
    for layer in range(2):
        for tap in range(2):
            for half in range(2):
                at, n = where[2 * tap + half]
                for tile in range(2):
                    dil[strided(layer, tap, half, tile, rows), :] = grads[layer][
                        at : at + n, tile * LANES : (tile + 1) * LANES
                    ]
    weight, mean, square = (ref[...] for ref in old[0])
    new_weight, new_mean, new_square = adamw(weight, mean, square, dil[...], scale)
    new[0][1][...] = new_weight
    new[0][2][...] = new_mean
    new[0][3][...] = new_square
    new[0][4][...] = new_weight.astype(BF16)
    for layer in range(2):
        for half in range(2):
            block = grads[layer][where[6][0] :, half * LANES : (half + 1) * LANES]
            eye = lax.broadcasted_iota(jnp.int32, (chans, chans), 0) == lax.broadcasted_iota(
                jnp.int32, (chans, chans), 1
            )
            column = block[:, mel + clips : mel + clips + 1]
            line = jnp.sum(jnp.where(eye, column, 0.0), axis=0, keepdims=True)
            write(1, (layer, slice(half, half + 1), slice(None)), line)
            write(2, (layer, half), block[:, :mel])
            speakers = old[3][0].shape[-1]
            write(3, (layer, half), table_gradient(block, who, mel, clips, speakers))
        for kind, section in ((4, 4), (5, 5)):
            at, n = where[section]
            write(kind, (layer,), grads[layer][at : at + n, :])


def on_device(
    x_input,
    mel_frames,
    sample_mask,
    clip_length_array,
    speaker_ids,
    cot_out,
    cot_skip,
    *states,
):
    parts = lax.axis_size("tm")
    held_rows, width = x_input.shape
    own, full = held_rows // 2, 2 * width
    wide = own + 2 * EDGE
    mel = mel_frames.shape[0]
    clips = clip_length_array.shape[0]
    hop = FIRST_DILATION // held_rows

    dil_shape = states[0].shape
    rows = dil_shape[2]
    views = (
        [dilated_view(s) for s in states[0:3]]
        + list(states[3:6])
        + [s.transpose(0, 2, 3, 1) for s in states[6:12]]
        + [s.transpose(0, 2, 1) for s in states[12:18]]
    )
    speakers = views[9].shape[-1]
    where, total = sections(rows)
    far = parts // NEAR
    taken = [views[k] for k in (0, 12, 15, 6, 9, 3)]
    packed_type = BF16 if rows % 32 == 0 else F32
    taken = [views[k] for k in (0, 12, 15, 6, 9, 3)]
    packed_type = BF16 if rows % 32 == 0 else F32
    taken.append(x_input)
    pack_one, pack_two, x_low = call(
        functools.partial(start_body, rows, mel, clips),
        (struct((total, 256), packed_type),) * 2 + (struct(x_input.shape, BF16),),
        *taken,
        scalars=(speaker_ids,),
        space=pl.ANY,
        grant=None,
        scratch=[pltpu.VMEM(v.shape, F32) for v in taken]
        + [pltpu.SemaphoreType.DMA((len(taken),))],
    )

    lag = shifted(x_low, "tm", hop)
    span = own + EDGE
    group_one, stacked = along_all(pack_one.astype(BF16), (lag,))
    group_two, stacked = along_all(pack_two.astype(BF16), (stacked,))
    kept, given = call(
        part_body,
        (struct((span, 4 * width)),) * 2,
        x_input,
        cot_out,
        cot_skip,
        lag,
        unread=(stacked,),
        scratch=[pltpu.VMEM(x_input.shape, F32)],
    )
    parts_one, relayed = near_exchange(group_one, (stacked,), LONG)
    parts_two, begun = near_exchange(group_two, (), LONG)
    joined_own = struct((own, 4 * full))
    edge = struct((EDGE, 4 * full + LANES))
    inner, side, near_edge, edge_sent = call(
        join_body,
        (joined_own, struct((own, LANES)), edge, edge),
        kept,
        swap_cores(given),
        mel_frames,
        sample_mask[None, :],
        unread=(relayed,),
        scratch=[pltpu.VMEM((span, 4 * full), F32), pltpu.VMEM((held_rows, LANES), F32)],
    )
    x_wide, cot_wide, skip_wide, lag_wide, cond, marks = call(
        functools.partial(widen_body, mel, clips),
        (
            struct((wide, full)),
            struct((wide, full)),
            struct((wide, full), BF16),
            struct((wide, full), BF16),
            struct((wide, LANES), BF16),
            struct((wide, LANES)),
        ),
        inner,
        side,
        near_edge,
        across_chips(edge_sent),
        scalars=(clip_length_array,),
        unread=(begun,),
    )
    w1_own, w1_oth = joined(parts_one, (marks,))

    half = struct((own, width))
    wave = struct((own, full))
    broad = struct((wide, full))
    low_half = struct((own, width), BF16)
    low_full = struct((own, full), BF16)
    packed = struct((BLOCKS, ROWS, 256), BF16)

    def forward(weights, *earlier, unread=(), flops=1024):
        return call(
            functools.partial(first_body, own),
            (broad, wave, low_full, half, half, low_half, TOKEN),
            x_wide,
            lag_wide,
            cond,
            marks,
            weights,
            *earlier,
            unread=unread,
            flops=flops,
        )

    res, skip, lag1, ta_own, sb_own, hid_own, _ = forward(w1_own, unread=(begun,), flops=LONG)
    u2, s1, _, ta_oth, sb_oth, hid_oth, token = forward(w1_oth, res, skip)

    w2_own, w2_oth = joined(parts_two, (token,))

    def middle(weights, *earlier):
        return call(
            functools.partial(second_body, own),
            (wave, wave, wave, TOKEN if earlier else broad, packed),
            u2,
            s1,
            cond,
            marks,
            cot_wide,
            skip_wide,
            weights,
            *earlier,
        )

    gate_two = call(
        second_forward_body, (struct((wide, width)),) * 2, u2, cond, marks, w2_own
    )
    *sums, grad_oth = middle(w2_oth)
    mixed, skip_total, g2, _, grad_own = middle(w2_own, *sums, *gate_two)

    def totals(terms, unread=()):
        return call(
            functools.partial(square_body, rows, mel, clips, speakers, len(terms)),
            (struct((total, 256)), struct((8, LANES))),
            *terms,
            scalars=(speaker_ids,),
            unread=unread,
        )

    def backward(weights, tanh_a, sig_b, hidden, *earlier, unread):
        last = bool(earlier)
        return call(
            functools.partial(third_body, own, last),
            (wave, low_full if last else TOKEN, TOKEN if last else wave, packed),
            g2,
            x_wide,
            lag1,
            cond,
            marks,
            skip_wide,
            tanh_a,
            sig_b,
            hidden,
            weights,
            *earlier,
            unread=unread,
        )

    grads2, sent2, token = cores_summed(grad_own, grad_oth)
    now, _, lag_sum, grad_oth = backward(w1_oth, ta_oth, sb_oth, hid_oth, unread=(token,))
    g1_part, dlag1, backed, grad_own = backward(
        w1_own, ta_own, sb_own, hid_own, now, lag_sum, unread=()
    )
    kept, given = call(
        divide_body,
        (struct((own, 4 * width)),) * 2,
        mixed,
        skip_total,
        g1_part,
        dlag1,
        scratch=[pltpu.VMEM((own, full), F32)],
    )
    mixed, skip_total, grad_input, push, token = call(
        finish_body, (struct((held_rows, width)),) * 4 + (TOKEN,), kept, swap_cores(given)
    )
    grads2, sent2, summed = near_summed(grads2, sent2, LONG, (backed,))
    grads1, sent1, _ = cores_summed(grad_own, grad_oth, (summed, token))
    last_got = across(sent2, 0)
    terms2, _ = far_terms(grads2, last_got, LONG)
    grads1, sent1, _ = near_summed(grads1, sent1, unread=(terms2[1], terms2[-1]))
    terms1, _ = far_terms(grads1, across(sent1, 0))
    sum2, squares2 = totals(terms2)
    sum1, squares1 = totals(terms1)
    squares = call(add_body, TOKEN, squares1, squares2)
    sent = call(spread_body, struct((parts, 1, LANES)), squares, swap_cores(squares))
    push = call(push_body, struct((held_rows, width), BF16), push, unread=(sent,))
    push = shifted(push, "tm", -hop)
    squares = lax.all_to_all(sent, "tm", split_axis=0, concat_axis=0, tiled=True)
    outs = [struct((1, 1)), struct((held_rows, width))]
    for view in views[0::3]:
        outs += [struct(view.shape)] * 4 + [struct(view.shape, BF16)]
    updated = call(
        functools.partial(update_body, rows, mel, clips),
        tuple(outs),
        sum1,
        sum2,
        squares.reshape(parts, LANES),
        *views,
        grad_input,
        push,
        scalars=(speaker_ids,),
    )
    grad_norm, grad_input = updated[0].reshape(()), updated[1]
    backs = (
        [lambda v: dilated_back(v, dil_shape), lambda v: v]
        + [lambda v: v.transpose(0, 3, 1, 2)] * 2
        + [lambda v: v.transpose(0, 2, 1)] * 2
    )
    new = [
        [back(v) for v in updated[2 + 5 * kind : 7 + 5 * kind]] for kind, back in enumerate(backs)
    ]
    return (
        mixed,
        skip_total,
        grad_input,
        grad_norm,
        *[group[0] for group in new],
        *[value for group in new for value in group[1:4]],
        *[group[4] for group in new],
    )


def solution(mesh):
    rows = P("tm", "mp")
    dil = P(None, None, "tm", None, "mp")
    bias = P(None, None, ("mp", "tm"))
    wide = P(None, None, None, ("mp", "tm"))
    square = P(None, "mp", "tm")
    kinds = (dil, bias, wide, wide, square, square)
    thrice = tuple(kind for kind in kinds for _ in range(3))
    return jax.shard_map(
        on_device,
        mesh=mesh,
        in_specs=(rows, P(None, "tm"), P("tm"), P(), P(), rows, rows) + thrice,
        out_specs=(rows, rows, rows, P()) + kinds + thrice + kinds,
        check_vma=False,
    )
```

```python
import functools

import jax
import jax.numpy as jnp
from jax import lax
from jax.experimental import pallas as pl
from jax.experimental.pallas import tpu as pltpu
from jax.sharding import PartitionSpec as P

FIRST_DILATION = 512
STEP = 10
ROOT_HALF = 0.7071067811865476
BETA_ONE = 0.9
BETA_TWO = 0.999
ADAM_EPS = 1e-08
LEARN_RATE = 0.07
DECAY = 0.01
CLIP_NORM = 1.0

F32 = jnp.float32
BF16 = jnp.bfloat16
LANES = 128
EDGE = 8
BLOCKS = 16
NEAR = 4
VMEM_BYTES = 26 * 1024 * 1024
BOTH = ("tm", "mp")


def struct(shape, dtype=F32):
    return jax.ShapeDtypeStruct(shape, dtype)


def call(body, out_shape, *operands, scalars=(), scratch=(), space=pltpu.VMEM, unread=(), flops=1024, grant=VMEM_BYTES):
    specs = [pl.BlockSpec(memory_space=pltpu.SMEM)] * len(scalars)
    specs += [pl.BlockSpec(memory_space=space)] * len(operands)
    specs += [pl.BlockSpec(memory_space=pl.ANY)] * len(unread)
    return pl.pallas_call(
        body,
        out_shape=out_shape,
        in_specs=specs,
        scratch_shapes=list(scratch),
        compiler_params=pltpu.CompilerParams(vmem_limit_bytes=grant),
        cost_estimate=pl.CostEstimate(flops=flops, bytes_accessed=1024, transcendentals=0),
    )(*scalars, *operands, *unread)


def dot(left, right):
    return jnp.dot(left, right, preferred_element_type=F32)


def dot_right(left, right):
    return lax.dot_general(left, right, (((1,), (1,)), ((), ())), preferred_element_type=F32)


def dot_left(left, right):
    return lax.dot_general(left, right, (((0,), (0,)), ((), ())), preferred_element_type=F32)


def place():
    index = lax.axis_index("tm")
    core = lax.axis_index("mp")
    return index // NEAR, index % NEAR, core, 1 + core, 2 - core


def route(target):
    return [
        (index * 2 + core, target(index, core) * 2 + core)
        for index in range(lax.axis_size("tm"))
        for core in range(2)
    ]


def across(value, bit):
    return lax.ppermute(value, BOTH, route(lambda i, c: i ^ (1 + (c ^ bit))))


def along_far(value, distance):
    far = lax.axis_size("tm") // NEAR
    return lax.ppermute(
        value, BOTH, route(lambda i, c: (i // NEAR + distance) % far * NEAR + i % NEAR)
    )


def swap_cores(value):
    return lax.ppermute(value, "mp", [(0, 1), (1, 0)])


def shifted(value, axis, distance):
    devices = range(lax.axis_size(axis))
    pairs = [(i - distance, i) for i in devices if i - distance in devices]
    return lax.ppermute(value, axis, pairs)


def across_chips(value):
    pairs = []
    for index in range(1, lax.axis_size("tm")):
        pairs += [(index * 2 - 1, index * 2), (index * 2, index * 2 - 1)]
    return lax.ppermute(value, BOTH, pairs)


def sections(rows):
    found, at = [], 0
    for count in (rows,) * 6 + (rows // 2,):
        found.append((at, count))
        at += count
    return found, at


WHERE, ROWS = sections(32)


def dilated_view(array):
    layers, taps, rows, halves, width = array.shape
    tiles = width // LANES
    split = array.reshape(layers, taps, rows, halves, tiles, LANES)
    return split.transpose(0, 1, 2, 4, 3, 5).reshape(-1, LANES)


def dilated_back(array, shape):
    layers, taps, rows, halves, width = shape
    tiles = width // LANES
    split = array.reshape(layers, taps, rows, tiles, halves, LANES)
    return split.transpose(0, 1, 2, 4, 3, 5).reshape(shape)


def strided(layer, tap, half, tile, rows):
    return pl.ds((layer * 2 + tap) * rows * 4 + tile * 2 + half, rows, stride=4)


def start_body(rows, mel, clips, who, *refs):
    sources, (out_one, out_two, low), held, sems = refs[:7], refs[7:10], refs[10:17], refs[17]
    copies = [
        pltpu.make_async_copy(source, target, sems.at[index])
        for index, (source, target) in enumerate(zip(sources, held))
    ]
    for copy in copies:
        copy.start()
    dil, res, skip, mel_w, table, bias, samples = held
    where, total = sections(rows)
    chans = rows // 2
    speakers = table.shape[-1]
    lane = lax.broadcasted_iota(jnp.int32, (1, speakers), 1)
    hot = jnp.concatenate([(lane == who[k]).astype(F32) for k in range(clips)], axis=0).astype(BF16)
    eye = lax.broadcasted_iota(jnp.int32, (chans, chans), 0) == lax.broadcasted_iota(
        jnp.int32, (chans, chans), 1
    )

    def write(out, at, count, columns, value):
        out[at : at + count, columns] = value.astype(out.dtype)

    for copy in copies[:-1]:
        copy.wait()
    for layer, out in enumerate((out_one, out_two)):
        for tap in range(2):
            for half in range(2):
                at, count = where[2 * tap + half]
                for tile in range(2):
                    part = dil[strided(layer, tap, half, tile, rows), :]
                    write(out, at, count, slice(tile * LANES, (tile + 1) * LANES), part)
        for kind, source in ((4, res), (5, skip)):
            at, count = where[kind]
            write(out, at, count, slice(None), source[layer])
        at, count = where[6]
        for half in range(2):
            picked = dot_right(table[layer, half].astype(BF16), hot)
            line = jnp.broadcast_to(bias[layer, half : half + 1, :], (chans, chans))
            column = jnp.sum(jnp.where(eye, line, 0.0), axis=1, keepdims=True)
            blank = jnp.zeros((chans, LANES - mel - clips - 1), F32)
            row = jnp.concatenate([mel_w[layer, half], picked, column, blank], axis=1)
            columns = slice(half * LANES, (half + 1) * LANES)
            write(out, at, count, columns, row.astype(BF16).astype(F32))
    copies[-1].wait()
    low[...] = samples[...].astype(BF16)


def assemble_body(group, first, second, last, *refs):
    out = refs[-1]
    count = group.shape[0]
    far, near, _, first_bit, second_bit = place()
    for ref, mask in ((group, 0), (first, first_bit), (second, second_bit), (last, 3)):
        for back in range(count):
            out[lax.rem(far + count - back, count) * NEAR + (near ^ mask)] = ref[back]


def relay_body(value, *refs):
    out, token = refs[-2:]
    out[...] = value[...]
    token[...] = jnp.zeros_like(token)


TOKEN = struct((8, LANES))
LONG = 20_000_000_000


def stack_body(count, *refs):
    out, token = refs[-2:]
    for index in range(count):
        out[index] = refs[index][...]
    token[...] = jnp.zeros_like(token)


def along_all(pack, unread):
    far = lax.axis_size("tm") // NEAR
    got = [along_far(pack, distance) for distance in range(1, far)]
    held, _ = call(relay_body, (struct(pack.shape, BF16), TOKEN), pack)
    return call(
        functools.partial(stack_body, far),
        (struct((far,) + pack.shape, BF16), TOKEN),
        held,
        *got,
        unread=unread,
    )


def near_exchange(group, before_last, flops=1024):
    first = across(group, 0)
    second = across(group, 1)
    passed, token = call(
        relay_body,
        (struct(first.shape, BF16), TOKEN),
        first,
        unread=(second,) + before_last,
        flops=flops,
    )
    return (group, first, second, across(passed, 1)), token


def joined(parts, before_end):
    count = NEAR * parts[0].shape[0]
    own = call(
        assemble_body, struct((count,) + parts[0].shape[1:], BF16), *parts, unread=before_end
    )
    if count != BLOCKS:
        own = to_canonical(own)
    return own, swap_cores(own)


def to_canonical(gathered):
    parts = gathered.shape[0]
    where, total = sections(BLOCKS * 32 // parts)
    return jnp.concatenate(
        [gathered[:, at : at + n, :].reshape(BLOCKS, -1, 256) for at, n in where], axis=1
    )


def from_canonical(packed, parts):
    where, total = sections(32)
    return jnp.concatenate(
        [packed[:, at : at + n, :].reshape(parts, -1, 256) for at, n in where], axis=1
    )


def piece(ref, kind):
    at, count = WHERE[kind]
    return ref[:, at : at + count, :].reshape(-1, 256)


def conditioning(ref, half):
    at, count = WHERE[6]
    return ref[:, at : at + count, half * LANES : (half + 1) * LANES].reshape(-1, LANES)


def slot(ordered, first, block):
    if not ordered:
        return block
    near = lax.axis_index("tm") % NEAR
    mask = (block % NEAR) ^ near
    group = jnp.where(mask == 3, 0, jnp.where(mask == 0, 3, jnp.where(mask == first, 2, 1)))
    return group * (BLOCKS // NEAR) + block // NEAR


def store(ref, slots, kind, value):
    at, count = WHERE[kind]
    value = value.astype(BF16)
    for block in range(BLOCKS):
        ref[slots[block], at : at + count, :] = value[block * count : (block + 1) * count]


def store_conditioning(ref, slots, half, value):
    at, count = WHERE[6]
    value = value.astype(BF16)
    for block in range(BLOCKS):
        ref[slots[block], at : at + count, half * LANES : (half + 1) * LANES] = value[
            block * count : (block + 1) * count
        ]


def order_body(own, other, own_out, other_out):
    parts = own.shape[0]
    far = parts // NEAR
    _, near, _, first, second = place()
    for source, out, bit, next_bit in (
        (own, own_out, first, second),
        (other, other_out, second, first),
    ):
        for group, mask in enumerate((3, next_bit, bit, 0)):
            for index in range(far):
                out[group * far + index] = source[index * NEAR + (near ^ mask)]


def first_sum_body(own, got, *refs):
    out, token = refs[-2:]
    half = out.shape[0]
    out[...] = own[:half] + got[:half]
    token[...] = jnp.zeros_like(token)


def second_sum_body(own, got, near_got, *refs):
    out, token = refs[-2:]
    count = out.shape[0]
    kept = slice(2 * count, 3 * count)
    out[...] = (
        own[kept].astype(F32) + got[kept].astype(F32) + near_got[:count].astype(F32)
    ).astype(BF16)
    token[...] = jnp.zeros_like(token)


def third_sum_body(own, got, near_got, last_got, *refs):
    far = place()[0]
    count = last_got.shape[0]
    token = refs[-1]
    token[...] = jnp.zeros_like(token)
    for distance, out in enumerate(refs[-count - 1 : -1]):
        index = lax.rem(far + distance, count)
        out[...] = (
            own[3 * count + index].astype(F32)
            + got[3 * count + index].astype(F32)
            + near_got[count + index].astype(F32)
            + last_got[index].astype(F32)
        ).astype(out.dtype)


def ordered(grads):
    parts = lax.axis_size("tm")
    return grads if parts == BLOCKS else from_canonical(grads, parts)


def cores_summed(own, other, unread=()):
    own, other = ordered(own), ordered(other)
    if own.shape[0] != BLOCKS:
        own, other = call(order_body, (struct(own.shape, BF16),) * 2, own, other)
    got = swap_cores(other)
    half = struct((own.shape[0] // 2,) + own.shape[1:], BF16)
    sent, token = call(first_sum_body, (half, TOKEN), own, got, unread=unread)
    return (own, got), sent, token


def near_summed(grads, sent, flops=1024, unread=()):
    near_got = across(sent, 1)
    shape = (grads[0].shape[0] // NEAR,) + grads[0].shape[1:]
    sent, token = call(
        second_sum_body,
        (struct(shape, BF16), TOKEN),
        *grads,
        near_got,
        flops=flops,
        unread=unread,
    )
    return grads + (near_got,), sent, token


def far_terms(grads, last_got, flops=1024, unread=()):
    far, *shape = last_got.shape
    kept, *sends, token = call(
        third_sum_body,
        (struct(shape),) + (struct(shape, BF16),) * (far - 1) + (TOKEN,),
        *grads,
        last_got,
        flops=flops,
        unread=unread,
    )
    return [kept] + [along_far(value, k + 1) for k, value in enumerate(sends)], token


def gates(weights, lag, xin, cond):
    za = dot(lag, piece(weights, 0)) + dot(xin, piece(weights, 2))
    za = za + dot_right(cond, conditioning(weights, 0))
    zb = dot(lag, piece(weights, 1)) + dot(xin, piece(weights, 3))
    zb = zb + dot_right(cond, conditioning(weights, 1))
    return jnp.tanh(za), jax.nn.sigmoid(zb)


def gate_gradients(weights, res_grad, skip_grad, keep, tanh_a, sig_b):
    hidden_grad = dot(res_grad, piece(weights, 4)) + dot(skip_grad, piece(weights, 5))
    hidden_grad = hidden_grad * keep
    grad_a = (hidden_grad * sig_b * (1.0 - tanh_a * tanh_a)).astype(BF16)
    grad_b = (hidden_grad * tanh_a * sig_b * (1.0 - sig_b)).astype(BF16)
    return grad_a, grad_b


def weight_gradients(out, bit, lag, xin, cond, grad_a, grad_b, res_grad, skip_grad, hidden):
    slots = [slot(lax.axis_size("tm") == BLOCKS, bit, block) for block in range(BLOCKS)]
    store(out, slots, 0, dot_left(lag, grad_a))
    store(out, slots, 1, dot_left(lag, grad_b))
    store(out, slots, 2, dot_left(xin, grad_a))
    store(out, slots, 3, dot_left(xin, grad_b))
    store(out, slots, 4, dot_left(res_grad, hidden))
    store(out, slots, 5, dot_left(skip_grad, hidden))
    store_conditioning(out, slots, 0, dot_left(grad_a, cond))
    store_conditioning(out, slots, 1, dot_left(grad_b, cond))


def first_body(own, x, lag_raw, cond, marks, weights, *refs):
    earlier, (u2, s1, lag_out, ta, sb, hid, token) = refs[:-7], refs[-7:]
    token[...] = jnp.zeros_like(token)
    keep = marks[:, 0:1]
    xin = x[...].astype(BF16)
    lag = (lag_raw[...].astype(F32) * marks[:, 1:2]).astype(BF16)
    tanh_a, sig_b = gates(weights, lag, xin, cond[...])
    hidden = (keep * tanh_a * sig_b).astype(BF16)
    res = dot_right(hidden, piece(weights, 4))
    skip = dot_right(hidden[:own], piece(weights, 5))
    ta[...] = tanh_a[:own]
    sb[...] = sig_b[:own]
    hid[...] = hidden[:own]
    lag_out[...] = lag[:own]
    if len(earlier) == 2:
        u2[...] = (x[...] + (earlier[0][...] + res)) * ROOT_HALF
        s1[...] = earlier[1][...] + skip
    else:
        u2[...] = res
        s1[...] = skip


def second_input(u2, marks):
    xin = u2[...].astype(BF16)
    lag = (pltpu.roll(xin.astype(F32), 1, 0) * marks[:, 2:3]).astype(BF16)
    return xin, lag


def second_forward_body(u2, cond, marks, weights, ta, sb):
    xin, lag = second_input(u2, marks)
    ta[...], sb[...] = gates(weights, lag, xin, cond[...])


def second_body(own, u2, s1, cond, marks, cot, cot_skip, weights, *refs):
    last = len(refs) > 5
    earlier, (mixed, total, g2, lag_sum, grads) = refs[:-5], refs[-5:]
    rows = u2.shape[0]
    keep = marks[:, 0:1]
    xin, lag = second_input(u2, marks)
    res_grad = (cot[...] * ROOT_HALF).astype(BF16)
    skip_grad = cot_skip[...]
    if last:
        tanh_a, sig_b = earlier[4][...], earlier[5][...]
    else:
        tanh_a, sig_b = gates(weights, lag, xin, cond[...])
    hidden = (keep * tanh_a * sig_b).astype(BF16)[:own]
    grad_a, grad_b = gate_gradients(weights, res_grad, skip_grad, keep, tanh_a, sig_b)
    _, _, _, first_bit, second_bit = place()
    weight_gradients(
        grads,
        first_bit if last else second_bit,
        lag[:own],
        xin[:own],
        cond[:own, :],
        grad_a[:own],
        grad_b[:own],
        res_grad[:own],
        skip_grad[:own],
        hidden,
    )
    res = dot_right(hidden, piece(weights, 4))
    skip = dot_right(hidden, piece(weights, 5))
    lag_grad = dot_right(grad_a, piece(weights, 0)) + dot_right(grad_b, piece(weights, 1))
    now = dot_right(grad_a[:own], piece(weights, 2)) + dot_right(grad_b[:own], piece(weights, 3))
    if last:
        res, skip, now, lag_grad = (
            before[...] + value for before, value in zip(earlier, (res, skip, now, lag_grad))
        )
        mixed[...] = (u2[:own, :] + res) * ROOT_HALF
        total[...] = s1[...] + skip
        pushed = (lag_grad * marks[:, 2:3]).astype(BF16).astype(F32)
        g2[...] = cot[:own, :] * ROOT_HALF + now + pltpu.roll(pushed, rows - 1, 0)[:own]
    else:
        mixed[...] = res
        total[...] = skip
        g2[...] = now
        lag_sum[...] = lag_grad


def third_body(own, last, g2, x, lag, cond, marks, cot_skip, ta, sb, hid, weights, *refs):
    earlier, (g1, dlag, lag_sum, grads) = refs[:-4], refs[-4:]
    keep = marks[:own, 0:1]
    xin = x[:own, :].astype(BF16)
    res_grad = (g2[...] * ROOT_HALF).astype(BF16)
    skip_grad = cot_skip[:own, :]
    grad_a, grad_b = gate_gradients(weights, res_grad, skip_grad, keep, ta[...], sb[...])
    _, _, _, first_bit, second_bit = place()
    weight_gradients(
        grads,
        first_bit if last else second_bit,
        lag[...],
        xin,
        cond[:own, :],
        grad_a,
        grad_b,
        res_grad,
        skip_grad,
        hid[...],
    )
    lag_grad = dot_right(grad_a, piece(weights, 0)) + dot_right(grad_b, piece(weights, 1))
    now = dot_right(grad_a, piece(weights, 2)) + dot_right(grad_b, piece(weights, 3))
    if last:
        lag_sum[...] = jnp.zeros_like(lag_sum)
        g1[...] = g2[...] * ROOT_HALF + (earlier[0][...] + now)
        dlag[...] = ((earlier[1][...] + lag_grad) * marks[:own, 1:2]).astype(BF16)
    else:
        g1[...] = now
        lag_sum[...] = lag_grad


def part_body(x, cot, skip, lag, *refs):
    core = place()[2]
    kept, given, held = refs[-3:]
    span, width = kept.shape[0], x.shape[1]
    beyond = x.shape[0] - span
    held[...] = lag[...].astype(F32)
    for index, ref in enumerate((x, cot, skip, held)):
        columns = slice(index * width, (index + 1) * width)
        kept[:, columns] = ref[pl.ds(core * beyond, span), :]
        given[:, columns] = ref[pl.ds((1 - core) * beyond, span), :]


def join_body(kept, got, mel, mask, *refs):
    core = place()[2]
    inner, side, near_edge, edge_sent, held, lines = refs[-6:]
    span, width = kept.shape[0], kept.shape[1] // 4
    own, beyond = inner.shape[0], mel.shape[1] - span
    for index in range(4):
        for source, at in ((kept, core), (got, 1 - core)):
            held[:, pl.ds(index * 2 * width + at * width, width)] = source[
                :, index * width : (index + 1) * width
            ]
    blank = jnp.zeros((LANES - mel.shape[0] - 1, mel.shape[1]), F32)
    lines[...] = jnp.concatenate([mel[...], mask[...].astype(F32), blank], axis=0).T
    inner[...] = held[pl.ds(core * EDGE, own), :]
    side[...] = lines[pl.ds(core * own, own), :]
    for ref, at in ((near_edge, (1 - core) * own), (edge_sent, core * own)):
        ref[:, LANES:] = held[pl.ds(at, EDGE), :]
        ref[:, :LANES] = lines[pl.ds(core * beyond + at, EDGE), :]


def widen_body(
    mel, clips, lengths, inner, side, near_edge, edge, *refs
):
    far, near, core = place()[:3]
    x_out, cot_out, skip_out, lag_out, cond, marks = refs[-6:]
    own, full = inner.shape[0], inner.shape[1] // 4
    wide = own + 2 * EDGE
    after = jnp.where(core == 0, near_edge[...], edge[...])
    before = jnp.where(core == 0, edge[...], near_edge[...])
    for index, ref in enumerate((x_out, cot_out, skip_out, lag_out)):
        at = LANES + index * full
        ref[...] = jnp.concatenate(
            [
                inner[:, index * full : (index + 1) * full],
                after[:, at : at + full],
                before[:, at : at + full],
            ],
            axis=0,
        ).astype(ref.dtype)
    side_wide = jnp.concatenate([side[...], after[:, :LANES], before[:, :LANES]], axis=0)
    lane = lax.broadcasted_iota(jnp.int32, (wide, LANES), 1)
    line = lax.broadcasted_iota(jnp.int32, (wide, LANES), 0)
    first = ((far * NEAR + near) * 2 + core) * own
    position = first + jnp.where(line < own + EDGE, line, line - wide)

    def segment(at):
        total = jnp.zeros((wide, LANES), jnp.int32)
        end = jnp.int32(0)
        for clip in range(clips):
            end = end + lengths[clip]
            total = total + (at >= end).astype(jnp.int32)
        return total

    here = segment(position)

    def valid(span):
        return ((position >= span) & (segment(position - span) == here)).astype(F32)

    hot = ((lane - mel) == here).astype(F32)
    value = jnp.where(lane < mel, side_wide, jnp.where(lane < mel + clips, hot, 0.0))
    cond[...] = jnp.where(lane == mel + clips, 1.0, value).astype(BF16)
    keep = side_wide[:, mel : mel + 1]
    marks[...] = jnp.where(
        lane == 0, keep, jnp.where(lane == 1, valid(FIRST_DILATION), valid(1))
    )


def divide_body(mixed, total, g1, push, *refs):
    core = place()[2]
    kept, given, held = refs[-3:]
    width = kept.shape[1] // 4
    held[...] = push[...].astype(F32)
    for index, ref in enumerate((mixed, total, g1, held)):
        columns = slice(index * width, (index + 1) * width)
        kept[:, columns] = ref[:, pl.ds(core * width, width)]
        given[:, columns] = ref[:, pl.ds((1 - core) * width, width)]


def finish_body(kept, got, *refs):
    core = place()[2]
    outs, token = refs[:-1], refs[-1]
    token[...] = jnp.zeros_like(token)
    own, width = kept.shape[0], kept.shape[1] // 4
    for index, ref in enumerate(outs):
        for source, at in ((kept, core), (got, 1 - core)):
            ref[pl.ds(at * own, own), :] = source[:, index * width : (index + 1) * width]


def push_body(push, *refs):
    refs[-1][...] = push[...].astype(BF16)


def table_gradient(cond_grad, who, mel, clips, speakers):
    lane = lax.broadcasted_iota(jnp.int32, (cond_grad.shape[0], speakers), 1)
    result = jnp.zeros((cond_grad.shape[0], speakers), F32)
    for clip in range(clips):
        column = cond_grad[:, mel + clip : mel + clip + 1]
        result = result + jnp.where(lane == who[clip], column, 0.0)
    return result


def square_body(rows, mel, clips, speakers, count, who, *refs):
    terms, (out, squares) = refs[:count], refs[-2:]
    where, total = sections(rows)
    start = where[6][0]
    value = terms[0][...]
    for term in terms[1:]:
        value = value + term[...].astype(F32)
    out[...] = value
    main = out[:start, :]
    amount = jnp.sum(main * main, keepdims=True)
    for half in range(2):
        block = out[start:, half * LANES : (half + 1) * LANES]
        lane = lax.broadcasted_iota(jnp.int32, block.shape, 1)
        plain = jnp.where((lane < mel) | (lane == mel + clips), block, 0.0)
        amount = amount + jnp.sum(plain * plain, keepdims=True)
        table = table_gradient(block, who, mel, clips, speakers)
        amount = amount + jnp.sum(table * table, keepdims=True)
    squares[...] = jnp.broadcast_to(amount, squares.shape)


def add_body(left, right, out):
    out[...] = left[...] + right[...]


def spread_body(left, right, out):
    total = left[0:1, :] + right[0:1, :]
    out[...] = jnp.broadcast_to(total[None], out.shape)


def adamw(weight, mean, square, gradient, scale):
    clipped = gradient * scale
    new_mean = BETA_ONE * mean + (1.0 - BETA_ONE) * clipped
    new_square = BETA_TWO * square + (1.0 - BETA_TWO) * clipped * clipped
    fix_one = 1.0 - BETA_ONE**STEP
    fix_two = 1.0 - BETA_TWO**STEP
    update = new_mean / fix_one / (jnp.sqrt(new_square / fix_two) + ADAM_EPS)
    return weight - LEARN_RATE * (update + DECAY * weight), new_mean, new_square


def update_body(rows, mel, clips, who, *refs):
    grads = refs[0:2]
    squares = refs[2]
    old = [refs[3 + 3 * kind : 6 + 3 * kind] for kind in range(6)]
    part, push, norm, grad_input = refs[21:25]
    new = [refs[25 + 5 * kind : 30 + 5 * kind] for kind in range(6)]
    grad_input[...] = part[...] + push[...].astype(F32)
    where, total = sections(rows)
    chans = rows // 2
    grad_norm = jnp.sqrt(jnp.sum(squares[...], axis=0, keepdims=True)[:, 0:1])
    norm[...] = grad_norm
    scale = jnp.minimum(1.0, CLIP_NORM / grad_norm)

    def write(kind, index, gradient):
        weight, mean, square = (ref[index] for ref in old[kind])
        new_weight, new_mean, new_square = adamw(weight, mean, square, gradient, scale)
        for ref, value in zip(
            new[kind],
            (gradient, new_weight, new_mean, new_square, new_weight.astype(BF16)),
        ):
            ref[index] = value

    dil = new[0][0]
    for layer in range(2):
        for tap in range(2):
            for half in range(2):
                at, n = where[2 * tap + half]
                for tile in range(2):
                    dil[strided(layer, tap, half, tile, rows), :] = grads[layer][
                        at : at + n, tile * LANES : (tile + 1) * LANES
                    ]
    weight, mean, square = (ref[...] for ref in old[0])
    new_weight, new_mean, new_square = adamw(weight, mean, square, dil[...], scale)
    new[0][1][...] = new_weight
    new[0][2][...] = new_mean
    new[0][3][...] = new_square
    new[0][4][...] = new_weight.astype(BF16)
    for layer in range(2):
        for half in range(2):
            block = grads[layer][where[6][0] :, half * LANES : (half + 1) * LANES]
            eye = lax.broadcasted_iota(jnp.int32, (chans, chans), 0) == lax.broadcasted_iota(
                jnp.int32, (chans, chans), 1
            )
            column = block[:, mel + clips : mel + clips + 1]
            line = jnp.sum(jnp.where(eye, column, 0.0), axis=0, keepdims=True)
            write(1, (layer, slice(half, half + 1), slice(None)), line)
            write(2, (layer, half), block[:, :mel])
            speakers = old[3][0].shape[-1]
            write(3, (layer, half), table_gradient(block, who, mel, clips, speakers))
        for kind, section in ((4, 4), (5, 5)):
            at, n = where[section]
            write(kind, (layer,), grads[layer][at : at + n, :])


def on_device(
    x_input,
    mel_frames,
    sample_mask,
    clip_length_array,
    speaker_ids,
    cot_out,
    cot_skip,
    *states,
):
    parts = lax.axis_size("tm")
    held_rows, width = x_input.shape
    own, full = held_rows // 2, 2 * width
    wide = own + 2 * EDGE
    mel = mel_frames.shape[0]
    clips = clip_length_array.shape[0]
    hop = FIRST_DILATION // held_rows

    dil_shape = states[0].shape
    rows = dil_shape[2]
    views = (
        [dilated_view(s) for s in states[0:3]]
        + list(states[3:6])
        + [s.transpose(0, 2, 3, 1) for s in states[6:12]]
        + [s.transpose(0, 2, 1) for s in states[12:18]]
    )
    speakers = views[9].shape[-1]
    where, total = sections(rows)
    far = parts // NEAR
    taken = [views[k] for k in (0, 12, 15, 6, 9, 3)]
    packed_type = BF16 if rows % 32 == 0 else F32
    taken = [views[k] for k in (0, 12, 15, 6, 9, 3)]
    packed_type = BF16 if rows % 32 == 0 else F32
    taken.append(x_input)
    pack_one, pack_two, x_low = call(
        functools.partial(start_body, rows, mel, clips),
        (struct((total, 256), packed_type),) * 2 + (struct(x_input.shape, BF16),),
        *taken,
        scalars=(speaker_ids,),
        space=pl.ANY,
        grant=None,
        scratch=[pltpu.VMEM(v.shape, F32) for v in taken]
        + [pltpu.SemaphoreType.DMA((len(taken),))],
    )

    lag = shifted(x_low, "tm", hop)
    span = own + EDGE
    group_one, stacked = along_all(pack_one.astype(BF16), (lag,))
    group_two, stacked = along_all(pack_two.astype(BF16), (stacked,))
    kept, given = call(
        part_body,
        (struct((span, 4 * width)),) * 2,
        x_input,
        cot_out,
        cot_skip,
        lag,
        unread=(stacked,),
        scratch=[pltpu.VMEM(x_input.shape, F32)],
    )
    parts_one, relayed = near_exchange(group_one, (stacked,), LONG)
    parts_two, begun = near_exchange(group_two, (), LONG)
    joined_own = struct((own, 4 * full))
    edge = struct((EDGE, 4 * full + LANES))
    inner, side, near_edge, edge_sent = call(
        join_body,
        (joined_own, struct((own, LANES)), edge, edge),
        kept,
        swap_cores(given),
        mel_frames,
        sample_mask[None, :],
        unread=(relayed,),
        scratch=[pltpu.VMEM((span, 4 * full), F32), pltpu.VMEM((held_rows, LANES), F32)],
    )
    x_wide, cot_wide, skip_wide, lag_wide, cond, marks = call(
        functools.partial(widen_body, mel, clips),
        (
            struct((wide, full)),
            struct((wide, full)),
            struct((wide, full), BF16),
            struct((wide, full), BF16),
            struct((wide, LANES), BF16),
            struct((wide, LANES)),
        ),
        inner,
        side,
        near_edge,
        across_chips(edge_sent),
        scalars=(clip_length_array,),
        unread=(begun,),
    )
    w1_own, w1_oth = joined(parts_one, (marks,))

    half = struct((own, width))
    wave = struct((own, full))
    broad = struct((wide, full))
    low_half = struct((own, width), BF16)
    low_full = struct((own, full), BF16)
    packed = struct((BLOCKS, ROWS, 256), BF16)

    def forward(weights, *earlier, unread=(), flops=1024):
        return call(
            functools.partial(first_body, own),
            (broad, wave, low_full, half, half, low_half, TOKEN),
            x_wide,
            lag_wide,
            cond,
            marks,
            weights,
            *earlier,
            unread=unread,
            flops=flops,
        )

    res, skip, lag1, ta_own, sb_own, hid_own, _ = forward(w1_own, unread=(begun,), flops=LONG)
    u2, s1, _, ta_oth, sb_oth, hid_oth, token = forward(w1_oth, res, skip)

    w2_own, w2_oth = joined(parts_two, (token,))

    def middle(weights, *earlier):
        return call(
            functools.partial(second_body, own),
            (wave, wave, wave, TOKEN if earlier else broad, packed),
            u2,
            s1,
            cond,
            marks,
            cot_wide,
            skip_wide,
            weights,
            *earlier,
        )

    gate_two = call(
        second_forward_body, (struct((wide, width)),) * 2, u2, cond, marks, w2_own
    )
    *sums, grad_oth = middle(w2_oth)
    mixed, skip_total, g2, _, grad_own = middle(w2_own, *sums, *gate_two)

    def totals(terms, unread=(), flops=1024):
        return call(
            functools.partial(square_body, rows, mel, clips, speakers, len(terms)),
            (struct((total, 256)), struct((8, LANES))),
            *terms,
            scalars=(speaker_ids,),
            unread=unread,
            flops=flops,
        )

    def backward(weights, tanh_a, sig_b, hidden, *earlier, unread):
        last = bool(earlier)
        return call(
            functools.partial(third_body, own, last),
            (wave, low_full if last else TOKEN, TOKEN if last else wave, packed),
            g2,
            x_wide,
            lag1,
            cond,
            marks,
            skip_wide,
            tanh_a,
            sig_b,
            hidden,
            weights,
            *earlier,
            unread=unread,
        )

    grads2, sent2, token = cores_summed(grad_own, grad_oth)
    now, _, lag_sum, grad_oth = backward(w1_oth, ta_oth, sb_oth, hid_oth, unread=(token,))
    g1_part, dlag1, backed, grad_own = backward(
        w1_own, ta_own, sb_own, hid_own, now, lag_sum, unread=()
    )
    kept, given = call(
        divide_body,
        (struct((own, 4 * width)),) * 2,
        mixed,
        skip_total,
        g1_part,
        dlag1,
        scratch=[pltpu.VMEM((own, full), F32)],
    )
    mixed, skip_total, grad_input, push, token = call(
        finish_body, (struct((held_rows, width)),) * 4 + (TOKEN,), kept, swap_cores(given)
    )
    grads2, sent2, summed = near_summed(grads2, sent2, LONG, (backed,))
    grads1, sent1, _ = cores_summed(grad_own, grad_oth, (summed, token))
    last_got = across(sent2, 0)
    terms2, _ = far_terms(grads2, last_got, LONG)
    grads1, sent1, _ = near_summed(grads1, sent1, unread=(terms2[1], terms2[-1]))
    terms1, token = far_terms(grads1, across(sent1, 0))
    sum2, squares2 = totals(terms2, (token,))
    push = call(push_body, struct((held_rows, width), BF16), push, unread=(squares2,))
    push = shifted(push, "tm", -hop)
    sum1, squares1 = totals(terms1, flops=LONG // 5)
    squares = call(add_body, TOKEN, squares1, squares2)
    sent = call(spread_body, struct((parts, 1, LANES)), squares, swap_cores(squares))
    squares = lax.all_to_all(sent, "tm", split_axis=0, concat_axis=0, tiled=True)
    outs = [struct((1, 1)), struct((held_rows, width))]
    for view in views[0::3]:
        outs += [struct(view.shape)] * 4 + [struct(view.shape, BF16)]
    updated = call(
        functools.partial(update_body, rows, mel, clips),
        tuple(outs),
        sum1,
        sum2,
        squares.reshape(parts, LANES),
        *views,
        grad_input,
        push,
        scalars=(speaker_ids,),
    )
    grad_norm, grad_input = updated[0].reshape(()), updated[1]
    backs = (
        [lambda v: dilated_back(v, dil_shape), lambda v: v]
        + [lambda v: v.transpose(0, 3, 1, 2)] * 2
        + [lambda v: v.transpose(0, 2, 1)] * 2
    )
    new = [
        [back(v) for v in updated[2 + 5 * kind : 7 + 5 * kind]] for kind, back in enumerate(backs)
    ]
    return (
        mixed,
        skip_total,
        grad_input,
        grad_norm,
        *[group[0] for group in new],
        *[value for group in new for value in group[1:4]],
        *[group[4] for group in new],
    )


def solution(mesh):
    rows = P("tm", "mp")
    dil = P(None, None, "tm", None, "mp")
    bias = P(None, None, ("mp", "tm"))
    wide = P(None, None, None, ("mp", "tm"))
    square = P(None, "mp", "tm")
    kinds = (dil, bias, wide, wide, square, square)
    thrice = tuple(kind for kind in kinds for _ in range(3))
    return jax.shard_map(
        on_device,
        mesh=mesh,
        in_specs=(rows, P(None, "tm"), P("tm"), P(), P(), rows, rows) + thrice,
        out_specs=(rows, rows, rows, P()) + kinds + thrice + kinds,
        check_vma=False,
    )
```

```python
import functools

import jax
import jax.numpy as jnp
from jax import lax
from jax.experimental import pallas as pl
from jax.experimental.pallas import tpu as pltpu
from jax.sharding import PartitionSpec as P

FIRST_DILATION = 512
STEP = 10
ROOT_HALF = 0.7071067811865476
BETA_ONE = 0.9
BETA_TWO = 0.999
ADAM_EPS = 1e-08
LEARN_RATE = 0.07
DECAY = 0.01
CLIP_NORM = 1.0

F32 = jnp.float32
BF16 = jnp.bfloat16
LANES = 128
EDGE = 8
BLOCKS = 16
NEAR = 4
VMEM_BYTES = 26 * 1024 * 1024
BOTH = ("tm", "mp")


def struct(shape, dtype=F32):
    return jax.ShapeDtypeStruct(shape, dtype)


def call(body, out_shape, *operands, scalars=(), scratch=(), space=pltpu.VMEM, unread=(), flops=1024, grant=VMEM_BYTES):
    specs = [pl.BlockSpec(memory_space=pltpu.SMEM)] * len(scalars)
    specs += [pl.BlockSpec(memory_space=space)] * len(operands)
    specs += [pl.BlockSpec(memory_space=pl.ANY)] * len(unread)
    return pl.pallas_call(
        body,
        out_shape=out_shape,
        in_specs=specs,
        scratch_shapes=list(scratch),
        compiler_params=pltpu.CompilerParams(vmem_limit_bytes=grant),
        cost_estimate=pl.CostEstimate(flops=flops, bytes_accessed=1024, transcendentals=0),
    )(*scalars, *operands, *unread)


def dot(left, right):
    return jnp.dot(left, right, preferred_element_type=F32)


def dot_right(left, right):
    return lax.dot_general(left, right, (((1,), (1,)), ((), ())), preferred_element_type=F32)


def dot_left(left, right):
    return lax.dot_general(left, right, (((0,), (0,)), ((), ())), preferred_element_type=F32)


def place():
    index = lax.axis_index("tm")
    core = lax.axis_index("mp")
    return index // NEAR, index % NEAR, core, 1 + core, 2 - core


def route(target):
    return [
        (index * 2 + core, target(index, core) * 2 + core)
        for index in range(lax.axis_size("tm"))
        for core in range(2)
    ]


def across(value, bit):
    return lax.ppermute(value, BOTH, route(lambda i, c: i ^ (1 + (c ^ bit))))


def along_far(value, distance):
    far = lax.axis_size("tm") // NEAR
    return lax.ppermute(
        value, BOTH, route(lambda i, c: (i // NEAR + distance) % far * NEAR + i % NEAR)
    )


def swap_cores(value):
    return lax.ppermute(value, "mp", [(0, 1), (1, 0)])


def shifted(value, axis, distance):
    devices = range(lax.axis_size(axis))
    pairs = [(i - distance, i) for i in devices if i - distance in devices]
    return lax.ppermute(value, axis, pairs)


def across_chips(value):
    pairs = []
    for index in range(1, lax.axis_size("tm")):
        pairs += [(index * 2 - 1, index * 2), (index * 2, index * 2 - 1)]
    return lax.ppermute(value, BOTH, pairs)


def sections(rows):
    found, at = [], 0
    for count in (rows,) * 6 + (rows // 2,):
        found.append((at, count))
        at += count
    return found, at


WHERE, ROWS = sections(32)


def dilated_view(array):
    layers, taps, rows, halves, width = array.shape
    tiles = width // LANES
    split = array.reshape(layers, taps, rows, halves, tiles, LANES)
    return split.transpose(0, 1, 2, 4, 3, 5).reshape(-1, LANES)


def dilated_back(array, shape):
    layers, taps, rows, halves, width = shape
    tiles = width // LANES
    split = array.reshape(layers, taps, rows, tiles, halves, LANES)
    return split.transpose(0, 1, 2, 4, 3, 5).reshape(shape)


def strided(layer, tap, half, tile, rows):
    return pl.ds((layer * 2 + tap) * rows * 4 + tile * 2 + half, rows, stride=4)


def start_body(rows, mel, clips, who, *refs):
    sources, (out_one, out_two, low), held, sems = refs[:7], refs[7:10], refs[10:17], refs[17]
    copies = [
        pltpu.make_async_copy(source, target, sems.at[index])
        for index, (source, target) in enumerate(zip(sources, held))
    ]
    for copy in copies:
        copy.start()
    dil, res, skip, mel_w, table, bias, samples = held
    where, total = sections(rows)
    chans = rows // 2
    speakers = table.shape[-1]
    lane = lax.broadcasted_iota(jnp.int32, (1, speakers), 1)
    hot = jnp.concatenate([(lane == who[k]).astype(F32) for k in range(clips)], axis=0).astype(BF16)
    eye = lax.broadcasted_iota(jnp.int32, (chans, chans), 0) == lax.broadcasted_iota(
        jnp.int32, (chans, chans), 1
    )

    def write(out, at, count, columns, value):
        out[at : at + count, columns] = value.astype(out.dtype)

    for copy in copies[:-1]:
        copy.wait()
    for layer, out in enumerate((out_one, out_two)):
        for tap in range(2):
            for half in range(2):
                at, count = where[2 * tap + half]
                for tile in range(2):
                    part = dil[strided(layer, tap, half, tile, rows), :]
                    write(out, at, count, slice(tile * LANES, (tile + 1) * LANES), part)
        for kind, source in ((4, res), (5, skip)):
            at, count = where[kind]
            write(out, at, count, slice(None), source[layer])
        at, count = where[6]
        for half in range(2):
            picked = dot_right(table[layer, half].astype(BF16), hot)
            line = jnp.broadcast_to(bias[layer, half : half + 1, :], (chans, chans))
            column = jnp.sum(jnp.where(eye, line, 0.0), axis=1, keepdims=True)
            blank = jnp.zeros((chans, LANES - mel - clips - 1), F32)
            row = jnp.concatenate([mel_w[layer, half], picked, column, blank], axis=1)
            columns = slice(half * LANES, (half + 1) * LANES)
            write(out, at, count, columns, row.astype(BF16).astype(F32))
    copies[-1].wait()
    low[...] = samples[...].astype(BF16)


def assemble_body(group, first, second, last, *refs):
    out = refs[-1]
    count = group.shape[0]
    far, near, _, first_bit, second_bit = place()
    for ref, mask in ((group, 0), (first, first_bit), (second, second_bit), (last, 3)):
        for back in range(count):
            out[lax.rem(far + count - back, count) * NEAR + (near ^ mask)] = ref[back]


def relay_body(value, *refs):
    out, token = refs[-2:]
    out[...] = value[...]
    token[...] = jnp.zeros_like(token)


TOKEN = struct((8, LANES))
LONG = 20_000_000_000


def stack_body(count, *refs):
    out, token = refs[-2:]
    for index in range(count):
        out[index] = refs[index][...]
    token[...] = jnp.zeros_like(token)


def along_all(pack, unread):
    far = lax.axis_size("tm") // NEAR
    got = [along_far(pack, distance) for distance in range(1, far)]
    held, _ = call(relay_body, (struct(pack.shape, BF16), TOKEN), pack)
    return call(
        functools.partial(stack_body, far),
        (struct((far,) + pack.shape, BF16), TOKEN),
        held,
        *got,
        unread=unread,
    )


def near_exchange(group, before_last, flops=1024):
    first = across(group, 0)
    second = across(group, 1)
    passed, token = call(
        relay_body,
        (struct(first.shape, BF16), TOKEN),
        first,
        unread=(second,) + before_last,
        flops=flops,
    )
    return (group, first, second, across(passed, 1)), token


def joined(parts, before_end):
    count = NEAR * parts[0].shape[0]
    own = call(
        assemble_body, struct((count,) + parts[0].shape[1:], BF16), *parts, unread=before_end
    )
    if count != BLOCKS:
        own = to_canonical(own)
    return own, swap_cores(own)


def to_canonical(gathered):
    parts = gathered.shape[0]
    where, total = sections(BLOCKS * 32 // parts)
    return jnp.concatenate(
        [gathered[:, at : at + n, :].reshape(BLOCKS, -1, 256) for at, n in where], axis=1
    )


def from_canonical(packed, parts):
    where, total = sections(32)
    return jnp.concatenate(
        [packed[:, at : at + n, :].reshape(parts, -1, 256) for at, n in where], axis=1
    )


def piece(ref, kind):
    at, count = WHERE[kind]
    return ref[:, at : at + count, :].reshape(-1, 256)


def conditioning(ref, half):
    at, count = WHERE[6]
    return ref[:, at : at + count, half * LANES : (half + 1) * LANES].reshape(-1, LANES)


def slot(ordered, first, block):
    if not ordered:
        return block
    near = lax.axis_index("tm") % NEAR
    mask = (block % NEAR) ^ near
    group = jnp.where(mask == 3, 0, jnp.where(mask == 0, 3, jnp.where(mask == first, 2, 1)))
    return group * (BLOCKS // NEAR) + block // NEAR


def store(ref, slots, kind, value):
    at, count = WHERE[kind]
    value = value.astype(BF16)
    for block in range(BLOCKS):
        ref[slots[block], at : at + count, :] = value[block * count : (block + 1) * count]


def store_conditioning(ref, slots, half, value):
    at, count = WHERE[6]
    value = value.astype(BF16)
    for block in range(BLOCKS):
        ref[slots[block], at : at + count, half * LANES : (half + 1) * LANES] = value[
            block * count : (block + 1) * count
        ]


def order_body(own, other, own_out, other_out):
    parts = own.shape[0]
    far = parts // NEAR
    _, near, _, first, second = place()
    for source, out, bit, next_bit in (
        (own, own_out, first, second),
        (other, other_out, second, first),
    ):
        for group, mask in enumerate((3, next_bit, bit, 0)):
            for index in range(far):
                out[group * far + index] = source[index * NEAR + (near ^ mask)]


def first_sum_body(own, got, *refs):
    out, token = refs[-2:]
    half = out.shape[0]
    out[...] = own[:half] + got[:half]
    token[...] = jnp.zeros_like(token)


def second_sum_body(own, got, near_got, *refs):
    out, token = refs[-2:]
    count = out.shape[0]
    kept = slice(2 * count, 3 * count)
    out[...] = (
        own[kept].astype(F32) + got[kept].astype(F32) + near_got[:count].astype(F32)
    ).astype(BF16)
    token[...] = jnp.zeros_like(token)


def third_sum_body(own, got, near_got, last_got, *refs):
    far = place()[0]
    count = last_got.shape[0]
    token = refs[-1]
    token[...] = jnp.zeros_like(token)
    for distance, out in enumerate(refs[-count - 1 : -1]):
        index = lax.rem(far + distance, count)
        out[...] = (
            own[3 * count + index].astype(F32)
            + got[3 * count + index].astype(F32)
            + near_got[count + index].astype(F32)
            + last_got[index].astype(F32)
        ).astype(out.dtype)


def ordered(grads):
    parts = lax.axis_size("tm")
    return grads if parts == BLOCKS else from_canonical(grads, parts)


def cores_summed(own, other, unread=()):
    own, other = ordered(own), ordered(other)
    if own.shape[0] != BLOCKS:
        own, other = call(order_body, (struct(own.shape, BF16),) * 2, own, other)
    got = swap_cores(other)
    half = struct((own.shape[0] // 2,) + own.shape[1:], BF16)
    sent, token = call(first_sum_body, (half, TOKEN), own, got, unread=unread)
    return (own, got), sent, token


def near_summed(grads, sent, flops=1024, unread=()):
    near_got = across(sent, 1)
    shape = (grads[0].shape[0] // NEAR,) + grads[0].shape[1:]
    sent, token = call(
        second_sum_body,
        (struct(shape, BF16), TOKEN),
        *grads,
        near_got,
        flops=flops,
        unread=unread,
    )
    return grads + (near_got,), sent, token


def far_terms(grads, last_got, flops=1024, unread=()):
    far, *shape = last_got.shape
    kept, *sends, token = call(
        third_sum_body,
        (struct(shape),) + (struct(shape, BF16),) * (far - 1) + (TOKEN,),
        *grads,
        last_got,
        flops=flops,
        unread=unread,
    )
    return [kept] + [along_far(value, k + 1) for k, value in enumerate(sends)], token


def gates(weights, lag, xin, cond):
    za = dot(lag, piece(weights, 0)) + dot(xin, piece(weights, 2))
    za = za + dot_right(cond, conditioning(weights, 0))
    zb = dot(lag, piece(weights, 1)) + dot(xin, piece(weights, 3))
    zb = zb + dot_right(cond, conditioning(weights, 1))
    return jnp.tanh(za), jax.nn.sigmoid(zb)


def gate_gradients(weights, res_grad, skip_grad, keep, tanh_a, sig_b):
    hidden_grad = dot(res_grad, piece(weights, 4)) + dot(skip_grad, piece(weights, 5))
    hidden_grad = hidden_grad * keep
    grad_a = (hidden_grad * sig_b * (1.0 - tanh_a * tanh_a)).astype(BF16)
    grad_b = (hidden_grad * tanh_a * sig_b * (1.0 - sig_b)).astype(BF16)
    return grad_a, grad_b


def weight_gradients(out, bit, lag, xin, cond, grad_a, grad_b, res_grad, skip_grad, hidden):
    slots = [slot(lax.axis_size("tm") == BLOCKS, bit, block) for block in range(BLOCKS)]
    store(out, slots, 0, dot_left(lag, grad_a))
    store(out, slots, 1, dot_left(lag, grad_b))
    store(out, slots, 2, dot_left(xin, grad_a))
    store(out, slots, 3, dot_left(xin, grad_b))
    store(out, slots, 4, dot_left(res_grad, hidden))
    store(out, slots, 5, dot_left(skip_grad, hidden))
    store_conditioning(out, slots, 0, dot_left(grad_a, cond))
    store_conditioning(out, slots, 1, dot_left(grad_b, cond))


def first_body(own, x, lag_raw, cond, marks, weights, *refs):
    earlier, (u2, s1, lag_out, ta, sb, hid, token) = refs[:-7], refs[-7:]
    token[...] = jnp.zeros_like(token)
    keep = marks[:, 0:1]
    xin = x[...].astype(BF16)
    lag = (lag_raw[...].astype(F32) * marks[:, 1:2]).astype(BF16)
    tanh_a, sig_b = gates(weights, lag, xin, cond[...])
    hidden = (keep * tanh_a * sig_b).astype(BF16)
    res = dot_right(hidden, piece(weights, 4))
    skip = dot_right(hidden[:own], piece(weights, 5))
    ta[...] = tanh_a[:own]
    sb[...] = sig_b[:own]
    hid[...] = hidden[:own]
    lag_out[...] = lag[:own]
    if len(earlier) == 2:
        u2[...] = (x[...] + (earlier[0][...] + res)) * ROOT_HALF
        s1[...] = earlier[1][...] + skip
    else:
        u2[...] = res
        s1[...] = skip


def second_input(u2, marks):
    xin = u2[...].astype(BF16)
    lag = (pltpu.roll(xin.astype(F32), 1, 0) * marks[:, 2:3]).astype(BF16)
    return xin, lag


def second_forward_body(u2, cond, marks, weights, ta, sb):
    xin, lag = second_input(u2, marks)
    ta[...], sb[...] = gates(weights, lag, xin, cond[...])


def second_body(own, u2, s1, cond, marks, cot, cot_skip, weights, *refs):
    last = len(refs) > 5
    earlier, (mixed, total, g2, lag_sum, grads) = refs[:-5], refs[-5:]
    rows = u2.shape[0]
    keep = marks[:, 0:1]
    xin, lag = second_input(u2, marks)
    res_grad = (cot[...] * ROOT_HALF).astype(BF16)
    skip_grad = cot_skip[...]
    if last:
        tanh_a, sig_b = earlier[4][...], earlier[5][...]
    else:
        tanh_a, sig_b = gates(weights, lag, xin, cond[...])
    hidden = (keep * tanh_a * sig_b).astype(BF16)[:own]
    grad_a, grad_b = gate_gradients(weights, res_grad, skip_grad, keep, tanh_a, sig_b)
    _, _, _, first_bit, second_bit = place()
    weight_gradients(
        grads,
        first_bit if last else second_bit,
        lag[:own],
        xin[:own],
        cond[:own, :],
        grad_a[:own],
        grad_b[:own],
        res_grad[:own],
        skip_grad[:own],
        hidden,
    )
    res = dot_right(hidden, piece(weights, 4))
    skip = dot_right(hidden, piece(weights, 5))
    lag_grad = dot_right(grad_a, piece(weights, 0)) + dot_right(grad_b, piece(weights, 1))
    now = dot_right(grad_a[:own], piece(weights, 2)) + dot_right(grad_b[:own], piece(weights, 3))
    if last:
        res, skip, now, lag_grad = (
            before[...] + value for before, value in zip(earlier, (res, skip, now, lag_grad))
        )
        mixed[...] = (u2[:own, :] + res) * ROOT_HALF
        total[...] = s1[...] + skip
        pushed = (lag_grad * marks[:, 2:3]).astype(BF16).astype(F32)
        g2[...] = cot[:own, :] * ROOT_HALF + now + pltpu.roll(pushed, rows - 1, 0)[:own]
    else:
        mixed[...] = res
        total[...] = skip
        g2[...] = now
        lag_sum[...] = lag_grad


def third_body(own, last, g2, x, lag, cond, marks, cot_skip, ta, sb, hid, weights, *refs):
    earlier, (g1, dlag, lag_sum, grads) = refs[:-4], refs[-4:]
    keep = marks[:own, 0:1]
    xin = x[:own, :].astype(BF16)
    res_grad = (g2[...] * ROOT_HALF).astype(BF16)
    skip_grad = cot_skip[:own, :]
    grad_a, grad_b = gate_gradients(weights, res_grad, skip_grad, keep, ta[...], sb[...])
    _, _, _, first_bit, second_bit = place()
    weight_gradients(
        grads,
        first_bit if last else second_bit,
        lag[...],
        xin,
        cond[:own, :],
        grad_a,
        grad_b,
        res_grad,
        skip_grad,
        hid[...],
    )
    lag_grad = dot_right(grad_a, piece(weights, 0)) + dot_right(grad_b, piece(weights, 1))
    now = dot_right(grad_a, piece(weights, 2)) + dot_right(grad_b, piece(weights, 3))
    if last:
        lag_sum[...] = jnp.zeros_like(lag_sum)
        g1[...] = g2[...] * ROOT_HALF + (earlier[0][...] + now)
        dlag[...] = ((earlier[1][...] + lag_grad) * marks[:own, 1:2]).astype(BF16)
    else:
        g1[...] = now
        lag_sum[...] = lag_grad


def part_body(x, cot, skip, lag, *refs):
    core = place()[2]
    kept, given, held = refs[-3:]
    span, width = kept.shape[0], x.shape[1]
    beyond = x.shape[0] - span
    held[...] = lag[...].astype(F32)
    for index, ref in enumerate((x, cot, skip, held)):
        columns = slice(index * width, (index + 1) * width)
        kept[:, columns] = ref[pl.ds(core * beyond, span), :]
        given[:, columns] = ref[pl.ds((1 - core) * beyond, span), :]


def join_body(kept, got, mel, mask, *refs):
    core = place()[2]
    inner, side, near_edge, edge_sent, held, lines = refs[-6:]
    span, width = kept.shape[0], kept.shape[1] // 4
    own, beyond = inner.shape[0], mel.shape[1] - span
    for index in range(4):
        for source, at in ((kept, core), (got, 1 - core)):
            held[:, pl.ds(index * 2 * width + at * width, width)] = source[
                :, index * width : (index + 1) * width
            ]
    blank = jnp.zeros((LANES - mel.shape[0] - 1, mel.shape[1]), F32)
    lines[...] = jnp.concatenate([mel[...], mask[...].astype(F32), blank], axis=0).T
    inner[...] = held[pl.ds(core * EDGE, own), :]
    side[...] = lines[pl.ds(core * own, own), :]
    for ref, at in ((near_edge, (1 - core) * own), (edge_sent, core * own)):
        ref[:, LANES:] = held[pl.ds(at, EDGE), :]
        ref[:, :LANES] = lines[pl.ds(core * beyond + at, EDGE), :]


def widen_body(
    mel, clips, lengths, inner, side, near_edge, edge, *refs
):
    far, near, core = place()[:3]
    x_out, cot_out, skip_out, lag_out, cond, marks = refs[-6:]
    own, full = inner.shape[0], inner.shape[1] // 4
    wide = own + 2 * EDGE
    after = jnp.where(core == 0, near_edge[...], edge[...])
    before = jnp.where(core == 0, edge[...], near_edge[...])
    for index, ref in enumerate((x_out, cot_out, skip_out, lag_out)):
        at = LANES + index * full
        ref[...] = jnp.concatenate(
            [
                inner[:, index * full : (index + 1) * full],
                after[:, at : at + full],
                before[:, at : at + full],
            ],
            axis=0,
        ).astype(ref.dtype)
    side_wide = jnp.concatenate([side[...], after[:, :LANES], before[:, :LANES]], axis=0)
    lane = lax.broadcasted_iota(jnp.int32, (wide, LANES), 1)
    line = lax.broadcasted_iota(jnp.int32, (wide, LANES), 0)
    first = ((far * NEAR + near) * 2 + core) * own
    position = first + jnp.where(line < own + EDGE, line, line - wide)

    def segment(at):
        total = jnp.zeros((wide, LANES), jnp.int32)
        end = jnp.int32(0)
        for clip in range(clips):
            end = end + lengths[clip]
            total = total + (at >= end).astype(jnp.int32)
        return total

    here = segment(position)

    def valid(span):
        return ((position >= span) & (segment(position - span) == here)).astype(F32)

    hot = ((lane - mel) == here).astype(F32)
    value = jnp.where(lane < mel, side_wide, jnp.where(lane < mel + clips, hot, 0.0))
    cond[...] = jnp.where(lane == mel + clips, 1.0, value).astype(BF16)
    keep = side_wide[:, mel : mel + 1]
    marks[...] = jnp.where(
        lane == 0, keep, jnp.where(lane == 1, valid(FIRST_DILATION), valid(1))
    )


def divide_body(mixed, total, g1, push, *refs):
    core = place()[2]
    kept, given, held = refs[-3:]
    width = kept.shape[1] // 4
    held[...] = push[...].astype(F32)
    for index, ref in enumerate((mixed, total, g1, held)):
        columns = slice(index * width, (index + 1) * width)
        kept[:, columns] = ref[:, pl.ds(core * width, width)]
        given[:, columns] = ref[:, pl.ds((1 - core) * width, width)]


def finish_body(kept, got, *refs):
    core = place()[2]
    outs, token = refs[:-1], refs[-1]
    token[...] = jnp.zeros_like(token)
    own, width = kept.shape[0], kept.shape[1] // 4
    for index, ref in enumerate(outs):
        for source, at in ((kept, core), (got, 1 - core)):
            ref[pl.ds(at * own, own), :] = source[:, index * width : (index + 1) * width]


def push_body(push, *refs):
    refs[-1][...] = push[...].astype(BF16)


def table_gradient(cond_grad, who, mel, clips, speakers):
    lane = lax.broadcasted_iota(jnp.int32, (cond_grad.shape[0], speakers), 1)
    result = jnp.zeros((cond_grad.shape[0], speakers), F32)
    for clip in range(clips):
        column = cond_grad[:, mel + clip : mel + clip + 1]
        result = result + jnp.where(lane == who[clip], column, 0.0)
    return result


def square_body(rows, mel, clips, speakers, count, who, *refs):
    terms, (out, squares) = refs[:count], refs[-2:]
    where, total = sections(rows)
    start = where[6][0]
    value = terms[0][...]
    for term in terms[1:]:
        value = value + term[...].astype(F32)
    out[...] = value
    main = out[:start, :]
    amount = jnp.sum(main * main, keepdims=True)
    for half in range(2):
        block = out[start:, half * LANES : (half + 1) * LANES]
        lane = lax.broadcasted_iota(jnp.int32, block.shape, 1)
        plain = jnp.where((lane < mel) | (lane == mel + clips), block, 0.0)
        amount = amount + jnp.sum(plain * plain, keepdims=True)
        table = table_gradient(block, who, mel, clips, speakers)
        amount = amount + jnp.sum(table * table, keepdims=True)
    squares[...] = jnp.broadcast_to(amount, squares.shape)


def add_body(left, right, out):
    out[...] = left[...] + right[...]


def spread_body(left, right, out):
    total = left[0:1, :] + right[0:1, :]
    out[...] = jnp.broadcast_to(total[None], out.shape)


def adamw(weight, mean, square, gradient, scale):
    clipped = gradient * scale
    new_mean = BETA_ONE * mean + (1.0 - BETA_ONE) * clipped
    new_square = BETA_TWO * square + (1.0 - BETA_TWO) * clipped * clipped
    fix_one = 1.0 - BETA_ONE**STEP
    fix_two = 1.0 - BETA_TWO**STEP
    update = new_mean / fix_one / (jnp.sqrt(new_square / fix_two) + ADAM_EPS)
    return weight - LEARN_RATE * (update + DECAY * weight), new_mean, new_square


def update_body(rows, mel, clips, who, *refs):
    grads = refs[0:2]
    squares = refs[2]
    old = [refs[3 + 3 * kind : 6 + 3 * kind] for kind in range(6)]
    part, push, norm, grad_input = refs[21:25]
    new = [refs[25 + 5 * kind : 30 + 5 * kind] for kind in range(6)]
    grad_input[...] = part[...] + push[...].astype(F32)
    where, total = sections(rows)
    chans = rows // 2
    grad_norm = jnp.sqrt(jnp.sum(squares[...], axis=0, keepdims=True)[:, 0:1])
    norm[...] = grad_norm
    scale = jnp.minimum(1.0, CLIP_NORM / grad_norm)

    def write(kind, index, gradient):
        weight, mean, square = (ref[index] for ref in old[kind])
        new_weight, new_mean, new_square = adamw(weight, mean, square, gradient, scale)
        for ref, value in zip(
            new[kind],
            (gradient, new_weight, new_mean, new_square, new_weight.astype(BF16)),
        ):
            ref[index] = value

    dil = new[0][0]
    for layer in range(2):
        for tap in range(2):
            for half in range(2):
                at, n = where[2 * tap + half]
                for tile in range(2):
                    dil[strided(layer, tap, half, tile, rows), :] = grads[layer][
                        at : at + n, tile * LANES : (tile + 1) * LANES
                    ]
    weight, mean, square = (ref[...] for ref in old[0])
    new_weight, new_mean, new_square = adamw(weight, mean, square, dil[...], scale)
    new[0][1][...] = new_weight
    new[0][2][...] = new_mean
    new[0][3][...] = new_square
    new[0][4][...] = new_weight.astype(BF16)
    for layer in range(2):
        for half in range(2):
            block = grads[layer][where[6][0] :, half * LANES : (half + 1) * LANES]
            eye = lax.broadcasted_iota(jnp.int32, (chans, chans), 0) == lax.broadcasted_iota(
                jnp.int32, (chans, chans), 1
            )
            column = block[:, mel + clips : mel + clips + 1]
            line = jnp.sum(jnp.where(eye, column, 0.0), axis=0, keepdims=True)
            write(1, (layer, slice(half, half + 1), slice(None)), line)
            write(2, (layer, half), block[:, :mel])
            speakers = old[3][0].shape[-1]
            write(3, (layer, half), table_gradient(block, who, mel, clips, speakers))
        for kind, section in ((4, 4), (5, 5)):
            at, n = where[section]
            write(kind, (layer,), grads[layer][at : at + n, :])


def on_device(
    x_input,
    mel_frames,
    sample_mask,
    clip_length_array,
    speaker_ids,
    cot_out,
    cot_skip,
    *states,
):
    parts = lax.axis_size("tm")
    held_rows, width = x_input.shape
    own, full = held_rows // 2, 2 * width
    wide = own + 2 * EDGE
    mel = mel_frames.shape[0]
    clips = clip_length_array.shape[0]
    hop = FIRST_DILATION // held_rows

    dil_shape = states[0].shape
    rows = dil_shape[2]
    views = (
        [dilated_view(s) for s in states[0:3]]
        + list(states[3:6])
        + [s.transpose(0, 2, 3, 1) for s in states[6:12]]
        + [s.transpose(0, 2, 1) for s in states[12:18]]
    )
    speakers = views[9].shape[-1]
    where, total = sections(rows)
    far = parts // NEAR
    taken = [views[k] for k in (0, 12, 15, 6, 9, 3)]
    packed_type = BF16 if rows % 32 == 0 else F32
    taken = [views[k] for k in (0, 12, 15, 6, 9, 3)]
    packed_type = BF16 if rows % 32 == 0 else F32
    taken.append(x_input)
    pack_one, pack_two, x_low = call(
        functools.partial(start_body, rows, mel, clips),
        (struct((total, 256), packed_type),) * 2 + (struct(x_input.shape, BF16),),
        *taken,
        scalars=(speaker_ids,),
        space=pl.ANY,
        grant=None,
        scratch=[pltpu.VMEM(v.shape, F32) for v in taken]
        + [pltpu.SemaphoreType.DMA((len(taken),))],
    )

    lag = shifted(x_low, "tm", hop)
    span = own + EDGE
    group_one, stacked = along_all(pack_one.astype(BF16), (lag,))
    group_two, stacked = along_all(pack_two.astype(BF16), (stacked,))
    kept, given = call(
        part_body,
        (struct((span, 4 * width)),) * 2,
        x_input,
        cot_out,
        cot_skip,
        lag,
        unread=(stacked,),
        scratch=[pltpu.VMEM(x_input.shape, F32)],
    )
    parts_one, relayed = near_exchange(group_one, (stacked,), LONG)
    parts_two, begun = near_exchange(group_two, (), LONG)
    joined_own = struct((own, 4 * full))
    edge = struct((EDGE, 4 * full + LANES))
    inner, side, near_edge, edge_sent = call(
        join_body,
        (joined_own, struct((own, LANES)), edge, edge),
        kept,
        swap_cores(given),
        mel_frames,
        sample_mask[None, :],
        unread=(relayed,),
        scratch=[pltpu.VMEM((span, 4 * full), F32), pltpu.VMEM((held_rows, LANES), F32)],
    )
    x_wide, cot_wide, skip_wide, lag_wide, cond, marks = call(
        functools.partial(widen_body, mel, clips),
        (
            struct((wide, full)),
            struct((wide, full)),
            struct((wide, full), BF16),
            struct((wide, full), BF16),
            struct((wide, LANES), BF16),
            struct((wide, LANES)),
        ),
        inner,
        side,
        near_edge,
        across_chips(edge_sent),
        scalars=(clip_length_array,),
        unread=(begun,),
    )
    w1_own, w1_oth = joined(parts_one, (marks,))

    half = struct((own, width))
    wave = struct((own, full))
    broad = struct((wide, full))
    low_half = struct((own, width), BF16)
    low_full = struct((own, full), BF16)
    packed = struct((BLOCKS, ROWS, 256), BF16)

    def forward(weights, *earlier, unread=(), flops=1024):
        return call(
            functools.partial(first_body, own),
            (broad, wave, low_full, half, half, low_half, TOKEN),
            x_wide,
            lag_wide,
            cond,
            marks,
            weights,
            *earlier,
            unread=unread,
            flops=flops,
        )

    res, skip, lag1, ta_own, sb_own, hid_own, _ = forward(w1_own, unread=(begun,), flops=LONG)
    u2, s1, _, ta_oth, sb_oth, hid_oth, token = forward(w1_oth, res, skip)

    w2_own, w2_oth = joined(parts_two, (token,))

    def middle(weights, *earlier):
        return call(
            functools.partial(second_body, own),
            (wave, wave, wave, TOKEN if earlier else broad, packed),
            u2,
            s1,
            cond,
            marks,
            cot_wide,
            skip_wide,
            weights,
            *earlier,
        )

    gate_two = call(
        second_forward_body, (struct((wide, width)),) * 2, u2, cond, marks, w2_own
    )
    *sums, grad_oth = middle(w2_oth)
    mixed, skip_total, g2, _, grad_own = middle(w2_own, *sums, *gate_two)

    def totals(terms, unread=(), flops=1024):
        return call(
            functools.partial(square_body, rows, mel, clips, speakers, len(terms)),
            (struct((total, 256)), struct((8, LANES))),
            *terms,
            scalars=(speaker_ids,),
            unread=unread,
            flops=flops,
        )

    def backward(weights, tanh_a, sig_b, hidden, *earlier, unread):
        last = bool(earlier)
        return call(
            functools.partial(third_body, own, last),
            (wave, low_full if last else TOKEN, TOKEN if last else wave, packed),
            g2,
            x_wide,
            lag1,
            cond,
            marks,
            skip_wide,
            tanh_a,
            sig_b,
            hidden,
            weights,
            *earlier,
            unread=unread,
        )

    grads2, sent2, token = cores_summed(grad_own, grad_oth)
    now, _, lag_sum, grad_oth = backward(w1_oth, ta_oth, sb_oth, hid_oth, unread=(token,))
    g1_part, dlag1, backed, grad_own = backward(
        w1_own, ta_own, sb_own, hid_own, now, lag_sum, unread=()
    )
    kept, given = call(
        divide_body,
        (struct((own, 4 * width)),) * 2,
        mixed,
        skip_total,
        g1_part,
        dlag1,
        scratch=[pltpu.VMEM((own, full), F32)],
    )
    mixed, skip_total, grad_input, push, token = call(
        finish_body, (struct((held_rows, width)),) * 4 + (TOKEN,), kept, swap_cores(given)
    )
    grads2, sent2, summed = near_summed(grads2, sent2, LONG, (backed,))
    grads1, sent1, _ = cores_summed(grad_own, grad_oth, (summed, token))
    last_got = across(sent2, 0)
    terms2, _ = far_terms(grads2, last_got, LONG)
    grads1, sent1, _ = near_summed(grads1, sent1, unread=(terms2[1],))
    terms1, token = far_terms(grads1, across(sent1, 0))
    sum2, squares2 = totals(terms2, (token,))
    push = call(push_body, struct((held_rows, width), BF16), push, unread=(squares2,))
    push = shifted(push, "tm", -hop)
    sum1, squares1 = totals(terms1, flops=LONG // 5)
    squares = call(add_body, TOKEN, squares1, squares2)
    sent = call(spread_body, struct((parts, 1, LANES)), squares, swap_cores(squares))
    squares = lax.all_to_all(sent, "tm", split_axis=0, concat_axis=0, tiled=True)
    outs = [struct((1, 1)), struct((held_rows, width))]
    for view in views[0::3]:
        outs += [struct(view.shape)] * 4 + [struct(view.shape, BF16)]
    updated = call(
        functools.partial(update_body, rows, mel, clips),
        tuple(outs),
        sum1,
        sum2,
        squares.reshape(parts, LANES),
        *views,
        grad_input,
        push,
        scalars=(speaker_ids,),
    )
    grad_norm, grad_input = updated[0].reshape(()), updated[1]
    backs = (
        [lambda v: dilated_back(v, dil_shape), lambda v: v]
        + [lambda v: v.transpose(0, 3, 1, 2)] * 2
        + [lambda v: v.transpose(0, 2, 1)] * 2
    )
    new = [
        [back(v) for v in updated[2 + 5 * kind : 7 + 5 * kind]] for kind, back in enumerate(backs)
    ]
    return (
        mixed,
        skip_total,
        grad_input,
        grad_norm,
        *[group[0] for group in new],
        *[value for group in new for value in group[1:4]],
        *[group[4] for group in new],
    )


def solution(mesh):
    rows = P("tm", "mp")
    dil = P(None, None, "tm", None, "mp")
    bias = P(None, None, ("mp", "tm"))
    wide = P(None, None, None, ("mp", "tm"))
    square = P(None, "mp", "tm")
    kinds = (dil, bias, wide, wide, square, square)
    thrice = tuple(kind for kind in kinds for _ in range(3))
    return jax.shard_map(
        on_device,
        mesh=mesh,
        in_specs=(rows, P(None, "tm"), P("tm"), P(), P(), rows, rows) + thrice,
        out_specs=(rows, rows, rows, P()) + kinds + thrice + kinds,
        check_vma=False,
    )
```
